32 devices in a mesh: tok: 8 (over z, y), qry: 4 (over x, core).
Axes of the slice: x: 2, y: 2, z: 4, core: 2. Of those that a mesh axis runs over, the one named last changes fastest.
Arguments:
- content_in: bfloat16 [64, 512, 768], P(('tok', 'qry')), may hold values from -6 to 6
- query_in: bfloat16 [64, 80, 768], P('tok', 'qry'), may hold values from -6 to 6
- seq_lengths: int32 [64], P('tok'), may hold values from 256 to 512, as said below
- perm_ranks: int32 [64, 512], P('tok'), may hold values from 0 to 511, as said below
- w_query: bfloat16 [768, 768], replicated, may hold values from -0.21875 to 0.21875
- w_key: bfloat16 [768, 768], replicated, may hold values from -0.21875 to 0.21875
- w_value: bfloat16 [768, 768], replicated, may hold values from -0.21875 to 0.21875
- w_output: bfloat16 [768, 768], replicated, may hold values from -1.25 to 1.25
- w_inner: bfloat16 [768, 3072], replicated, may hold values from -0.21875 to 0.21875
- w_outer: bfloat16 [3072, 768], replicated, may hold values from -0.109375 to 0.109375
- b_before: bfloat16 [2, 768], replicated, may hold values from -3 to 3
- b_after: bfloat16 [2, 768], replicated, may hold values from -3 to 3
- b_hidden: bfloat16 [3072], replicated, may hold values from -3 to 3
- norm_gain: bfloat16 [2, 768], replicated, may hold values from 0.5 to 1.5
- norm_shift: bfloat16 [2, 768], replicated, may hold values from -3 to 3
- rel_table: bfloat16 [12, 32], replicated, may hold values from -4 to 4
- cot_content: bfloat16 [64, 512, 768], P(('tok', 'qry')), may hold values from -6 to 6
- cot_query: bfloat16 [64, 80, 768], P('tok', 'qry'), may hold values from -6 to 6
Outputs:
- content_out: bfloat16 [64, 512, 768], P(('tok', 'qry'))
- query_out: bfloat16 [64, 80, 768], P('tok', 'qry')
- d_content: float32 [64, 512, 768], P(('tok', 'qry'))
- d_query: float32 [64, 80, 768], P('tok', 'qry')
- g_query: float32 [768, 768], P('tok')
- g_key: float32 [768, 768], P('tok')
- g_value: float32 [768, 768], P('tok')
- g_output: float32 [768, 768], P('tok')
- g_inner: float32 [768, 3072], P('tok')
- g_outer: float32 [3072, 768], P('tok')
- g_before: float32 [2, 768], P(None, 'tok')
- g_after: float32 [2, 768], P(None, 'tok')
- g_hidden: float32 [3072], P('tok')
- g_gain: float32 [2, 768], P(None, 'tok')
- g_shift: float32 [2, 768], P(None, 'tok')
- g_table: float32 [12, 32], replicated
The draws below stay inside these ranges and needn't reach their ends.
Inputs may be any that keep to these rules, and one draw needn't show every extreme that they name: `seq_lengths`: lengths of the sequences; some sequence has length 512 and some half of 512. `perm_ranks`: each row is a permutation of 0 to 511 that gives the positions below the sequence's length the ranks below that length.
All inputs are finite; a program needn't handle non-finite values.
Results may differ from the reference program's by a relative error of at most 0.017.
Values may be sent and summed in bfloat16 or wider, within the bound.
No kernel may reach another device: no remote copies, remote signals or barrier semaphores. Data moves between devices by JAX's collectives and lax.ppermute only.
A program may use at most 256 MiB of HBM per device.

```python
from functools import partial
import jax
import jax.numpy as jnp
from jax import lax

D = 768
FF = 3072
HEADS = 12
HEAD_DIM = 64
BUCKETS = 32
SEQ_LEN = 512
PRED = 80
SEQ_DEV = 2
SEQS = 64
N_QRY = 4


def shared_lengths(key):
    key = jax.random.fold_in(key, 101)
    key_draw, key_pick = jax.random.split(key)
    lengths_all = jax.random.randint(key_draw, (SEQS,), SEQ_LEN // 2, SEQ_LEN + 1)
    chosen = jax.random.randint(key_pick, (), 0, SEQS)
    places = jnp.arange(SEQS)
    lengths_all = jnp.where(places == chosen, SEQ_LEN, lengths_all)
    lengths_all = jnp.where(places == (chosen + 1) % SEQS, SEQ_LEN // 2, lengths_all)
    return lengths_all.astype(jnp.int32)


def draw_seq_lengths(key, part):
    return shared_lengths(key)


def draw_perm_ranks(key, part):
    lengths_all = shared_lengths(key)
    key = jax.random.fold_in(key, 7)
    columns = jnp.arange(SEQ_LEN, dtype=jnp.int32)[None, :]
    scores = jax.random.randint(key, (SEQS, SEQ_LEN), 0, 2 ** 20) * SEQ_LEN + columns
    padded = (columns >= lengths_all[:, None]).astype(jnp.int32)
    scores = scores + padded * 2 ** 30
    sorted_at = jnp.argsort(scores, axis=1)
    return jnp.argsort(sorted_at, axis=1).astype(jnp.int32)


def level_of(own_key, dims, cuts, smallest, high):
    def one(position, parts):
        heights = jax.random.uniform(jax.random.fold_in(jax.random.fold_in(own_key, 6), position), (parts,), jnp.float32, smallest / len(cuts), high / len(cuts))
        return jnp.repeat(jnp.exp(heights), dims[position] // parts).reshape((-1,) + (1,) * (len(dims) - position - 1))

    loudness = one(*cuts[0])
    for cut in cuts[1:]:
        loudness = loudness * one(*cut)
    return loudness


def bell_draw(rng, dims, scale, bound, cuts=(), held_as=jnp.bfloat16):
    loudness = level_of(rng, dims, cuts, -0.22, 0.18) if cuts else 1.0
    values = jax.random.normal(rng, dims, jnp.float32) * scale * loudness
    return jnp.minimum(jnp.maximum(values, -bound), bound).astype(held_as)


def setup_inputs(seed: int = 0) -> dict:
    arg_keys = jax.random.split(jax.random.key(seed), 19)
    return {
        "content_in": bell_draw(arg_keys[0], (SEQS, SEQ_LEN, D), 1.0, 6.0, ((0, 32),)),
        "query_in": bell_draw(arg_keys[1], (SEQS, PRED, D), 1.0, 6.0, ((0, 8), (1, 4))),
        "seq_lengths": draw_seq_lengths(jax.random.fold_in(arg_keys[18], 71), 0),
        "perm_ranks": draw_perm_ranks(jax.random.fold_in(arg_keys[18], 71), 0),
        "w_query": bell_draw(arg_keys[4], (D, D), D ** -0.5, 0.21875),
        "w_key": bell_draw(arg_keys[5], (D, D), D ** -0.5, 0.21875),
        "w_value": bell_draw(arg_keys[6], (D, D), D ** -0.5, 0.21875),
        "w_output": bell_draw(arg_keys[7], (D, D), (D * 16 // SEQ_LEN) ** -0.5, 1.25),
        "w_inner": bell_draw(arg_keys[8], (D, FF), D ** -0.5, 0.21875),
        "w_outer": bell_draw(arg_keys[9], (FF, D), FF ** -0.5, 0.109375),
        "b_before": bell_draw(arg_keys[10], (2, D), 0.5, 3.0),
        "b_after": bell_draw(arg_keys[11], (2, D), 0.5, 3.0),
        "b_hidden": bell_draw(arg_keys[12], (FF,), 0.5, 3.0),
        "norm_gain": jnp.clip(1.0 + 0.1 * jax.random.normal(arg_keys[13], (2, D), jnp.float32), 0.5, 1.5).astype(jnp.bfloat16),
        "norm_shift": bell_draw(arg_keys[14], (2, D), 0.5, 3.0),
        "rel_table": bell_draw(arg_keys[15], (HEADS, BUCKETS), 1.0, 4.0),
        "cot_content": bell_draw(arg_keys[16], (SEQS, SEQ_LEN, D), 1.0, 6.0, ((0, 32),)),
        "cot_query": bell_draw(arg_keys[17], (SEQS, PRED, D), 1.0, 6.0, ((0, 8), (1, 4))),
    }


EPS = 1e-05
NEG = -1e+30
HIGH_PRECISION = lax.Precision.HIGHEST
BORDERS = (12, 16, 23, 32, 46, 64, 91)

@jax.custom_vjp
def low(v):
    return lax.optimization_barrier(v.astype(jnp.bfloat16)).astype(jnp.float32)

@jax.custom_vjp
def low_back(v):
    return v

def low_keep(v):
    return (low(v), None)

def low_pass(kept, grad):
    return (grad,)

def back_keep(v):
    return (v, None)

def back_low(kept, grad):
    return (low(grad),)
low.defvjp(low_keep, low_pass)
low_back.defvjp(back_keep, back_low)

def bucket_of(offset):
    distance = jnp.abs(offset)
    beyond = 8 + sum(((distance >= border).astype(jnp.int32) for border in BORDERS))
    return jnp.where(distance < 8, distance, beyond) + 16 * (offset > 0).astype(jnp.int32)

def layer_norm(inputs, gain_row, shift_row):
    centre = inputs - lax.optimization_barrier(jnp.mean(inputs, axis=-1, keepdims=True))
    spread = lax.optimization_barrier(jnp.mean(centre * centre, axis=-1, keepdims=True))
    return centre * lax.rsqrt(spread + EPS) * gain_row + shift_row

def attention(query_vectors, key_matrix_rows, value_matrix_rows, position_bias, visible):
    row_count = query_vectors.shape[0]
    q_heads = query_vectors.reshape(row_count, HEADS, HEAD_DIM)
    k_heads = key_matrix_rows.reshape(SEQ_LEN, HEADS, HEAD_DIM)
    v_heads = value_matrix_rows.reshape(SEQ_LEN, HEADS, HEAD_DIM)
    scores = jnp.einsum('rhd,lhd->hrl', q_heads, k_heads, precision=HIGH_PRECISION) * 0.125 + position_bias
    scores = jnp.where(visible[None], low_back(scores), NEG)
    shifted = jnp.exp(scores - lax.optimization_barrier(jnp.max(scores, axis=-1, keepdims=True)))
    attn_probs = shifted / lax.optimization_barrier(jnp.sum(shifted, axis=-1, keepdims=True))
    context = jnp.einsum('hrl,lhd->rhd', low(attn_probs), v_heads, precision=HIGH_PRECISION)
    return low_back(low(context.reshape(row_count, D)))

def branch(stream_in, context, weights):
    w_query, w_key, w_value, w_output, w_inner, w_outer, b_before, b_after, b_hidden, norm_gain, norm_shift, rel_table = weights
    attended = low_back(jnp.dot(context, w_output, precision=HIGH_PRECISION) + b_after[0])
    hidden = layer_norm(stream_in + attended, norm_gain[0], norm_shift[0])
    inner_pre = low_back(jnp.dot(low(hidden), w_inner, precision=HIGH_PRECISION) + b_hidden)
    activated = low(jax.nn.gelu(inner_pre, approximate=False))
    outer_sum = low_back(jnp.dot(activated, w_outer, precision=HIGH_PRECISION) + b_after[1])
    return layer_norm(hidden + outer_sum, norm_gain[1], norm_shift[1])

def sequence_layer(content_row, query_row, length, ranking, weights):
    w_query, w_key, w_value, w_output, w_inner, w_outer, b_before, b_after, b_hidden, norm_gain, norm_shift, rel_table = weights
    places = jnp.arange(SEQ_LEN, dtype=jnp.int32)
    threshold = jnp.maximum(length - PRED, jnp.minimum(ranking, length))
    seen_content = (ranking[None, :] < threshold[:, None]) | (places[:, None] == places[None, :])
    slot_rank = length - PRED + jnp.arange(PRED, dtype=jnp.int32)
    seen_query = ranking[None, :] < slot_rank[:, None]
    slot_place = lax.optimization_barrier(jnp.sum(jnp.where(ranking[None, :] == slot_rank[:, None], places[None, :], 0), axis=1)).astype(jnp.int32)
    bias_content = rel_table[:, bucket_of(places[None, :] - places[:, None])]
    bias_query = rel_table[:, bucket_of(places[None, :] - slot_place[:, None])]
    q_content = low_back(low(jnp.dot(content_row, w_query, precision=HIGH_PRECISION) + b_before[0]))
    k_content = low_back(low(jnp.dot(content_row, w_key, precision=HIGH_PRECISION)))
    v_content = low_back(low(jnp.dot(content_row, w_value, precision=HIGH_PRECISION) + b_before[1]))
    q_query = low_back(low(jnp.dot(query_row, w_query, precision=HIGH_PRECISION) + b_before[0]))
    ctx_content = attention(q_content, k_content, v_content, bias_content, seen_content)
    ctx_query = attention(q_query, k_content, v_content, bias_query, seen_query)
    return (branch(content_row, ctx_content, weights), branch(query_row, ctx_query, weights))

def forward(content_all, query_all, lengths_all, ranks_all, weights):
    per_block = SEQ_DEV * N_QRY
    layer_fn = jax.vmap(partial(sequence_layer, weights=weights))

    def block_layer(pieces):
        return layer_fn(pieces[0], pieces[1], pieces[2], pieces[3])
    pieces = (content_all.reshape(-1, per_block, SEQ_LEN, D), query_all.reshape(-1, per_block, PRED, D), lengths_all.reshape(-1, per_block), ranks_all.reshape(-1, per_block, SEQ_LEN))
    out_content, out_query = lax.map(jax.checkpoint(block_layer), pieces)
    return (out_content.reshape(SEQS, SEQ_LEN, D), out_query.reshape(SEQS, PRED, D))

def reference(content_in, query_in, seq_lengths, perm_ranks, w_query, w_key, w_value, w_output, w_inner, w_outer, b_before, b_after, b_hidden, norm_gain, norm_shift, rel_table, cot_content, cot_query):
    weights = tuple((argument.astype(jnp.float32) for argument in (w_query, w_key, w_value, w_output, w_inner, w_outer, b_before, b_after, b_hidden, norm_gain, norm_shift, rel_table)))

    def apply_layer(content_all, query_all, weight_set):
        return forward(content_all, query_all, seq_lengths, perm_ranks, weight_set)
    outputs, pullback = jax.vjp(apply_layer, content_in.astype(jnp.float32), query_in.astype(jnp.float32), weights)
    d_content, d_query, gradients = pullback((cot_content.astype(jnp.float32), cot_query.astype(jnp.float32)))
    return (outputs[0].astype(jnp.bfloat16), outputs[1].astype(jnp.bfloat16), d_content, d_query, gradients[0], gradients[1], gradients[2], gradients[3], gradients[4], gradients[5], gradients[6], gradients[7], gradients[8], gradients[9], gradients[10], gradients[11])
```

```python
import functools

import jax
import jax.numpy as jnp
from jax import lax
from jax.experimental import pallas as pl
from jax.experimental.pallas import tpu as pltpu
from jax.sharding import PartitionSpec as P

HEADS = 12
HEAD = 64
BUCKETS = 32
PRED = 80
EPS = 1e-05
NEG = -1e30
BORDERS = (12, 16, 23, 32, 46, 64, 91)
LOG2E = 1.4426950408889634
LN2 = 0.6931471805599453
SQRT_HALF = 0.7071067811865476
INV_ROOT = 0.3989422804014327
F32 = jnp.float32
BF16 = jnp.bfloat16
PAIRS = HEADS // 2
TILE = 128
VMEM_LIMIT = 60 * 1024 * 1024
STEP = 320
BACK_STEP = 256
SUB = 64
CHUNK = 768
GRAD_TILE = 512


def nn(a, b):
    return lax.dot_general(a, b, (((1,), (0,)), ((), ())), preferred_element_type=F32)


def nt(a, b):
    return lax.dot_general(a, b, (((1,), (1,)), ((), ())), preferred_element_type=F32)


def tn(a, b):
    return lax.dot_general(a, b, (((0,), (0,)), ((), ())), preferred_element_type=F32)


def bucket_of(offset):
    distance = jnp.abs(offset)
    beyond = 8 + sum(((distance >= border).astype(jnp.int32) for border in BORDERS))
    return jnp.where(distance < 8, distance, beyond) + 16 * (offset > 0).astype(jnp.int32)


def full_spec(shape):
    zeros = (0,) * len(shape)
    return pl.BlockSpec(shape, lambda *_: zeros, pipeline_mode=pl.Buffered(1))


def params():
    return pltpu.CompilerParams(vmem_limit_bytes=VMEM_LIMIT)


def slot_position(rank_row, slot_rank, width):
    lanes = lax.broadcasted_iota(jnp.int32, (1, width), 1).astype(F32)
    place = jnp.sum(jnp.where(rank_row == slot_rank, lanes, 0.0), axis=1, keepdims=True)
    place = place.astype(jnp.int32)
    return place >> 7, place & 127


def pieces(start, size, length, sub):
    at = start
    while at < start + size:
        limit = length if at < length else start + size
        many = min(sub, start + size - at, limit - at)
        yield at, many
        at += many


def row_steps(total, step):
    return [(at, min(step, total - at)) for at in range(0, total, step)]


def plus(total, term):
    return term if total is None else total + term


def attention_forward_kernel(
    xc, xq, wq, wk, wv, before, rank_row, thr_c, thr_q, offsets, table,
    ctx_out, e_out, rr_out, q_out, k_out, v_out, mask, s_buf,
):
    pair = pl.program_id(1)
    length = xc.shape[1]
    slots = xq.shape[1]
    total = length + slots
    tiles = length // TILE

    @pl.when(pair == 0)
    def _():
        scale = 0.125 * LOG2E
        x = xc[0]
        bias = before[...].astype(F32)
        q_out[0, :length] = ((nn(x, wq[...]) + bias[0:1]) * scale).astype(BF16)
        k_out[0] = nn(x, wk[...]).astype(BF16)
        v_out[0] = (nn(x, wv[...]) + bias[1:2]).astype(BF16)
        q_out[0, length:] = ((nn(xq[0], wq[...]) + bias[0:1]) * scale).astype(BF16)
        ranks = rank_row[0]
        for i in range(tiles):
            rows = slice(i * TILE, (i + 1) * TILE)
            seen = ranks < thr_c[0, rows]
            row = lax.broadcasted_iota(jnp.int32, (TILE, length), 0) + i * TILE
            col = lax.broadcasted_iota(jnp.int32, (TILE, length), 1)
            mask[rows] = jnp.where(seen | (row == col), 0.0, NEG)
        mask[length:] = jnp.where(ranks < thr_q[0], 0.0, NEG)

    cols = pl.ds(pl.multiple_of(pair * TILE, TILE), TILE)
    k_pair = k_out[0, :, cols]
    v_pair = v_out[0, :, cols]
    q_pair = q_out[0, :, cols]
    lane = lax.broadcasted_iota(jnp.int32, (1, TILE), 1)
    block_of, row_of = slot_position(rank_row[0], thr_q[0], length)
    pick = (row_of == lax.broadcasted_iota(jnp.int32, (slots, TILE), 1)).astype(BF16)
    zero = jnp.zeros((), BF16)
    setup = []
    for h in range(2):
        own = (lane < HEAD) if h == 0 else (lane >= HEAD)
        strip = pltpu.roll(
            jnp.broadcast_to(offsets[h], (TILE, 512)), 0, 1, stride=1, stride_axis=0
        )[:, : 3 * TILE]
        setup.append((
            jnp.where(own, q_pair, zero),
            jnp.where(own, v_pair, zero),
            strip * LOG2E,
            nn(pick, strip.astype(BF16)) * LOG2E,
            table[2 * pair + h, 15] * LOG2E,
            table[2 * pair + h, 31] * LOG2E,
        ))
    inverse = {}
    context = {}

    def scores(h, at, size):
        s_buf[h, at : at + size] = nt(setup[h][0][at : at + size], k_pair)

    def normalise(h, at, size):
        strip, slot_strip, far_low, far_high = setup[h][2:]
        for t, m in pieces(at, size, length, SUB):
            s = s_buf[h, t : t + m]
            parts = []
            for j in range(tiles):
                if t < length:
                    i, a = t // TILE, t % TILE
                    d = j - i + 1
                    if 0 <= d <= 2:
                        bias = strip[a : a + m, d * TILE : (d + 1) * TILE]
                    else:
                        bias = far_high if j > i else far_low
                else:
                    a = t - length
                    away = j - block_of[a : a + m]
                    bias = jnp.where(away >= 2, far_high, far_low)
                    for d in range(3):
                        near = slot_strip[a : a + m, d * TILE : (d + 1) * TILE]
                        bias = jnp.where(away == d - 1, near, bias)
                parts.append(s[:, j * TILE : (j + 1) * TILE] + bias)
            s = jnp.concatenate(parts, axis=1) + mask[t : t + m]
            top = jnp.max(s, axis=1, keepdims=True)
            e = jnp.exp2(s - top)
            e_out[0, h, t : t + m] = e.astype(BF16)
            inverse[h, t] = 1.0 / jnp.sum(e, axis=1, keepdims=True)

    def attend(h, at, size):
        context[h, at] = nn(e_out[0, h, at : at + size], setup[h][1])
        if h == 0:
            return
        both = context.pop((0, at)) + context.pop((1, at))
        for t, m in pieces(at, size, length, SUB):
            r = jnp.where(lane < HEAD, inverse[0, t], inverse[1, t])
            rr_out[0, t : t + m] = r
            ctx_out[0, t : t + m] = (both[t - at : t - at + m] * r).astype(BF16)

    work = [(h, at, size) for at, size in row_steps(total, STEP) for h in range(2)]
    scores(*work[0])
    for n, item in enumerate(work):
        if n + 1 < len(work):
            scores(*work[n + 1])
        normalise(*item)
        if n:
            attend(*work[n - 1])
    attend(*work[-1])


def attention_forward(xc, xq, wq, wk, wv, before, rank_row, thr_c, thr_q, offsets, table):
    seqs, length, width = xc.shape
    slots = xq.shape[1]
    rows = length + slots

    def by_seq(shape):
        return pl.BlockSpec((1,) + shape, lambda s, p: (s, 0, 0))

    by_pair = pl.BlockSpec((1, rows, TILE), lambda s, p: (s, 0, p))
    return pl.pallas_call(
        attention_forward_kernel,
        grid=(seqs, PAIRS),
        in_specs=[
            by_seq((length, width)),
            by_seq((slots, width)),
            full_spec((width, width)),
            full_spec((width, width)),
            full_spec((width, width)),
            full_spec((2, width)),
            by_seq((1, length)),
            by_seq((length, 1)),
            by_seq((slots, 1)),
            pl.BlockSpec((2, 1, 512), lambda s, p: (p, 0, 0)),
            pl.BlockSpec(memory_space=pltpu.SMEM),
        ],
        out_specs=[
            by_pair,
            pl.BlockSpec((1, 2, rows, length), lambda s, p: (s, p, 0, 0)),
            by_pair,
            by_seq((rows, width)),
            by_seq((length, width)),
            by_seq((length, width)),
        ],
        out_shape=[
            jax.ShapeDtypeStruct((seqs, rows, width), BF16),
            jax.ShapeDtypeStruct((seqs, HEADS, rows, length), BF16),
            jax.ShapeDtypeStruct((seqs, rows, width), F32),
            jax.ShapeDtypeStruct((seqs, rows, width), BF16),
            jax.ShapeDtypeStruct((seqs, length, width), BF16),
            jax.ShapeDtypeStruct((seqs, length, width), BF16),
        ],
        scratch_shapes=[pltpu.VMEM((rows, length), F32), pltpu.VMEM((2, rows, length), F32)],
        compiler_params=params(),
        name="attention_forward",
    )(xc, xq, wq, wk, wv, before, rank_row, thr_c, thr_q, offsets, table)


def attention_backward_kernel(
    first, q, k, v, e_in, ctx, d_ctx, rr, rank_row, thr_q,
    dq_out, dk_out, dv_out, sums, table_out, near_acc, far_acc, dp_buf, ds_buf, sums_acc,
):
    seq = pl.program_id(1)
    length = k.shape[1]
    slots = thr_q.shape[1]
    total = length + slots
    tiles = length // TILE

    @pl.when(seq == 0)
    def _():
        near_acc[...] = jnp.zeros_like(near_acc)
        far_acc[...] = jnp.zeros_like(far_acc)
        sums_acc[...] = jnp.zeros_like(sums_acc)

    lane = lax.broadcasted_iota(jnp.int32, (1, TILE), 1)
    block_of, row_of = slot_position(rank_row[0], thr_q[0], length)
    pick = (row_of == lax.broadcasted_iota(jnp.int32, (slots, TILE), 1)).astype(BF16)
    q_pair, k_pair, v_pair = q[0], k[0], v[0]
    d_context = d_ctx[0].astype(F32) * rr[0]
    product = d_context * ctx[0].astype(F32)
    zero = jnp.zeros((), BF16)
    low_d = d_context.astype(BF16)
    d_turned, q_turned = low_d.T, q_pair.T
    setup = []
    for h in range(2):
        own = (lane < HEAD) if h == 0 else (lane >= HEAD)
        setup.append((
            jnp.where(own, k_pair, zero),
            jnp.where(own, low_d, zero),
            jnp.sum(jnp.where(own, product, 0.0), axis=1, keepdims=True),
        ))
    near = [[{}, {}, {}], [{}, {}, {}]]
    far = [[None, None], [None, None]]
    spread = [None, None]
    dq, dk, dv = {}, [None, None], [None, None]

    def fold(x):
        return jnp.sum(x.reshape(-1, 8, TILE), axis=0)

    def d_probs(h, at, size):
        dp_buf[h, at : at + size] = nt(setup[h][1][at : at + size], v_pair)

    def d_scores(h, at, size):
        for t, m in pieces(at, size, length, SUB):
            ds = e_in[0, h, t : t + m].astype(F32) * (dp_buf[h, t : t + m] - setup[h][2][t : t + m])
            ds_buf[h, t : t + m] = ds.astype(BF16)
            parts = [ds[:, j * TILE : (j + 1) * TILE] for j in range(tiles)]
            if t < length:
                i, a = t // TILE, t % TILE
                for j in range(tiles):
                    if abs(j - i) <= 1:
                        group = near[h][j - i + 1]
                        group[a] = plus(group.get(a), parts[j])
                    else:
                        side = 1 if j > i else 0
                        far[h][side] = plus(far[h][side], fold(parts[j]))
            else:
                a = t - length
                slot_near = [0.0] * 3
                low = high = 0.0
                for j in range(tiles):
                    away = j - block_of[a : a + m]
                    for d in range(3):
                        slot_near[d] = slot_near[d] + jnp.where(away == d - 1, parts[j], 0.0)
                    high = high + jnp.where(away >= 2, parts[j], 0.0)
                    low = low + jnp.where(away <= -2, parts[j], 0.0)
                far[h][0] = plus(far[h][0], fold(low))
                far[h][1] = plus(far[h][1], fold(high))
                slot_near = jnp.concatenate(slot_near, axis=1).astype(BF16)
                spread[h] = plus(spread[h], tn(pick[a : a + m], slot_near))

    def d_queries(h, at, size):
        dq[at] = plus(dq.get(at), nn(ds_buf[h, at : at + size], setup[h][0]))

    def d_values(h):
        dv[h] = nn(d_turned[h * HEAD : (h + 1) * HEAD], e_in[0, h])

    def d_keys(h):
        dk[h] = nn(q_turned[h * HEAD : (h + 1) * HEAD], ds_buf[h])

    steps = row_steps(total, BACK_STEP)
    work = [(h, at, size) for h in range(2) for at, size in steps]
    d_probs(*work[0])
    d_values(0)
    for n, item in enumerate(work):
        if n + 1 < len(work):
            d_probs(*work[n + 1])
        d_scores(*item)
        if n == len(steps) - 1:
            d_values(1)
        if n:
            d_queries(*work[n - 1])
        if n == len(steps):
            d_keys(0)
    d_queries(*work[-1])
    d_keys(1)

    for h in range(2):
        columns = [
            jnp.concatenate([group[a] for a in sorted(group)], axis=0) for group in near[h]
        ]
        near_acc[h] += jnp.concatenate(columns, axis=1) + spread[h]
        far_acc[h, 0] += far[h][0]
        far_acc[h, 1] += far[h][1]
    dq_sum = None
    for at, size in steps:
        low = (dq[at] * 0.125).astype(BF16)
        dq_out[0, at : at + size] = low
        dq_sum = plus(dq_sum, fold(low.astype(F32)))
    dk_out[0] = (jnp.concatenate(dk, axis=0).T * LN2).astype(BF16)
    low = jnp.concatenate(dv, axis=0).T.astype(BF16)
    dv_out[0] = low
    sums_acc[0] += dq_sum
    sums_acc[1] += fold(low.astype(F32))

    @pl.when(seq == pl.num_programs(1) - 1)
    def _():
        for n in range(2):
            sums[n : n + 1] = jnp.sum(sums_acc[n], axis=0, keepdims=True)
        row = lax.broadcasted_iota(jnp.int32, (8, 512), 0)
        place = lax.broadcasted_iota(jnp.int32, (512, TILE), 0)
        bucket = bucket_of(jnp.where(place < 384, place, place - 512) - 128)
        column = lax.broadcasted_iota(jnp.int32, (512, TILE), 1)
        one_hot = (bucket == column).astype(BF16)
        lane32 = lax.broadcasted_iota(jnp.int32, (1, TILE), 1)
        for h in range(2):
            x = jnp.concatenate([near_acc[h], jnp.zeros((TILE, 512 - 3 * TILE), F32)], axis=1)
            half = TILE // 2
            while half >= 8:
                x = x[:half] + pltpu.roll(x[half:], 512 - half, 1)
                half //= 2
            for bit in (4, 2, 1):
                x = jnp.where((row & bit) != 0, pltpu.roll(x, 512 - bit, 1), x)
            high = x.astype(BF16)
            rest = (x - high.astype(F32)).astype(BF16)
            total_h = jnp.sum(nn(high, one_hot) + nn(rest, one_hot), axis=0, keepdims=True)
            low_far = jnp.sum(far_acc[h, 0])
            high_far = jnp.sum(far_acc[h, 1])
            total_h = total_h + jnp.where(lane32 == 15, low_far, 0.0)
            table_out[0, h : h + 1] = total_h + jnp.where(lane32 == 31, high_far, 0.0)


def attention_backward(half, q, k, v, e, ctx, d_ctx, rr, rank_row, thr_q):
    seqs, length, width = k.shape
    rows = q.shape[1]
    slots = rows - length
    count = PAIRS // 2

    def pick(n):
        return pl.BlockSpec((1, n, TILE), lambda p, s, half: (s, 0, half[0] * count + p))

    def put(n):
        return pl.BlockSpec((1, n, TILE), lambda p, s, half: (s, 0, p))

    def by_seq(shape):
        return pl.BlockSpec((1,) + shape, lambda p, s, half: (s, 0, 0))

    wide = count * TILE
    return pl.pallas_call(
        attention_backward_kernel,
        grid_spec=pltpu.PrefetchScalarGridSpec(
            num_scalar_prefetch=1,
            grid=(count, seqs),
            in_specs=[
                pick(rows), pick(length), pick(length),
                pl.BlockSpec(
                    (1, 2, rows, length), lambda p, s, half: (s, half[0] * count + p, 0, 0)
                ),
                pick(rows), pick(rows), pick(rows),
                by_seq((1, length)), by_seq((slots, 1)),
            ],
            out_specs=[
                put(rows), put(length), put(length),
                pl.BlockSpec((2, TILE), lambda p, s, half: (0, p)),
                pl.BlockSpec((1, 2, TILE), lambda p, s, half: (p, 0, 0)),
            ],
            scratch_shapes=[
                pltpu.VMEM((2, TILE, 3 * TILE), F32),
                pltpu.VMEM((2, 2, 8, TILE), F32),
                pltpu.VMEM((2, rows, length), F32),
                pltpu.VMEM((2, rows, length), BF16),
                pltpu.VMEM((2, 8, TILE), F32),
            ],
        ),
        out_shape=[
            jax.ShapeDtypeStruct((seqs, rows, wide), BF16),
            jax.ShapeDtypeStruct((seqs, length, wide), BF16),
            jax.ShapeDtypeStruct((seqs, length, wide), BF16),
            jax.ShapeDtypeStruct((2, wide), F32),
            jax.ShapeDtypeStruct((count, 2, TILE), F32),
        ],
        compiler_params=params(),
        name="attention_backward",
    )(half, q, k, v, e, ctx, d_ctx, rr, rank_row, thr_q)


def normal_parts(u):
    density = jnp.exp2((-0.5 * LOG2E) * (u * u))
    t = 1.0 / (1.0 + (0.3275911 * SQRT_HALF) * jnp.abs(u))
    tail = t * (
        0.127414796
        + t * (-0.142248368 + t * (0.7107068705 + t * (-0.7265760135 + t * 0.5307027145)))
    )
    tail = tail * density
    return jnp.where(u >= 0, 1.0 - tail, tail), density


def norm_parts(u):
    mean = jnp.mean(u, axis=1, keepdims=True)
    centre = u - mean
    spread = jnp.mean(centre * centre, axis=1, keepdims=True)
    scale = lax.rsqrt(spread + EPS)
    return centre * scale, scale


def norm_back(y, gain, unit, scale):
    e = y * gain
    mean = jnp.mean(e, axis=1, keepdims=True)
    along = jnp.mean(e * unit, axis=1, keepdims=True)
    return (e - mean - unit * along) * scale


def column_sum(x):
    return jnp.sum(x.reshape(-1, 8, x.shape[1]), axis=0)


def weight_copies(w_output, w_inner, w_outer, wo, wi, wu, sems, forward):
    first = [pltpu.make_async_copy(w_output, wo, sems.at[0])]
    chunks = []
    for n in range(w_inner.shape[1] // CHUNK):
        part = pl.ds(n * CHUNK, CHUNK)
        inner = pltpu.make_async_copy(w_inner.at[:, part], wi.at[:, part], sems.at[1 + 2 * n])
        outer = pltpu.make_async_copy(w_outer.at[part], wu.at[part], sems.at[2 + 2 * n])
        chunks += [inner, outer] if forward else [outer, inner]
    return first + chunks if forward else chunks + first


def weight_scratch(width, ff):
    return [
        pltpu.VMEM((width, width), BF16),
        pltpu.VMEM((width, ff), BF16),
        pltpu.VMEM((ff, width), BF16),
        pltpu.SemaphoreType.DMA((1 + 2 * (ff // CHUNK),)),
    ]


def rows_forward_kernel(
    half, ctx, xc, xq, cot_c, cot_q, w_output, w_inner, w_outer, after, hidden_bias, gain, shift,
    out_c, out_q, slope_out, hidden_out, unit_out, scale_out, outer_out, sums, grad_other, grad_mine,
    wo, wi, wu, sems, acc, act, outer, sums_acc,
):
    step = pl.program_id(0)
    seqs = pl.num_programs(0) - act.shape[1] // GRAD_TILE
    rows = acc.shape[0]

    def row_part():
        copies = weight_copies(w_output, w_inner, w_outer, wo, wi, wu, sems, True)

        @pl.when(step == 0)
        def _():
            for copy in copies:
                copy.start()

        def ready(n):
            @pl.when(step == 0)
            def _():
                copies[n].wait()

        at = pl.multiple_of(step * rows, 16)
        length = xc.shape[1]
        after_f, gain_f, shift_f = (a[...].astype(F32) for a in (after, gain, shift))
        stream = jnp.concatenate([xc[0], xq[0]], axis=0).astype(F32)
        ready(0)
        first = stream + nn(ctx[0], wo[...]) + after_f[0:1]
        unit, scale = norm_parts(first)
        unit_out[...] = unit.astype(BF16)
        scale_out[...] = jnp.broadcast_to(scale, scale_out.shape)
        hidden = unit * gain_f[0:1] + shift_f[0:1]
        low = hidden.astype(BF16)
        hidden_out[...] = low
        acc[...] = hidden + after_f[1:2]
        for n in range(wi.shape[1] // CHUNK):
            part = slice(n * CHUNK, (n + 1) * CHUNK)
            ready(1 + 2 * n)
            u = nn(low, wi[:, part]) + hidden_bias[:, part].astype(F32)
            phi, density = normal_parts(u)
            active = (u * phi).astype(BF16)
            act[pl.ds(at, rows), part] = active
            slope_out[:, part] = (phi + u * density * INV_ROOT).astype(BF16)
            ready(2 + 2 * n)
            acc[...] += nn(active, wu[part, :])
        unit2, scale2 = norm_parts(acc[...])
        out = (unit2 * gain_f[1:2] + shift_f[1:2]).astype(BF16)
        out_c[0] = out[:length]
        out_q[0] = out[length:]
        y = jnp.concatenate([cot_c[0], cot_q[0]], axis=0).astype(F32)
        d_second = norm_back(y, gain_f[1:2], unit2, scale2)
        d_outer = d_second.astype(BF16)
        outer_out[...] = d_outer
        outer[pl.ds(at, rows)] = d_outer
        terms = [column_sum(y * unit2), column_sum(y), column_sum(d_outer.astype(F32))]
        for n, term in enumerate(terms):
            sums_acc[n] += term
            sums[n : n + 1] = jnp.sum(sums_acc[n], axis=0, keepdims=True)

    @pl.when(step == 0)
    def _():
        for acc_ref in (sums_acc,):
            acc_ref[...] = jnp.zeros_like(acc_ref)

    @pl.when(step < seqs)
    def _():
        row_part()

    @pl.when(step >= seqs)
    def _():
        cols = pl.ds(pl.multiple_of((step - seqs) * GRAD_TILE, GRAD_TILE), GRAD_TILE)
        grad = tn(act[:, cols], outer[...]).astype(BF16)
        part = grad.shape[1] // 2
        first = half[0] == 0
        grad_mine[...] = jnp.where(first, grad[:, :part], grad[:, part:])
        grad_other[...] = jnp.where(first, grad[:, part:], grad[:, :part])


def rows_backward_kernel(
    half, outer, slope, unit, scale, hidden, ctx, w_output, w_inner, w_outer, gain,
    first_c, first_q, d_ctx, sums, inner_sums, grad_other, grad_mine,
    wo, wi, wu, sems, acc, inner, attended, hidden_t, ctx_t, sums_acc, inner_acc,
):
    step = pl.program_id(0)
    tiles = 3
    seqs = pl.num_programs(0) - 2 * tiles
    rows = acc.shape[0]
    width, ff = wi.shape

    def row_part():
        copies = weight_copies(w_output, w_inner, w_outer, wo, wi, wu, sems, False)

        @pl.when(step == 0)
        def _():
            for copy in copies:
                copy.start()

        def ready(n):
            @pl.when(step == 0)
            def _():
                copies[n].wait()

        at = pl.multiple_of(step * rows, 16)
        acc[...] = outer[...].astype(F32)
        chunks = ff // CHUNK
        for n in range(chunks):
            part = slice(n * CHUNK, (n + 1) * CHUNK)
            ready(2 * n)
            d_act = nt(outer[...], wu[part, :])
            d_inner = (d_act * slope[:, part].astype(F32)).astype(BF16)
            inner[pl.ds(at, rows), part] = d_inner
            term = column_sum(d_inner.astype(F32))
            inner_acc[:, part] += term
            ready(2 * n + 1)
            acc[...] += nt(d_inner, wi[:, part])
        inner_sums[...] = jnp.sum(inner_acc[...], axis=0, keepdims=True)
        unit1 = unit[...].astype(F32)
        d_hidden = acc[...]
        d_first = norm_back(d_hidden, gain[0:1].astype(F32), unit1, scale[:, :1])
        length = first_c.shape[1]
        first_c[0] = d_first[:length]
        first_q[0] = d_first[length:]
        low = d_first.astype(BF16)
        attended[pl.ds(at, rows)] = low
        ready(2 * chunks)
        d_ctx[0] = nt(low, wo[...]).astype(BF16)
        terms = [column_sum(d_hidden * unit1), column_sum(d_hidden), column_sum(low.astype(F32))]
        for n, term in enumerate(terms):
            sums_acc[n] += term
            sums[n : n + 1] = jnp.sum(sums_acc[n], axis=0, keepdims=True)

    @pl.when(step == 0)
    def _():
        for acc_ref in (sums_acc, inner_acc):
            acc_ref[...] = jnp.zeros_like(acc_ref)

    @pl.when(step < seqs)
    def _():
        row_part()

    @pl.when(step == seqs)
    def _():
        hidden_t[...] = hidden[...].T
        ctx_t[...] = ctx[...].T

    wide, narrow = ff // 2 // tiles, width // 2 // tiles

    def grad(which, tile):
        at = pl.multiple_of(which * (ff // 2) + tile * wide, wide)
        to = pl.multiple_of(which * (width // 2) + tile * narrow, narrow)
        left = nn(hidden_t[...], inner[:, pl.ds(at, wide)]).astype(BF16)
        right = nn(ctx_t[...], attended[:, pl.ds(to, narrow)]).astype(BF16)
        return jnp.concatenate([left, right], axis=1)

    @pl.when(jnp.logical_and(step >= seqs, step < seqs + tiles))
    def _():
        grad_other[...] = grad(1 - half[0], step - seqs)

    @pl.when(step >= seqs + tiles)
    def _():
        grad_mine[...] = grad(half[0], step - seqs - tiles)


def rows_forward(
    half, ctx, xc, xq, cot_c, cot_q, w_output, w_inner, w_outer, after, hidden_bias, gain, shift
):
    seqs, rows, width = ctx.shape
    length, slots = xc.shape[1], xq.shape[1]
    ff = w_inner.shape[1]
    total = seqs * rows

    def by_seq(n):
        return pl.BlockSpec((1, n, width), lambda s, half: (jnp.minimum(s, seqs - 1), 0, 0))

    def block(n):
        return pl.BlockSpec((rows, n), lambda s, half: (jnp.minimum(s, seqs - 1), 0))

    grad_block = pl.BlockSpec(
        (GRAD_TILE, width // 2), lambda s, half: (jnp.maximum(s - seqs, 0), 0)
    )
    hbm = pl.BlockSpec(memory_space=pl.ANY)
    return pl.pallas_call(
        rows_forward_kernel,
        grid_spec=pltpu.PrefetchScalarGridSpec(
            num_scalar_prefetch=1,
            grid=(seqs + ff // GRAD_TILE,),
            in_specs=[
            by_seq(rows), by_seq(length), by_seq(slots), by_seq(length), by_seq(slots),
            hbm, hbm, hbm,
            full_spec((2, width)), full_spec((1, ff)), full_spec((2, width)), full_spec((2, width)),
        ],
        out_specs=[
            by_seq(length), by_seq(slots), block(ff), block(width),
            block(width), block(TILE), block(width), full_spec((3, width)),
            grad_block, grad_block,
        ],
        scratch_shapes=weight_scratch(width, ff) + [
            pltpu.VMEM((rows, width), F32),
            pltpu.VMEM((total, ff), BF16),
            pltpu.VMEM((total, width), BF16),
            pltpu.VMEM((3, 8, width), F32),
        ],
        ),
        out_shape=[
            jax.ShapeDtypeStruct((seqs, length, width), BF16),
            jax.ShapeDtypeStruct((seqs, slots, width), BF16),
            jax.ShapeDtypeStruct((total, ff), BF16),
            jax.ShapeDtypeStruct((total, width), BF16),
            jax.ShapeDtypeStruct((total, width), BF16),
            jax.ShapeDtypeStruct((total, TILE), F32),
            jax.ShapeDtypeStruct((total, width), BF16),
            jax.ShapeDtypeStruct((3, width), F32),
            jax.ShapeDtypeStruct((ff, width // 2), BF16),
            jax.ShapeDtypeStruct((ff, width // 2), BF16),
        ],
        compiler_params=params(),
        name="rows_forward",
    )(half, ctx, xc, xq, cot_c, cot_q, w_output, w_inner, w_outer, after, hidden_bias, gain, shift)


def rows_backward(half, seqs, slots, outer, slope, unit, scale, hidden, ctx, w_output, w_inner, w_outer, gain):
    total, width = outer.shape
    rows = total // seqs
    ff = w_inner.shape[1]
    tiles = 3
    wide = (ff + width) // 2

    def block(n):
        return pl.BlockSpec((rows, n), lambda s, half: (jnp.minimum(s, seqs - 1), 0))

    def by_seq(n):
        return pl.BlockSpec((1, n, width), lambda s, half: (jnp.minimum(s, seqs - 1), 0, 0))

    def grad_block(start):
        return pl.BlockSpec(
            (width, wide // tiles), lambda s, half: (0, jnp.clip(s - start, 0, tiles - 1))
        )

    hbm = pl.BlockSpec(memory_space=pl.ANY)
    return pl.pallas_call(
        rows_backward_kernel,
        grid_spec=pltpu.PrefetchScalarGridSpec(
            num_scalar_prefetch=1,
            grid=(seqs + 2 * tiles,),
            in_specs=[
                block(width), block(ff), block(width), block(TILE),
                full_spec((total, width)), full_spec((total, width)),
                hbm, hbm, hbm, full_spec((2, width)),
            ],
            out_specs=[
                by_seq(rows - slots), by_seq(slots), by_seq(rows),
                full_spec((3, width)), full_spec((1, ff)),
                grad_block(seqs), grad_block(seqs + tiles),
            ],
            scratch_shapes=weight_scratch(width, ff) + [
                pltpu.VMEM((rows, width), F32),
                pltpu.VMEM((total, ff), BF16),
                pltpu.VMEM((total, width), BF16),
                pltpu.VMEM((width, total), BF16),
                pltpu.VMEM((width, total), BF16),
                pltpu.VMEM((3, 8, width), F32),
                pltpu.VMEM((8, ff), F32),
            ],
        ),
        out_shape=[
            jax.ShapeDtypeStruct((seqs, rows - slots, width), F32),
            jax.ShapeDtypeStruct((seqs, slots, width), F32),
            jax.ShapeDtypeStruct((seqs, rows, width), BF16),
            jax.ShapeDtypeStruct((3, width), F32),
            jax.ShapeDtypeStruct((1, ff), F32),
            jax.ShapeDtypeStruct((width, wide), BF16),
            jax.ShapeDtypeStruct((width, wide), BF16),
        ],
        compiler_params=params(),
        name="rows_backward",
    )(half, outer, slope, unit, scale, hidden, ctx, w_output, w_inner, w_outer, gain)


def grad_before_kernel(xc, xq, dq, dk, dv, *rest):
    out = rest[-1]
    length = xc.shape[1]
    wide = dq.shape[2]
    q_sum = k_sum = v_sum = None
    for s in range(xc.shape[0]):
        turned = jnp.concatenate([xc[s], xq[s]], axis=0).T
        q_sum = plus(q_sum, nn(turned, dq[s]))
        k_sum = plus(k_sum, nn(turned[:, :length], dk[s]))
        v_sum = plus(v_sum, nn(turned[:, :length], dv[s]))
    for n, total in enumerate((q_sum, k_sum, v_sum)):
        cols = slice(n * wide, (n + 1) * wide)
        if len(rest) == 3:
            total = total + rest[1][:, cols].astype(F32)
        out[:, cols] = total.astype(BF16)
    if len(rest) == 3:
        out[:, 3 * wide :] = rest[0][...].T.astype(BF16)


def grad_before(xc, xq, dq, dk, dv, vectors=None, got=None):
    seqs, length, width = xc.shape
    slots = xq.shape[1]
    wide = dq.shape[2]
    part = width // 2
    total = 3 * wide
    extra, extra_specs = [], []
    if vectors is not None:
        total += vectors.shape[0]
        extra = [vectors, got]
        extra_specs = [
            pl.BlockSpec((vectors.shape[0], part), lambda i: (0, i)),
            pl.BlockSpec((part, 3 * wide), lambda i: (i, 0)),
        ]
    return pl.pallas_call(
        grad_before_kernel,
        grid=(2,),
        in_specs=[
            pl.BlockSpec((seqs, length, part), lambda i: (0, 0, i)),
            pl.BlockSpec((seqs, slots, part), lambda i: (0, 0, i)),
            full_spec(dq.shape), full_spec(dk.shape), full_spec(dv.shape),
        ] + extra_specs,
        out_specs=pl.BlockSpec((part, total), lambda i: (i, 0)),
        out_shape=jax.ShapeDtypeStruct((width, total), BF16),
        compiler_params=params(),
        name="grad_before",
    )(xc, xq, dq, dk, dv, *extra)


def content_grad_kernel(
    half, first, dq_o, dk_o, dv_o, dq_m, dk_m, dv_m, wq_o, wk_o, wv_o, wq_m, wk_m, wv_m, out,
):
    length = dk_o.shape[1]
    left = [dq_o[0, :length], dk_o[0], dv_o[0], dq_m[0, :length], dk_m[0], dv_m[0]]
    right = [wq_o[...], wk_o[...], wv_o[...], wq_m[...], wk_m[...], wv_m[...]]
    out[0] = first[0] + nt(jnp.concatenate(left, axis=1), jnp.concatenate(right, axis=1))


def slot_grad_kernel(half, first, dq_o, dq_m, wq, out):
    seqs, rows, part = dq_o.shape
    slots = out.shape[1]
    length = rows - slots
    first_half = half[0] == 0
    a, b = wq[:, :part], wq[:, part:]
    w_m, w_o = jnp.where(first_half, a, b), jnp.where(first_half, b, a)
    for s in range(seqs):
        grad = nt(dq_o[s, length:], w_o) + nt(dq_m[s, length:], w_m)
        out[s] = (first[s] + grad).astype(BF16)


def slot_grad(half, first, dq_o, dq_m, wq, slots):
    vmem = pl.BlockSpec(memory_space=pltpu.VMEM)
    return pl.pallas_call(
        slot_grad_kernel,
        in_specs=[pl.BlockSpec(memory_space=pltpu.SMEM)] + [vmem] * 4,
        out_specs=vmem,
        out_shape=jax.ShapeDtypeStruct((dq_o.shape[0], slots, wq.shape[0]), BF16),
        compiler_params=params(),
        name="slot_grad",
    )(half, first, dq_o, dq_m, wq)


def content_grad(half, first, other, mine, wq, wk, wv):
    seqs, rows, part = other[0].shape
    length = other[1].shape[1]
    width = wq.shape[0]

    def by_seq(n):
        return pl.BlockSpec((1, n, part), lambda s, half: (s, 0, 0))

    grads = [by_seq(rows), by_seq(length), by_seq(length)]
    w_other = pl.BlockSpec((width, part), lambda s, half: (0, 1 - half[0]))
    w_mine = pl.BlockSpec((width, part), lambda s, half: (0, half[0]))
    return pl.pallas_call(
        content_grad_kernel,
        grid_spec=pltpu.PrefetchScalarGridSpec(
            num_scalar_prefetch=1,
            grid=(seqs,),
            in_specs=[pl.BlockSpec((1, length, width), lambda s, half: (s, 0, 0))]
            + grads * 2 + [w_other] * 3 + [w_mine] * 3,
            out_specs=pl.BlockSpec((1, length, width), lambda s, half: (s, 0, 0)),
        ),
        out_shape=jax.ShapeDtypeStruct((seqs, length, width), F32),
        compiler_params=params(),
        name="content_grad",
    )(half, first, *other, *mine, wq, wk, wv, wq, wk, wv)


def swap(value, axis, count, stride):
    return lax.ppermute(value, axis, [(i, i ^ stride) for i in range(count)])


def take(value, dim, index):
    return lax.dynamic_index_in_dim(value, index, dim, keepdims=False)


def low_sum(*terms):
    total = None
    for term in terms:
        total = plus(total, term.astype(F32))
    return total.astype(BF16)


def first_kernel(bits, *refs):
    terms, (send_a, send_b, keep_a, keep_b) = refs[:-4], refs[-4:]
    x, y = bits[0], bits[1]
    cut = send_a.shape[2]

    def total(g, row, col, rows):
        out = None
        for term in terms:
            out = plus(out, term[g, row, col, rows].astype(F32))
        return out.astype(BF16)

    for g in range(send_a.shape[0]):
        for n in range(2):
            send_a[g, n] = total(g, n, 1 - x, slice(0, cut))
            keep_a[g, n] = total(g, n, x, slice(0, cut))
            send_b[g, n] = total(g, 1 - y, n, slice(cut, 2 * cut))
            keep_b[g, n] = total(g, y, n, slice(cut, 2 * cut))


def second_kernel(bits, keep_a, keep_b, got_a, got_b, send_a, send_b, left_a, left_b):
    x, y = bits[0], bits[1]

    def total(keep, got, g, n):
        return (keep[g, n].astype(F32) + got[g, n].astype(F32)).astype(BF16)

    for g in range(send_a.shape[0]):
        send_a[g] = total(keep_a, got_a, g, 1 - y)
        left_a[g] = total(keep_a, got_a, g, y)
        send_b[g] = total(keep_b, got_b, g, 1 - x)
        left_b[g] = total(keep_b, got_b, g, x)


def third_kernel(bits, left_a, left_b, got_a, got_b, out):
    cut = left_a.shape[1]
    out[:, :cut] = (left_a[...].astype(F32) + got_a[...].astype(F32)).astype(BF16)
    out[:, cut:] = (left_b[...].astype(F32) + got_b[...].astype(F32)).astype(BF16)


def part_sum_kernel(parts, out):
    total = parts[0].astype(F32)
    for n in range(1, parts.shape[0]):
        total = total + parts[n].astype(F32)
    out[...] = total.astype(BF16)


def staged(kernel, bits, arrays, shapes, name):
    vmem = pl.BlockSpec(memory_space=pltpu.VMEM)
    return pl.pallas_call(
        kernel,
        in_specs=[pl.BlockSpec(memory_space=pltpu.SMEM)] + [vmem] * len(arrays),
        out_specs=[vmem] * len(shapes),
        out_shape=[jax.ShapeDtypeStruct(shape, BF16) for shape in shapes],
        compiler_params=params(),
        name=name,
    )(bits, *arrays)


class Reduction:
    def __init__(self, tok):
        self.tok = tok
        x = lax.axis_index("qry") // 2
        y = lax.axis_index("tok") % 2
        self.x = x
        self.bits = jnp.stack([x, y]).astype(jnp.int32)

    def first_sends(self, *terms):
        rows, cols = terms[0].shape
        deep = rows // self.tok // 2
        shape = (self.tok // 2, 2, 2, deep, cols)
        outs = [(self.tok // 2, 2, deep // 2, cols)] * 4
        *sends, self.keep_a, self.keep_b = staged(
            first_kernel, self.bits, [t.reshape(shape) for t in terms], outs, "first_sums"
        )
        return sends

    def first_moves(self, sends):
        return [swap(sends[0], "qry", 4, 2), swap(sends[1], "tok", self.tok, 1)]

    def second_sends(self, got):
        shape = self.keep_a.shape
        outs = [(shape[0],) + shape[2:]] * 4
        *sends, self.left_a, self.left_b = staged(
            second_kernel, self.bits, [self.keep_a, self.keep_b, *got], outs, "second_sums"
        )
        return sends

    def second_moves(self, sends):
        return [swap(sends[0], "tok", self.tok, 1), swap(sends[1], "qry", 4, 2)]

    def third_sends(self, got):
        rest, deep, cols = self.left_a.shape
        (out,) = staged(
            third_kernel, self.bits, [self.left_a, self.left_b, *got], [(rest, 2 * deep, cols)], "third_sums"
        )
        return out

    def third_moves(self, send):
        if self.tok == 2:
            return send
        groups = [list(range(bit, self.tok, 2)) for bit in range(2)]
        return lax.all_to_all(send, "tok", 0, 0, tiled=True, axis_index_groups=groups)

    def far_sends(self, got):
        self.own = pl.pallas_call(
            part_sum_kernel,
            out_shape=jax.ShapeDtypeStruct(got.shape[1:], BF16),
            name="part_sums",
        )(got)
        return self.own

    def far_moves(self, send):
        return swap(send, "qry", 4, 2)

    def near_sends(self, got):
        low = self.x == 0
        self.own = jnp.concatenate(
            [jnp.where(low, self.own, got), jnp.where(low, got, self.own)], axis=0
        )
        return self.own

    def near_moves(self, send):
        return swap(send, "qry", 4, 1)


def beside(transfers, compute=None, arrays=()):
    moves = [move for move, _ in transfers]
    sends = [send for _, send in transfers]
    sends, arrays = lax.optimization_barrier((sends, tuple(arrays)))
    got = [move(send) for move, send in zip(moves, sends)]
    out = compute(*arrays) if compute is not None else ()
    return lax.optimization_barrier((got, out))


def in_core_order(first, own, got):
    a, b = own[...].astype(F32), got[...].astype(F32)
    return jnp.where(first, a, b), jnp.where(first, b, a)


def place_outer_kernel(core, own, got, outer):
    part = own.shape[1]
    first, second = in_core_order(core[0] == 0, own, got)
    outer[:, :part] = first
    outer[:, part:] = second


def place_inner_kernel(core, own, got, inner, output):
    tiles = 3
    wide, narrow = inner.shape[1] // 2 // tiles, output.shape[1] // 2 // tiles
    for n, half in enumerate(in_core_order(core[0] == 0, own, got)):
        for t in range(tiles):
            at = t * (wide + narrow)
            to = (n * tiles + t) * wide
            inner[:, to : to + wide] = half[:, at : at + wide]
            to = (n * tiles + t) * narrow
            output[:, to : to + narrow] = half[:, at + wide : at + wide + narrow]


def place_before_kernel(core, own, got, query, key, value, vectors):
    part = query.shape[1] // 2
    first, second = in_core_order(core[0] == 0, own, got)
    for n, ref in enumerate((query, key, value)):
        ref[:, :part] = first[:, n * part : (n + 1) * part]
        ref[:, part:] = second[:, n * part : (n + 1) * part]
    vectors[...] = (first[:, 3 * part :] + second[:, 3 * part :]).T


def place_sums(kernel, core, own, got, shapes):
    vmem = pl.BlockSpec(memory_space=pltpu.VMEM)
    return pl.pallas_call(
        kernel,
        in_specs=[pl.BlockSpec(memory_space=pltpu.SMEM), vmem, vmem],
        out_specs=[vmem] * len(shapes),
        out_shape=[jax.ShapeDtypeStruct(shape, F32) for shape in shapes],
        name="place_sums",
    )(core, own, got)


def on_device(
    content_in, query_in, seq_lengths, perm_ranks, w_query, w_key, w_value, w_output, w_inner,
    w_outer, b_before, b_after, b_hidden, norm_gain, norm_shift, rel_table, cot_content, cot_query,
    tok,
):
    seqs, length, width = content_in.shape
    group = lax.axis_index("qry")
    core = group % 2
    other = jnp.reshape(1 - core, (1,)).astype(jnp.int32)
    mine = jnp.reshape(core, (1,)).astype(jnp.int32)
    lengths = lax.dynamic_slice_in_dim(seq_lengths, group * seqs, seqs)
    ranks = lax.dynamic_slice_in_dim(perm_ranks, group * seqs, seqs, 0)

    both = jnp.concatenate([query_in, cot_query], axis=2)
    both = lax.all_to_all(both, "qry", 0, 1, tiled=True)
    xq, cot_q = both[:, :, :width], both[:, :, width:]
    slots = xq.shape[1]
    floor = lengths[:, None] - PRED
    thr_c = jnp.maximum(floor, jnp.minimum(ranks, lengths[:, None]))[:, :, None]
    thr_q = (floor + jnp.arange(slots, dtype=jnp.int32)[None, :])[:, :, None]
    rank_row = ranks[:, None, :]
    place = jnp.arange(512, dtype=jnp.int32)
    one_hot = bucket_of(jnp.where(place < 384, place, place - 512) - 128)
    one_hot = (one_hot[None, :] == jnp.arange(BUCKETS, dtype=jnp.int32)[:, None]).astype(BF16)
    offsets = jnp.dot(rel_table, one_hot, preferred_element_type=F32)[:, None, :]

    ctx, e, rr, q, k, v = attention_forward(
        content_in, xq, w_query, w_key, w_value, b_before, rank_row, thr_c, thr_q, offsets,
        rel_table.astype(F32),
    )
    (out_c, out_q, slope, hidden, unit, scale, outer, sums_f, o_other, o_mine) = rows_forward(
        mine, ctx, content_in, xq, cot_content, cot_q, w_output, w_inner, w_outer, b_after,
        b_hidden[None], norm_gain, norm_shift,
    )
    ff = slope.shape[1]
    share = width // tok
    part = width // 2

    red_i = Reduction(tok)
    red_b = Reduction(tok)

    def to_slots(a):
        return lax.all_to_all(a, "qry", 1, 0, tiled=True)

    def slot_blocks(a):
        a = a.reshape(seqs, 4, slots // 4, width)
        return [take(a, 1, group ^ n) for n in range(4)]

    def slot_moves(blocks):
        return [swap(blocks[n], "qry", 4, n) for n in range(1, 4)]

    def slot_rows(own, got):
        every = jnp.stack([own, *got])
        return jnp.concatenate([take(every, 0, group ^ n) for n in range(4)], axis=0)

    def swap_core(a):
        return swap(a, "qry", 4, 1)

    def over_tok(a):
        return lax.psum_scatter(a, "tok", scatter_dimension=0, tiled=True)

    (got_o,), (first_c, first_q, d_ctx, sums_b, inner_sums, i_other, i_mine) = beside(
        [(swap_core, o_other)],
        lambda a: rows_backward(
            mine, seqs, slots, a, slope, unit, scale, hidden, ctx.reshape(-1, width), w_output,
            w_inner, w_outer, norm_gain,
        ),
        (outer,),
    )
    o_sum = over_tok(o_mine.astype(F32) + got_o.astype(F32))
    (got_i,), back_other = beside(
        [(swap_core, i_other)],
        lambda a: attention_backward(other, q, k, v, e, ctx, a, rr, rank_row, thr_q),
        (d_ctx,),
    )

    def grad_and_backward(dq, dk, dv, cotangent):
        b_other = grad_before(content_in, xq, dq, dk, dv)
        b_other, cotangent = lax.optimization_barrier((b_other, cotangent))
        got = swap_core(b_other)
        return got, attention_backward(mine, q, k, v, e, ctx, cotangent, rr, rank_row, thr_q)

    (got_i, out_q), (got_b, back_mine) = beside(
        [(red_i.first_moves, red_i.first_sends(i_mine, got_i)), (to_slots, out_q)],
        grad_and_backward,
        (*back_other[:3], d_ctx),
    )

    def in_order(a, b, axis):
        return jnp.where(
            core == 0, jnp.concatenate([b, a], axis=axis), jnp.concatenate([a, b], axis=axis)
        )

    table = in_order(back_other[4], back_mine[4], 0)[:, :, :BUCKETS]
    table = jnp.tile(table.reshape(-1, share), (1, tok))
    wide_sums = jnp.swapaxes(inner_sums.reshape(tok, ff // width, share), 0, 1)
    vectors = jnp.concatenate(
        [
            in_order(back_other[3], back_mine[3], 1),
            sums_b[2:], sums_f[2:], sums_b[:1], sums_f[:1], sums_b[1:2], sums_f[1:2],
            wide_sums.reshape(-1, width), table,
        ]
    )
    vectors = jnp.pad(vectors, ((0, TILE - vectors.shape[0]), (0, 0)))
    (got_i,), b_mine = beside(
        [(red_i.second_moves, red_i.second_sends(got_i))],
        lambda a: grad_before(content_in, xq, a, *back_mine[1:3], vectors, got_b),
        (back_mine[0],),
    )
    d_query = slot_grad(mine, first_q, back_other[0], back_mine[0], w_query, slots)
    d_query = slot_blocks(d_query)
    send_i = red_i.third_sends(got_i)
    send_b = red_b.first_sends(b_mine)
    send_i, send_b, d_query, first_c = lax.optimization_barrier(
        (send_i, send_b, d_query, first_c)
    )
    got_i = red_i.third_moves(send_i)
    got_b = red_b.first_moves(send_b)
    got_q = slot_moves(d_query)
    d_content = content_grad(
        mine, first_c, back_other[:3], back_mine[:3], w_query, w_key, w_value
    )
    got_b, d_content = lax.optimization_barrier((got_b, d_content))
    (got_b,), d_query = beside(
        [(red_b.second_moves, red_b.second_sends(got_b))],
        lambda *a: slot_rows(a[0], a[1:]).astype(F32),
        (d_query[0], *got_q),
    )

    def swap_x(a):
        return swap(a, "qry", 4, 2)

    (got_b, got_i, got_o), _ = beside(
        [
            (red_b.third_moves, red_b.third_sends(got_b)),
            (red_i.far_moves, red_i.far_sends(got_i)),
            (swap_x, o_sum.astype(BF16)),
        ],
    )
    o_sum = low_sum(o_sum, got_o)
    (got_b, got_o, got_i), _ = beside(
        [
            (red_b.far_moves, red_b.far_sends(got_b)),
            (swap_core, o_sum),
            (red_i.near_moves, red_i.near_sends(got_i)),
        ]
    )
    (got_b,), ((g_outer,), (g_inner, g_output)) = beside(
        [(red_b.near_moves, red_b.near_sends(got_b))],
        lambda a, b: (
            place_sums(place_outer_kernel, mine, o_sum, a, [(ff // tok, width)]),
            place_sums(place_inner_kernel, mine, red_i.own, b, [(share, ff), (share, width)]),
        ),
        (got_o, got_i),
    )
    g_query, g_key, g_value, vectors = place_sums(
        place_before_kernel, mine, red_b.own, got_b, [(share, width)] * 3 + [(TILE, share)]
    )
    g_hidden = vectors[8 : 8 + ff // width].reshape(-1)
    g_table = vectors[8 + ff // width :].reshape(-1)[: HEADS * BUCKETS].reshape(HEADS, BUCKETS)
    return (
        out_c, out_q, d_content, d_query, g_query, g_key, g_value, g_output, g_inner, g_outer,
        vectors[0:2], vectors[2:4], g_hidden, vectors[4:6], vectors[6:8], g_table,
    )


def solution(mesh):
    rows = P(("tok", "qry"), None, None)
    slots = P("tok", "qry", None)
    return jax.shard_map(
        functools.partial(on_device, tok=mesh.shape["tok"]),
        mesh=mesh,
        in_specs=(rows, slots, P("tok"), P("tok", None)) + (P(),) * 12 + (rows, slots),
        out_specs=(rows, slots, rows, slots)
        + (P("tok", None),) * 6
        + (P(None, "tok"), P(None, "tok"), P("tok"), P(None, "tok"), P(None, "tok"), P()),
        check_vma=False,
    )
```

```python
import functools

import jax
import jax.numpy as jnp
from jax import lax
from jax.experimental import pallas as pl
from jax.experimental.pallas import tpu as pltpu
from jax.sharding import PartitionSpec as P

HEADS = 12
HEAD = 64
BUCKETS = 32
PRED = 80
EPS = 1e-05
NEG = -1e30
BORDERS = (12, 16, 23, 32, 46, 64, 91)
LOG2E = 1.4426950408889634
LN2 = 0.6931471805599453
SQRT_HALF = 0.7071067811865476
INV_ROOT = 0.3989422804014327
F32 = jnp.float32
BF16 = jnp.bfloat16
PAIRS = HEADS // 2
TILE = 128
VMEM_LIMIT = 60 * 1024 * 1024
STEP = 320
BACK_STEP = 256
SUB = 64
CHUNK = 768
GRAD_TILE = 512


def nn(a, b):
    return lax.dot_general(a, b, (((1,), (0,)), ((), ())), preferred_element_type=F32)


def nt(a, b):
    return lax.dot_general(a, b, (((1,), (1,)), ((), ())), preferred_element_type=F32)


def tn(a, b):
    return lax.dot_general(a, b, (((0,), (0,)), ((), ())), preferred_element_type=F32)


def bucket_of(offset):
    distance = jnp.abs(offset)
    beyond = 8 + sum(((distance >= border).astype(jnp.int32) for border in BORDERS))
    return jnp.where(distance < 8, distance, beyond) + 16 * (offset > 0).astype(jnp.int32)


def full_spec(shape):
    zeros = (0,) * len(shape)
    return pl.BlockSpec(shape, lambda *_: zeros, pipeline_mode=pl.Buffered(1))


def params():
    return pltpu.CompilerParams(vmem_limit_bytes=VMEM_LIMIT)


def slot_position(rank_row, slot_rank, width):
    lanes = lax.broadcasted_iota(jnp.int32, (1, width), 1).astype(F32)
    place = jnp.sum(jnp.where(rank_row == slot_rank, lanes, 0.0), axis=1, keepdims=True)
    place = place.astype(jnp.int32)
    return place >> 7, place & 127


def pieces(start, size, length, sub):
    at = start
    while at < start + size:
        limit = length if at < length else start + size
        many = min(sub, start + size - at, limit - at)
        yield at, many
        at += many


def row_steps(total, step):
    return [(at, min(step, total - at)) for at in range(0, total, step)]


def plus(total, term):
    return term if total is None else total + term


Q_SCALE = 0.125 * LOG2E


def project_kernel(xc, wq, wk, wv, before, q_out, k_out, v_out):
    x = xc[0]
    bias = before[...].astype(F32)
    q_out[0] = ((nn(x, wq[...]) + bias[0:1]) * Q_SCALE).astype(BF16)
    k_out[0] = nn(x, wk[...]).astype(BF16)
    v_out[0] = (nn(x, wv[...]) + bias[1:2]).astype(BF16)


def project(xc, wq, wk, wv, before):
    seqs, length, width = xc.shape
    rows = pl.BlockSpec((1, length // 2, width), lambda s, i: (s, i, 0))
    weight = full_spec((width, width))
    return pl.pallas_call(
        project_kernel,
        grid=(seqs, 2),
        in_specs=[rows, weight, weight, weight, full_spec((2, width))],
        out_specs=[rows] * 3,
        out_shape=[jax.ShapeDtypeStruct(xc.shape, BF16)] * 3,
        compiler_params=params(),
        name="project",
    )(xc, wq, wk, wv, before)


def attention_forward_kernel(
    q_in, k_in, v_in, xq, wq, before, rank_row, thr_c, thr_q, offsets, table,
    ctx_out, e_out, rr_out, q_out, mask, s_buf,
):
    pair = pl.program_id(1)
    length = q_in.shape[1]
    slots = xq.shape[1]
    total = length + slots
    tiles = length // TILE

    @pl.when(pair == 0)
    def _():
        bias = before[...].astype(F32)[0:1]
        q_out[0, :length] = q_in[0]
        q_out[0, length:] = ((nn(xq[0], wq[...]) + bias) * Q_SCALE).astype(BF16)
        ranks = rank_row[0]
        for i in range(tiles):
            rows = slice(i * TILE, (i + 1) * TILE)
            seen = ranks < thr_c[0, rows]
            row = lax.broadcasted_iota(jnp.int32, (TILE, length), 0) + i * TILE
            col = lax.broadcasted_iota(jnp.int32, (TILE, length), 1)
            mask[rows] = jnp.where(seen | (row == col), 0.0, NEG)
        mask[length:] = jnp.where(ranks < thr_q[0], 0.0, NEG)

    cols = pl.ds(pl.multiple_of(pair * TILE, TILE), TILE)
    k_pair = k_in[0, :, cols]
    v_pair = v_in[0, :, cols]
    q_pair = q_out[0, :, cols]
    lane = lax.broadcasted_iota(jnp.int32, (1, TILE), 1)
    block_of, row_of = slot_position(rank_row[0], thr_q[0], length)
    pick = (row_of == lax.broadcasted_iota(jnp.int32, (slots, TILE), 1)).astype(BF16)
    zero = jnp.zeros((), BF16)
    setup = []
    for h in range(2):
        own = (lane < HEAD) if h == 0 else (lane >= HEAD)
        strip = pltpu.roll(
            jnp.broadcast_to(offsets[h], (TILE, 512)), 0, 1, stride=1, stride_axis=0
        )[:, : 3 * TILE]
        setup.append((
            jnp.where(own, q_pair, zero),
            jnp.where(own, v_pair, zero),
            strip * LOG2E,
            nn(pick, strip.astype(BF16)) * LOG2E,
            table[2 * pair + h, 15] * LOG2E,
            table[2 * pair + h, 31] * LOG2E,
        ))
    inverse = {}
    context = {}

    def scores(h, at, size):
        s_buf[h, at : at + size] = nt(setup[h][0][at : at + size], k_pair)

    def normalise(h, at, size):
        strip, slot_strip, far_low, far_high = setup[h][2:]
        for t, m in pieces(at, size, length, SUB):
            s = s_buf[h, t : t + m]
            parts = []
            for j in range(tiles):
                if t < length:
                    i, a = t // TILE, t % TILE
                    d = j - i + 1
                    if 0 <= d <= 2:
                        bias = strip[a : a + m, d * TILE : (d + 1) * TILE]
                    else:
                        bias = far_high if j > i else far_low
                else:
                    a = t - length
                    away = j - block_of[a : a + m]
                    bias = jnp.where(away >= 2, far_high, far_low)
                    for d in range(3):
                        near = slot_strip[a : a + m, d * TILE : (d + 1) * TILE]
                        bias = jnp.where(away == d - 1, near, bias)
                parts.append(s[:, j * TILE : (j + 1) * TILE] + bias)
            s = jnp.concatenate(parts, axis=1) + mask[t : t + m]
            top = jnp.max(s, axis=1, keepdims=True)
            e = jnp.exp2(s - top)
            e_out[0, h, t : t + m] = e.astype(BF16)
            inverse[h, t] = 1.0 / jnp.sum(e, axis=1, keepdims=True)

    def attend(h, at, size):
        context[h, at] = nn(e_out[0, h, at : at + size], setup[h][1])
        if h == 0:
            return
        both = context.pop((0, at)) + context.pop((1, at))
        for t, m in pieces(at, size, length, SUB):
            r = jnp.where(lane < HEAD, inverse[0, t], inverse[1, t])
            rr_out[0, t : t + m] = r
            ctx_out[0, t : t + m] = (both[t - at : t - at + m] * r).astype(BF16)

    work = [(h, at, size) for at, size in row_steps(total, STEP) for h in range(2)]
    scores(*work[0])
    for n, item in enumerate(work):
        if n + 1 < len(work):
            scores(*work[n + 1])
        normalise(*item)
        if n:
            attend(*work[n - 1])
    attend(*work[-1])


def attention_forward(q, k, v, xq, wq, before, rank_row, thr_c, thr_q, offsets, table):
    seqs, length, width = q.shape
    slots = xq.shape[1]
    rows = length + slots

    def by_seq(shape):
        return pl.BlockSpec((1,) + shape, lambda s, p: (s, 0, 0))

    by_pair = pl.BlockSpec((1, rows, TILE), lambda s, p: (s, 0, p))
    return pl.pallas_call(
        attention_forward_kernel,
        grid=(seqs, PAIRS),
        in_specs=[
            by_seq((length, width)),
            by_seq((length, width)),
            by_seq((length, width)),
            by_seq((slots, width)),
            full_spec((width, width)),
            full_spec((2, width)),
            by_seq((1, length)),
            by_seq((length, 1)),
            by_seq((slots, 1)),
            pl.BlockSpec((2, 1, 512), lambda s, p: (p, 0, 0)),
            pl.BlockSpec(memory_space=pltpu.SMEM),
        ],
        out_specs=[
            by_pair,
            pl.BlockSpec((1, 2, rows, length), lambda s, p: (s, p, 0, 0)),
            by_pair,
            by_seq((rows, width)),
        ],
        out_shape=[
            jax.ShapeDtypeStruct((seqs, rows, width), BF16),
            jax.ShapeDtypeStruct((seqs, HEADS, rows, length), BF16),
            jax.ShapeDtypeStruct((seqs, rows, width), F32),
            jax.ShapeDtypeStruct((seqs, rows, width), BF16),
        ],
        scratch_shapes=[pltpu.VMEM((rows, length), F32), pltpu.VMEM((2, rows, length), F32)],
        compiler_params=params(),
        name="attention_forward",
    )(q, k, v, xq, wq, before, rank_row, thr_c, thr_q, offsets, table)


def attention_backward_kernel(
    first, q, k, v, e_in, ctx, d_ctx, rr, rank_row, thr_q,
    dq_out, dk_out, dv_out, sums, table_out, near_acc, far_acc, dp_buf, ds_buf, sums_acc,
):
    seq = pl.program_id(1)
    length = k.shape[1]
    slots = thr_q.shape[1]
    total = length + slots
    tiles = length // TILE

    @pl.when(seq == 0)
    def _():
        near_acc[...] = jnp.zeros_like(near_acc)
        far_acc[...] = jnp.zeros_like(far_acc)
        sums_acc[...] = jnp.zeros_like(sums_acc)

    lane = lax.broadcasted_iota(jnp.int32, (1, TILE), 1)
    block_of, row_of = slot_position(rank_row[0], thr_q[0], length)
    pick = (row_of == lax.broadcasted_iota(jnp.int32, (slots, TILE), 1)).astype(BF16)
    q_pair, k_pair, v_pair = q[0], k[0], v[0]
    d_context = d_ctx[0].astype(F32) * rr[0]
    product = d_context * ctx[0].astype(F32)
    zero = jnp.zeros((), BF16)
    low_d = d_context.astype(BF16)
    d_turned, q_turned = low_d.T, q_pair.T
    setup = []
    for h in range(2):
        own = (lane < HEAD) if h == 0 else (lane >= HEAD)
        setup.append((
            jnp.where(own, k_pair, zero),
            jnp.where(own, low_d, zero),
            jnp.sum(jnp.where(own, product, 0.0), axis=1, keepdims=True),
        ))
    near = [[{}, {}, {}], [{}, {}, {}]]
    far = [[None, None], [None, None]]
    spread = [None, None]
    dq, dk, dv = {}, [None, None], [None, None]

    def fold(x):
        return jnp.sum(x.reshape(-1, 8, TILE), axis=0)

    def d_probs(h, at, size):
        dp_buf[h, at : at + size] = nt(setup[h][1][at : at + size], v_pair)

    def d_scores(h, at, size):
        for t, m in pieces(at, size, length, SUB):
            ds = e_in[0, h, t : t + m].astype(F32) * (dp_buf[h, t : t + m] - setup[h][2][t : t + m])
            ds_buf[h, t : t + m] = ds.astype(BF16)
            parts = [ds[:, j * TILE : (j + 1) * TILE] for j in range(tiles)]
            if t < length:
                i, a = t // TILE, t % TILE
                for j in range(tiles):
                    if abs(j - i) <= 1:
                        group = near[h][j - i + 1]
                        group[a] = plus(group.get(a), parts[j])
                    else:
                        side = 1 if j > i else 0
                        far[h][side] = plus(far[h][side], fold(parts[j]))
            else:
                a = t - length
                slot_near = [0.0] * 3
                low = high = 0.0
                for j in range(tiles):
                    away = j - block_of[a : a + m]
                    for d in range(3):
                        slot_near[d] = slot_near[d] + jnp.where(away == d - 1, parts[j], 0.0)
                    high = high + jnp.where(away >= 2, parts[j], 0.0)
                    low = low + jnp.where(away <= -2, parts[j], 0.0)
                far[h][0] = plus(far[h][0], fold(low))
                far[h][1] = plus(far[h][1], fold(high))
                slot_near = jnp.concatenate(slot_near, axis=1).astype(BF16)
                spread[h] = plus(spread[h], tn(pick[a : a + m], slot_near))

    def d_queries(h, at, size):
        dq[at] = plus(dq.get(at), nn(ds_buf[h, at : at + size], setup[h][0]))

    def d_values(h):
        dv[h] = nn(d_turned[h * HEAD : (h + 1) * HEAD], e_in[0, h])

    def d_keys(h):
        dk[h] = nn(q_turned[h * HEAD : (h + 1) * HEAD], ds_buf[h])

    steps = row_steps(total, BACK_STEP)
    work = [(h, at, size) for h in range(2) for at, size in steps]
    d_probs(*work[0])
    d_values(0)
    for n, item in enumerate(work):
        if n + 1 < len(work):
            d_probs(*work[n + 1])
        d_scores(*item)
        if n == len(steps) - 1:
            d_values(1)
        if n:
            d_queries(*work[n - 1])
        if n == len(steps):
            d_keys(0)
    d_queries(*work[-1])
    d_keys(1)

    for h in range(2):
        columns = [
            jnp.concatenate([group[a] for a in sorted(group)], axis=0) for group in near[h]
        ]
        near_acc[h] += jnp.concatenate(columns, axis=1) + spread[h]
        far_acc[h, 0] += far[h][0]
        far_acc[h, 1] += far[h][1]
    dq_sum = None
    for at, size in steps:
        low = (dq[at] * 0.125).astype(BF16)
        dq_out[0, at : at + size] = low
        dq_sum = plus(dq_sum, fold(low.astype(F32)))
    dk_out[0] = (jnp.concatenate(dk, axis=0).T * LN2).astype(BF16)
    low = jnp.concatenate(dv, axis=0).T.astype(BF16)
    dv_out[0] = low
    sums_acc[0] += dq_sum
    sums_acc[1] += fold(low.astype(F32))

    @pl.when(seq == pl.num_programs(1) - 1)
    def _():
        for n in range(2):
            sums[n : n + 1] = jnp.sum(sums_acc[n], axis=0, keepdims=True)
        row = lax.broadcasted_iota(jnp.int32, (8, 512), 0)
        place = lax.broadcasted_iota(jnp.int32, (512, TILE), 0)
        bucket = bucket_of(jnp.where(place < 384, place, place - 512) - 128)
        column = lax.broadcasted_iota(jnp.int32, (512, TILE), 1)
        one_hot = (bucket == column).astype(BF16)
        lane32 = lax.broadcasted_iota(jnp.int32, (1, TILE), 1)
        for h in range(2):
            x = jnp.concatenate([near_acc[h], jnp.zeros((TILE, 512 - 3 * TILE), F32)], axis=1)
            half = TILE // 2
            while half >= 8:
                x = x[:half] + pltpu.roll(x[half:], 512 - half, 1)
                half //= 2
            for bit in (4, 2, 1):
                x = jnp.where((row & bit) != 0, pltpu.roll(x, 512 - bit, 1), x)
            high = x.astype(BF16)
            rest = (x - high.astype(F32)).astype(BF16)
            total_h = jnp.sum(nn(high, one_hot) + nn(rest, one_hot), axis=0, keepdims=True)
            low_far = jnp.sum(far_acc[h, 0])
            high_far = jnp.sum(far_acc[h, 1])
            total_h = total_h + jnp.where(lane32 == 15, low_far, 0.0)
            table_out[0, h : h + 1] = total_h + jnp.where(lane32 == 31, high_far, 0.0)


def attention_backward(half, q, k, v, e, ctx, d_ctx, rr, rank_row, thr_q):
    seqs, length, width = k.shape
    rows = q.shape[1]
    slots = rows - length
    count = PAIRS // 2

    def pick(n):
        return pl.BlockSpec((1, n, TILE), lambda p, s, half: (s, 0, half[0] * count + p))

    def put(n):
        return pl.BlockSpec((1, n, TILE), lambda p, s, half: (s, 0, p))

    def by_seq(shape):
        return pl.BlockSpec((1,) + shape, lambda p, s, half: (s, 0, 0))

    wide = count * TILE
    return pl.pallas_call(
        attention_backward_kernel,
        grid_spec=pltpu.PrefetchScalarGridSpec(
            num_scalar_prefetch=1,
            grid=(count, seqs),
            in_specs=[
                pick(rows), pick(length), pick(length),
                pl.BlockSpec(
                    (1, 2, rows, length), lambda p, s, half: (s, half[0] * count + p, 0, 0)
                ),
                pick(rows), pick(rows), pick(rows),
                by_seq((1, length)), by_seq((slots, 1)),
            ],
            out_specs=[
                put(rows), put(length), put(length),
                pl.BlockSpec((2, TILE), lambda p, s, half: (0, p)),
                pl.BlockSpec((1, 2, TILE), lambda p, s, half: (p, 0, 0)),
            ],
            scratch_shapes=[
                pltpu.VMEM((2, TILE, 3 * TILE), F32),
                pltpu.VMEM((2, 2, 8, TILE), F32),
                pltpu.VMEM((2, rows, length), F32),
                pltpu.VMEM((2, rows, length), BF16),
                pltpu.VMEM((2, 8, TILE), F32),
            ],
        ),
        out_shape=[
            jax.ShapeDtypeStruct((seqs, rows, wide), BF16),
            jax.ShapeDtypeStruct((seqs, length, wide), BF16),
            jax.ShapeDtypeStruct((seqs, length, wide), BF16),
            jax.ShapeDtypeStruct((2, wide), F32),
            jax.ShapeDtypeStruct((count, 2, TILE), F32),
        ],
        compiler_params=params(),
        name="attention_backward",
    )(half, q, k, v, e, ctx, d_ctx, rr, rank_row, thr_q)


def normal_parts(u):
    density = jnp.exp2((-0.5 * LOG2E) * (u * u))
    t = 1.0 / (1.0 + (0.3275911 * SQRT_HALF) * jnp.abs(u))
    tail = t * (
        0.127414796
        + t * (-0.142248368 + t * (0.7107068705 + t * (-0.7265760135 + t * 0.5307027145)))
    )
    tail = tail * density
    return jnp.where(u >= 0, 1.0 - tail, tail), density


def norm_parts(u):
    mean = jnp.mean(u, axis=1, keepdims=True)
    centre = u - mean
    spread = jnp.mean(centre * centre, axis=1, keepdims=True)
    scale = lax.rsqrt(spread + EPS)
    return centre * scale, scale


def norm_back(y, gain, unit, scale):
    e = y * gain
    mean = jnp.mean(e, axis=1, keepdims=True)
    along = jnp.mean(e * unit, axis=1, keepdims=True)
    return (e - mean - unit * along) * scale


def column_sum(x):
    return jnp.sum(x.reshape(-1, 8, x.shape[1]), axis=0)


def weight_copies(w_output, w_inner, w_outer, wo, wi, wu, sems, forward):
    first = [pltpu.make_async_copy(w_output, wo, sems.at[0])]
    chunks = []
    for n in range(w_inner.shape[1] // CHUNK):
        part = pl.ds(n * CHUNK, CHUNK)
        inner = pltpu.make_async_copy(w_inner.at[:, part], wi.at[:, part], sems.at[1 + 2 * n])
        outer = pltpu.make_async_copy(w_outer.at[part], wu.at[part], sems.at[2 + 2 * n])
        chunks += [inner, outer] if forward else [outer, inner]
    return first + chunks if forward else chunks + first


def weight_scratch(width, ff):
    return [
        pltpu.VMEM((width, width), BF16),
        pltpu.VMEM((width, ff), BF16),
        pltpu.VMEM((ff, width), BF16),
        pltpu.SemaphoreType.DMA((1 + 2 * (ff // CHUNK),)),
    ]


def rows_forward_kernel(
    ctx, xc, xq, cot_c, cot_q, w_output, w_inner, w_outer, after, hidden_bias, gain, shift,
    out_c, out_q, slope_out, hidden_out, unit_out, scale_out, outer_out, sums, grad_out,
    wo, wi, wu, sems, acc, act, outer, sums_acc,
):
    step = pl.program_id(0)
    seqs = pl.num_programs(0) - act.shape[1] // GRAD_TILE
    rows = acc.shape[0]

    def row_part():
        copies = weight_copies(w_output, w_inner, w_outer, wo, wi, wu, sems, True)

        @pl.when(step == 0)
        def _():
            for copy in copies:
                copy.start()

        def ready(n):
            @pl.when(step == 0)
            def _():
                copies[n].wait()

        at = pl.multiple_of(step * rows, 16)
        length = xc.shape[1]
        after_f, gain_f, shift_f = (a[...].astype(F32) for a in (after, gain, shift))
        stream = jnp.concatenate([xc[0], xq[0]], axis=0).astype(F32)
        ready(0)
        first = stream + nn(ctx[0], wo[...]) + after_f[0:1]
        unit, scale = norm_parts(first)
        unit_out[...] = unit.astype(BF16)
        scale_out[...] = jnp.broadcast_to(scale, scale_out.shape)
        hidden = unit * gain_f[0:1] + shift_f[0:1]
        low = hidden.astype(BF16)
        hidden_out[...] = low
        acc[...] = hidden + after_f[1:2]
        for n in range(wi.shape[1] // CHUNK):
            part = slice(n * CHUNK, (n + 1) * CHUNK)
            ready(1 + 2 * n)
            u = nn(low, wi[:, part]) + hidden_bias[:, part].astype(F32)
            phi, density = normal_parts(u)
            active = (u * phi).astype(BF16)
            act[pl.ds(at, rows), part] = active
            slope_out[:, part] = (phi + u * density * INV_ROOT).astype(BF16)
            ready(2 + 2 * n)
            acc[...] += nn(active, wu[part, :])
        unit2, scale2 = norm_parts(acc[...])
        out = (unit2 * gain_f[1:2] + shift_f[1:2]).astype(BF16)
        out_c[0] = out[:length]
        out_q[0] = out[length:]
        y = jnp.concatenate([cot_c[0], cot_q[0]], axis=0).astype(F32)
        d_second = norm_back(y, gain_f[1:2], unit2, scale2)
        d_outer = d_second.astype(BF16)
        outer_out[...] = d_outer
        outer[pl.ds(at, rows)] = d_outer
        terms = [column_sum(y * unit2), column_sum(y), column_sum(d_outer.astype(F32))]
        for n, term in enumerate(terms):
            sums_acc[n] += term
            sums[n : n + 1] = jnp.sum(sums_acc[n], axis=0, keepdims=True)

    @pl.when(step == 0)
    def _():
        for acc_ref in (sums_acc,):
            acc_ref[...] = jnp.zeros_like(acc_ref)

    @pl.when(step < seqs)
    def _():
        row_part()

    @pl.when(step >= seqs)
    def _():
        cols = pl.ds(pl.multiple_of((step - seqs) * GRAD_TILE, GRAD_TILE), GRAD_TILE)
        grad_out[...] = tn(act[:, cols], outer[...]).astype(BF16)


def rows_backward_kernel(
    half, outer, slope, unit, scale, hidden, ctx, w_output, w_inner, w_outer, gain,
    first_c, first_q, d_ctx, sums, inner_sums, grad_other, grad_mine,
    wo, wi, wu, sems, acc, inner, attended, hidden_t, ctx_t, sums_acc, inner_acc,
):
    step = pl.program_id(0)
    tiles = 3
    seqs = pl.num_programs(0) - 2 * tiles
    rows = acc.shape[0]
    width, ff = wi.shape

    def row_part():
        copies = weight_copies(w_output, w_inner, w_outer, wo, wi, wu, sems, False)

        @pl.when(step == 0)
        def _():
            for copy in copies:
                copy.start()

        def ready(n):
            @pl.when(step == 0)
            def _():
                copies[n].wait()

        at = pl.multiple_of(step * rows, 16)
        acc[...] = outer[...].astype(F32)
        chunks = ff // CHUNK
        for n in range(chunks):
            part = slice(n * CHUNK, (n + 1) * CHUNK)
            ready(2 * n)
            d_act = nt(outer[...], wu[part, :])
            d_inner = (d_act * slope[:, part].astype(F32)).astype(BF16)
            inner[pl.ds(at, rows), part] = d_inner
            term = column_sum(d_inner.astype(F32))
            inner_acc[:, part] += term
            ready(2 * n + 1)
            acc[...] += nt(d_inner, wi[:, part])
        inner_sums[...] = jnp.sum(inner_acc[...], axis=0, keepdims=True)
        unit1 = unit[...].astype(F32)
        d_hidden = acc[...]
        d_first = norm_back(d_hidden, gain[0:1].astype(F32), unit1, scale[:, :1])
        length = first_c.shape[1]
        first_c[0] = d_first[:length]
        first_q[0] = d_first[length:]
        low = d_first.astype(BF16)
        attended[pl.ds(at, rows)] = low
        ready(2 * chunks)
        d_ctx[0] = nt(low, wo[...]).astype(BF16)
        terms = [column_sum(d_hidden * unit1), column_sum(d_hidden), column_sum(low.astype(F32))]
        for n, term in enumerate(terms):
            sums_acc[n] += term
            sums[n : n + 1] = jnp.sum(sums_acc[n], axis=0, keepdims=True)

    @pl.when(step == 0)
    def _():
        for acc_ref in (sums_acc, inner_acc):
            acc_ref[...] = jnp.zeros_like(acc_ref)

    @pl.when(step < seqs)
    def _():
        row_part()

    @pl.when(step == seqs)
    def _():
        hidden_t[...] = hidden[...].T
        ctx_t[...] = ctx[...].T

    wide, narrow = ff // 2 // tiles, width // 2 // tiles

    def grad(which, tile):
        at = pl.multiple_of(which * (ff // 2) + tile * wide, wide)
        to = pl.multiple_of(which * (width // 2) + tile * narrow, narrow)
        left = nn(hidden_t[...], inner[:, pl.ds(at, wide)]).astype(BF16)
        right = nn(ctx_t[...], attended[:, pl.ds(to, narrow)]).astype(BF16)
        return jnp.concatenate([left, right], axis=1)

    @pl.when(jnp.logical_and(step >= seqs, step < seqs + tiles))
    def _():
        grad_other[...] = grad(1 - half[0], step - seqs)

    @pl.when(step >= seqs + tiles)
    def _():
        grad_mine[...] = grad(half[0], step - seqs - tiles)


def rows_forward(
    ctx, xc, xq, cot_c, cot_q, w_output, w_inner, w_outer, after, hidden_bias, gain, shift
):
    seqs, rows, width = ctx.shape
    length, slots = xc.shape[1], xq.shape[1]
    ff = w_inner.shape[1]
    total = seqs * rows

    def by_seq(n):
        return pl.BlockSpec((1, n, width), lambda s: (jnp.minimum(s, seqs - 1), 0, 0))

    def block(n):
        return pl.BlockSpec((rows, n), lambda s: (jnp.minimum(s, seqs - 1), 0))

    grad_block = pl.BlockSpec(
        (GRAD_TILE, width), lambda s: (jnp.maximum(s - seqs, 0), 0)
    )
    hbm = pl.BlockSpec(memory_space=pl.ANY)
    return pl.pallas_call(
        rows_forward_kernel,
        grid_spec=pltpu.PrefetchScalarGridSpec(
            num_scalar_prefetch=0,
            grid=(seqs + ff // GRAD_TILE,),
            in_specs=[
            by_seq(rows), by_seq(length), by_seq(slots), by_seq(length), by_seq(slots),
            hbm, hbm, hbm,
            full_spec((2, width)), full_spec((1, ff)), full_spec((2, width)), full_spec((2, width)),
        ],
        out_specs=[
            by_seq(length), by_seq(slots), block(ff), block(width),
            block(width), block(TILE), block(width), full_spec((3, width)),
            grad_block,
        ],
        scratch_shapes=weight_scratch(width, ff) + [
            pltpu.VMEM((rows, width), F32),
            pltpu.VMEM((total, ff), BF16),
            pltpu.VMEM((total, width), BF16),
            pltpu.VMEM((3, 8, width), F32),
        ],
        ),
        out_shape=[
            jax.ShapeDtypeStruct((seqs, length, width), BF16),
            jax.ShapeDtypeStruct((seqs, slots, width), BF16),
            jax.ShapeDtypeStruct((total, ff), BF16),
            jax.ShapeDtypeStruct((total, width), BF16),
            jax.ShapeDtypeStruct((total, width), BF16),
            jax.ShapeDtypeStruct((total, TILE), F32),
            jax.ShapeDtypeStruct((total, width), BF16),
            jax.ShapeDtypeStruct((3, width), F32),
            jax.ShapeDtypeStruct((ff, width), BF16),
        ],
        compiler_params=params(),
        name="rows_forward",
    )(ctx, xc, xq, cot_c, cot_q, w_output, w_inner, w_outer, after, hidden_bias, gain, shift)


def rows_backward(half, seqs, slots, outer, slope, unit, scale, hidden, ctx, w_output, w_inner, w_outer, gain):
    total, width = outer.shape
    rows = total // seqs
    ff = w_inner.shape[1]
    tiles = 3
    wide = (ff + width) // 2

    def block(n):
        return pl.BlockSpec((rows, n), lambda s, half: (jnp.minimum(s, seqs - 1), 0))

    def by_seq(n):
        return pl.BlockSpec((1, n, width), lambda s, half: (jnp.minimum(s, seqs - 1), 0, 0))

    def grad_block(start):
        return pl.BlockSpec(
            (width, wide // tiles), lambda s, half: (0, jnp.clip(s - start, 0, tiles - 1))
        )

    hbm = pl.BlockSpec(memory_space=pl.ANY)
    return pl.pallas_call(
        rows_backward_kernel,
        grid_spec=pltpu.PrefetchScalarGridSpec(
            num_scalar_prefetch=1,
            grid=(seqs + 2 * tiles,),
            in_specs=[
                block(width), block(ff), block(width), block(TILE),
                full_spec((total, width)), full_spec((total, width)),
                hbm, hbm, hbm, full_spec((2, width)),
            ],
            out_specs=[
                by_seq(rows - slots), by_seq(slots), by_seq(rows),
                full_spec((3, width)), full_spec((1, ff)),
                grad_block(seqs), grad_block(seqs + tiles),
            ],
            scratch_shapes=weight_scratch(width, ff) + [
                pltpu.VMEM((rows, width), F32),
                pltpu.VMEM((total, ff), BF16),
                pltpu.VMEM((total, width), BF16),
                pltpu.VMEM((width, total), BF16),
                pltpu.VMEM((width, total), BF16),
                pltpu.VMEM((3, 8, width), F32),
                pltpu.VMEM((8, ff), F32),
            ],
        ),
        out_shape=[
            jax.ShapeDtypeStruct((seqs, rows - slots, width), F32),
            jax.ShapeDtypeStruct((seqs, slots, width), F32),
            jax.ShapeDtypeStruct((seqs, rows, width), BF16),
            jax.ShapeDtypeStruct((3, width), F32),
            jax.ShapeDtypeStruct((1, ff), F32),
            jax.ShapeDtypeStruct((width, wide), BF16),
            jax.ShapeDtypeStruct((width, wide), BF16),
        ],
        compiler_params=params(),
        name="rows_backward",
    )(half, outer, slope, unit, scale, hidden, ctx, w_output, w_inner, w_outer, gain)


def grad_before_kernel(xc, xq, dq, dk, dv, *rest):
    out = rest[-1]
    length = xc.shape[1]
    wide = dq.shape[2]
    q_sum = k_sum = v_sum = None
    for s in range(xc.shape[0]):
        turned = jnp.concatenate([xc[s], xq[s]], axis=0).T
        q_sum = plus(q_sum, nn(turned, dq[s]))
        k_sum = plus(k_sum, nn(turned[:, :length], dk[s]))
        v_sum = plus(v_sum, nn(turned[:, :length], dv[s]))
    for n, total in enumerate((q_sum, k_sum, v_sum)):
        cols = slice(n * wide, (n + 1) * wide)
        if len(rest) == 3:
            total = total + rest[1][:, cols].astype(F32)
        out[:, cols] = total.astype(BF16)
    if len(rest) == 3:
        out[:, 3 * wide :] = rest[0][...].T.astype(BF16)


def grad_before(xc, xq, dq, dk, dv, vectors=None, got=None):
    seqs, length, width = xc.shape
    slots = xq.shape[1]
    wide = dq.shape[2]
    part = width // 2
    total = 3 * wide
    extra, extra_specs = [], []
    if vectors is not None:
        total += vectors.shape[0]
        extra = [vectors, got]
        extra_specs = [
            pl.BlockSpec((vectors.shape[0], part), lambda i: (0, i)),
            pl.BlockSpec((part, 3 * wide), lambda i: (i, 0)),
        ]
    return pl.pallas_call(
        grad_before_kernel,
        grid=(2,),
        in_specs=[
            pl.BlockSpec((seqs, length, part), lambda i: (0, 0, i)),
            pl.BlockSpec((seqs, slots, part), lambda i: (0, 0, i)),
            full_spec(dq.shape), full_spec(dk.shape), full_spec(dv.shape),
        ] + extra_specs,
        out_specs=pl.BlockSpec((part, total), lambda i: (i, 0)),
        out_shape=jax.ShapeDtypeStruct((width, total), BF16),
        compiler_params=params(),
        name="grad_before",
    )(xc, xq, dq, dk, dv, *extra)


def input_grad_kernel(
    half, first_c, first_q, dq_o, dk_o, dv_o, dq_m, dk_m, dv_m, wq_o, wk_o, wv_o, wq_m, wk_m, wv_m,
    out_c, out_q,
):
    length = dk_o.shape[1]
    left = [dq_o[0, :length], dk_o[0], dv_o[0], dq_m[0, :length], dk_m[0], dv_m[0]]
    right = [wq_o[...], wk_o[...], wv_o[...], wq_m[...], wk_m[...], wv_m[...]]
    out_c[0] = first_c[0] + nt(jnp.concatenate(left, axis=1), jnp.concatenate(right, axis=1))
    dq = jnp.concatenate([dq_o[0, length:], dq_m[0, length:]], axis=1)
    wq = jnp.concatenate([wq_o[...], wq_m[...]], axis=1)
    out_q[0] = (first_q[0] + nt(dq, wq)).astype(BF16)


def input_grad(half, first_c, first_q, other, mine, wq, wk, wv):
    seqs, rows, part = other[0].shape
    length = other[1].shape[1]
    width = wq.shape[0]

    def by_seq(n, cols):
        return pl.BlockSpec((1, n, cols), lambda s, half: (s, 0, 0))

    grads = [by_seq(rows, part), by_seq(length, part), by_seq(length, part)]
    firsts = [by_seq(length, width), by_seq(rows - length, width)]
    w_other = pl.BlockSpec((width, part), lambda s, half: (0, 1 - half[0]))
    w_mine = pl.BlockSpec((width, part), lambda s, half: (0, half[0]))
    return pl.pallas_call(
        input_grad_kernel,
        grid_spec=pltpu.PrefetchScalarGridSpec(
            num_scalar_prefetch=1,
            grid=(seqs,),
            in_specs=firsts + grads * 2 + [w_other] * 3 + [w_mine] * 3,
            out_specs=firsts,
        ),
        out_shape=[
            jax.ShapeDtypeStruct((seqs, length, width), F32),
            jax.ShapeDtypeStruct((seqs, rows - length, width), BF16),
        ],
        compiler_params=params(),
        name="input_grad",
    )(half, first_c, first_q, *other, *mine, wq, wk, wv, wq, wk, wv)


def swap(value, axis, count, stride):
    return lax.ppermute(value, axis, [(i, i ^ stride) for i in range(count)])


def take(value, dim, index):
    return lax.dynamic_index_in_dim(value, index, dim, keepdims=False)


def low_sum(*terms):
    total = None
    for term in terms:
        total = plus(total, term.astype(F32))
    return total.astype(BF16)


def first_kernel(bits, *refs):
    terms, (send_a, send_b, keep_a, keep_b) = refs[:-4], refs[-4:]
    x, y = bits[0], bits[1]
    cut = send_a.shape[2]

    def total(g, row, col, rows):
        out = None
        for term in terms:
            out = plus(out, term[g, row, col, rows].astype(F32))
        return out.astype(BF16)

    for g in range(send_a.shape[0]):
        for n in range(2):
            send_a[g, n] = total(g, n, 1 - x, slice(0, cut))
            keep_a[g, n] = total(g, n, x, slice(0, cut))
            send_b[g, n] = total(g, 1 - y, n, slice(cut, 2 * cut))
            keep_b[g, n] = total(g, y, n, slice(cut, 2 * cut))


def second_kernel(bits, keep_a, keep_b, got_a, got_b, send_a, send_b, left_a, left_b):
    x, y = bits[0], bits[1]

    def total(keep, got, g, n):
        return (keep[g, n].astype(F32) + got[g, n].astype(F32)).astype(BF16)

    for g in range(send_a.shape[0]):
        send_a[g] = total(keep_a, got_a, g, 1 - y)
        left_a[g] = total(keep_a, got_a, g, y)
        send_b[g] = total(keep_b, got_b, g, 1 - x)
        left_b[g] = total(keep_b, got_b, g, x)


def third_kernel(bits, left_a, left_b, got_a, got_b, out):
    cut = left_a.shape[1]
    out[:, :cut] = (left_a[...].astype(F32) + got_a[...].astype(F32)).astype(BF16)
    out[:, cut:] = (left_b[...].astype(F32) + got_b[...].astype(F32)).astype(BF16)


def part_sum_kernel(parts, out):
    total = parts[0].astype(F32)
    for n in range(1, parts.shape[0]):
        total = total + parts[n].astype(F32)
    out[...] = total.astype(BF16)


def staged(kernel, bits, arrays, shapes, name):
    vmem = pl.BlockSpec(memory_space=pltpu.VMEM)
    return pl.pallas_call(
        kernel,
        in_specs=[pl.BlockSpec(memory_space=pltpu.SMEM)] + [vmem] * len(arrays),
        out_specs=[vmem] * len(shapes),
        out_shape=[jax.ShapeDtypeStruct(shape, BF16) for shape in shapes],
        compiler_params=params(),
        name=name,
    )(bits, *arrays)


class Reduction:
    def __init__(self, tok):
        self.tok = tok
        x = lax.axis_index("qry") // 2
        y = lax.axis_index("tok") % 2
        self.x = x
        self.bits = jnp.stack([x, y]).astype(jnp.int32)

    def first_sends(self, *terms):
        rows, cols = terms[0].shape
        deep = rows // self.tok // 2
        shape = (self.tok // 2, 2, 2, deep, cols)
        outs = [(self.tok // 2, 2, deep // 2, cols)] * 4
        *sends, self.keep_a, self.keep_b = staged(
            first_kernel, self.bits, [t.reshape(shape) for t in terms], outs, "first_sums"
        )
        return sends

    def first_moves(self, sends):
        return [swap(sends[0], "qry", 4, 2), swap(sends[1], "tok", self.tok, 1)]

    def second_sends(self, got):
        shape = self.keep_a.shape
        outs = [(shape[0],) + shape[2:]] * 4
        *sends, self.left_a, self.left_b = staged(
            second_kernel, self.bits, [self.keep_a, self.keep_b, *got], outs, "second_sums"
        )
        return sends

    def second_moves(self, sends):
        return [swap(sends[0], "tok", self.tok, 1), swap(sends[1], "qry", 4, 2)]

    def third_sends(self, got):
        rest, deep, cols = self.left_a.shape
        (out,) = staged(
            third_kernel, self.bits, [self.left_a, self.left_b, *got], [(rest, 2 * deep, cols)], "third_sums"
        )
        return out

    def third_moves(self, send):
        if self.tok == 2:
            return send
        groups = [list(range(bit, self.tok, 2)) for bit in range(2)]
        return lax.all_to_all(send, "tok", 0, 0, tiled=True, axis_index_groups=groups)

    def far_sends(self, got):
        self.own = pl.pallas_call(
            part_sum_kernel,
            out_shape=jax.ShapeDtypeStruct(got.shape[1:], BF16),
            name="part_sums",
        )(got)
        return self.own

    def far_moves(self, send):
        return swap(send, "qry", 4, 2)

    def near_sends(self, got):
        low = self.x == 0
        self.own = jnp.concatenate(
            [jnp.where(low, self.own, got), jnp.where(low, got, self.own)], axis=0
        )
        return self.own

    def near_moves(self, send):
        return swap(send, "qry", 4, 1)


def beside(transfers, compute=None, arrays=()):
    moves = [move for move, _ in transfers]
    sends = [send for _, send in transfers]
    sends, arrays = lax.optimization_barrier((sends, tuple(arrays)))
    got = [move(send) for move, send in zip(moves, sends)]
    out = compute(*arrays) if compute is not None else ()
    return lax.optimization_barrier((got, out))


def in_core_order(first, own, got):
    a, b = own[...].astype(F32), got[...].astype(F32)
    return jnp.where(first, a, b), jnp.where(first, b, a)


def place_outer_kernel(core, own, got, outer):
    part = own.shape[1]
    first, second = in_core_order(core[0] == 0, own, got)
    outer[:, :part] = first
    outer[:, part:] = second


def place_inner_kernel(core, own, got, inner, output):
    tiles = 3
    wide, narrow = inner.shape[1] // 2 // tiles, output.shape[1] // 2 // tiles
    for n, half in enumerate(in_core_order(core[0] == 0, own, got)):
        for t in range(tiles):
            at = t * (wide + narrow)
            to = (n * tiles + t) * wide
            inner[:, to : to + wide] = half[:, at : at + wide]
            to = (n * tiles + t) * narrow
            output[:, to : to + narrow] = half[:, at + wide : at + wide + narrow]


def place_before_kernel(core, own, got, query, key, value, vectors):
    part = query.shape[1] // 2
    first, second = in_core_order(core[0] == 0, own, got)
    for n, ref in enumerate((query, key, value)):
        ref[:, :part] = first[:, n * part : (n + 1) * part]
        ref[:, part:] = second[:, n * part : (n + 1) * part]
    vectors[...] = (first[:, 3 * part :] + second[:, 3 * part :]).T


def place_sums(kernel, core, own, got, shapes):
    vmem = pl.BlockSpec(memory_space=pltpu.VMEM)
    return pl.pallas_call(
        kernel,
        in_specs=[pl.BlockSpec(memory_space=pltpu.SMEM), vmem, vmem],
        out_specs=[vmem] * len(shapes),
        out_shape=[jax.ShapeDtypeStruct(shape, F32) for shape in shapes],
        name="place_sums",
    )(core, own, got)


def on_device(
    content_in, query_in, seq_lengths, perm_ranks, w_query, w_key, w_value, w_output, w_inner,
    w_outer, b_before, b_after, b_hidden, norm_gain, norm_shift, rel_table, cot_content, cot_query,
    tok,
):
    seqs, length, width = content_in.shape
    group = lax.axis_index("qry")
    core = group % 2
    other = jnp.reshape(1 - core, (1,)).astype(jnp.int32)
    mine = jnp.reshape(core, (1,)).astype(jnp.int32)
    lengths = lax.dynamic_slice_in_dim(seq_lengths, group * seqs, seqs)
    ranks = lax.dynamic_slice_in_dim(perm_ranks, group * seqs, seqs, 0)

    both = jnp.concatenate([query_in, cot_query], axis=2)
    (both,), (q_content, k, v) = beside(
        [(lambda a: lax.all_to_all(a, "qry", 0, 1, tiled=True), both)],
        lambda: project(content_in, w_query, w_key, w_value, b_before),
    )
    xq, cot_q = both[:, :, :width], both[:, :, width:]
    slots = xq.shape[1]
    floor = lengths[:, None] - PRED
    thr_c = jnp.maximum(floor, jnp.minimum(ranks, lengths[:, None]))[:, :, None]
    thr_q = (floor + jnp.arange(slots, dtype=jnp.int32)[None, :])[:, :, None]
    rank_row = ranks[:, None, :]
    place = jnp.arange(512, dtype=jnp.int32)
    one_hot = bucket_of(jnp.where(place < 384, place, place - 512) - 128)
    one_hot = (one_hot[None, :] == jnp.arange(BUCKETS, dtype=jnp.int32)[:, None]).astype(BF16)
    offsets = jnp.dot(rel_table, one_hot, preferred_element_type=F32)[:, None, :]

    ctx, e, rr, q = attention_forward(
        q_content, k, v, xq, w_query, b_before, rank_row, thr_c, thr_q, offsets,
        rel_table.astype(F32),
    )
    (out_c, out_q, slope, hidden, unit, scale, outer, sums_f, g_outer) = rows_forward(
        ctx, content_in, xq, cot_content, cot_q, w_output, w_inner, w_outer, b_after,
        b_hidden[None], norm_gain, norm_shift,
    )
    ff = slope.shape[1]
    share = width // tok
    part = width // 2

    red_i = Reduction(tok)
    red_b = Reduction(tok)

    def slot_blocks(a):
        a = a.reshape(seqs, 4, slots // 4, a.shape[2])
        return [take(a, 1, group ^ n) for n in range(4)]

    def slot_moves(blocks):
        return [swap(blocks[n], "qry", 4, n) for n in range(1, 4)]

    def slot_rows(own, got):
        every = jnp.stack([own, *got])
        return jnp.concatenate([take(every, 0, group ^ n) for n in range(4)], axis=0)

    def swap_core(a):
        return swap(a, "qry", 4, 1)

    def over_tok(a):
        return lax.psum_scatter(a, "tok", scatter_dimension=0, tiled=True)

    o_sum = over_tok(g_outer)
    first_c, first_q, d_ctx, sums_b, inner_sums, i_other, i_mine = rows_backward(
        mine, seqs, slots, outer, slope, unit, scale, hidden, ctx.reshape(-1, width), w_output,
        w_inner, w_outer, norm_gain,
    )
    (got_i,), back_other = beside(
        [(swap_core, i_other)],
        lambda a: attention_backward(other, q, k, v, e, ctx, a, rr, rank_row, thr_q),
        (d_ctx,),
    )

    def grad_and_backward(dq, dk, dv, cotangent):
        b_other = grad_before(content_in, xq, dq, dk, dv)
        b_other, cotangent = lax.optimization_barrier((b_other, cotangent))
        got = swap_core(b_other)
        return got, attention_backward(mine, q, k, v, e, ctx, cotangent, rr, rank_row, thr_q)

    (got_i,), (got_b, back_mine) = beside(
        [(red_i.first_moves, red_i.first_sends(i_mine, got_i))],
        grad_and_backward,
        (*back_other[:3], d_ctx),
    )

    def in_order(a, b, axis):
        return jnp.where(
            core == 0, jnp.concatenate([b, a], axis=axis), jnp.concatenate([a, b], axis=axis)
        )

    table = in_order(back_other[4], back_mine[4], 0)[:, :, :BUCKETS]
    table = jnp.tile(table.reshape(-1, share), (1, tok))
    wide_sums = jnp.swapaxes(inner_sums.reshape(tok, ff // width, share), 0, 1)
    vectors = jnp.concatenate(
        [
            in_order(back_other[3], back_mine[3], 1),
            sums_b[2:], sums_f[2:], sums_b[:1], sums_f[:1], sums_b[1:2], sums_f[1:2],
            wide_sums.reshape(-1, width), table,
        ]
    )
    vectors = jnp.pad(vectors, ((0, TILE - vectors.shape[0]), (0, 0)))
    o_parts = o_sum.reshape(ff // tok, 2, part)
    (got_i, got_o), b_mine = beside(
        [
            (red_i.second_moves, red_i.second_sends(got_i)),
            (swap_core, take(o_parts, 1, 1 - core)),
        ],
        lambda a: grad_before(content_in, xq, a, *back_mine[1:3], vectors, got_b),
        (back_mine[0],),
    )
    o_sum = low_sum(take(o_parts, 1, core), got_o)
    send_i = red_i.third_sends(got_i)
    send_b = red_b.first_sends(b_mine)
    send_i, send_b, first_c = lax.optimization_barrier((send_i, send_b, first_c))
    got_i = red_i.third_moves(send_i)
    got_b = red_b.first_moves(send_b)
    d_content, d_query = input_grad(
        mine, first_c, first_q, back_other[:3], back_mine[:3], w_query, w_key, w_value
    )
    got_b, d_content, d_query = lax.optimization_barrier((got_b, d_content, d_query))
    (got_b,), rows_q = beside(
        [(red_b.second_moves, red_b.second_sends(got_b))],
        lambda *a: slot_blocks(jnp.concatenate(a, axis=2)),
        (out_q, d_query),
    )

    def swap_x(a):
        return swap(a, "qry", 4, 2)

    (got_b, got_i, got_o, got_q), _ = beside(
        [
            (red_b.third_moves, red_b.third_sends(got_b)),
            (red_i.far_moves, red_i.far_sends(got_i)),
            (swap_x, o_sum),
            (slot_moves, rows_q),
        ],
    )
    o_sum = low_sum(o_sum, got_o)
    (got_b, got_o, got_i), rows_q = beside(
        [
            (red_b.far_moves, red_b.far_sends(got_b)),
            (swap_core, o_sum),
            (red_i.near_moves, red_i.near_sends(got_i)),
        ],
        lambda *a: slot_rows(a[0], a[1:]),
        (rows_q[0], *got_q),
    )
    out_q, d_query = rows_q[:, :, :width], rows_q[:, :, width:].astype(F32)
    (got_b,), ((g_outer,), (g_inner, g_output)) = beside(
        [(red_b.near_moves, red_b.near_sends(got_b))],
        lambda a, b: (
            place_sums(place_outer_kernel, mine, o_sum, a, [(ff // tok, width)]),
            place_sums(place_inner_kernel, mine, red_i.own, b, [(share, ff), (share, width)]),
        ),
        (got_o, got_i),
    )
    g_query, g_key, g_value, vectors = place_sums(
        place_before_kernel, mine, red_b.own, got_b, [(share, width)] * 3 + [(TILE, share)]
    )
    g_hidden = vectors[8 : 8 + ff // width].reshape(-1)
    g_table = vectors[8 + ff // width :].reshape(-1)[: HEADS * BUCKETS].reshape(HEADS, BUCKETS)
    return (
        out_c, out_q, d_content, d_query, g_query, g_key, g_value, g_output, g_inner, g_outer,
        vectors[0:2], vectors[2:4], g_hidden, vectors[4:6], vectors[6:8], g_table,
    )


def solution(mesh):
    rows = P(("tok", "qry"), None, None)
    slots = P("tok", "qry", None)
    return jax.shard_map(
        functools.partial(on_device, tok=mesh.shape["tok"]),
        mesh=mesh,
        in_specs=(rows, slots, P("tok"), P("tok", None)) + (P(),) * 12 + (rows, slots),
        out_specs=(rows, slots, rows, slots)
        + (P("tok", None),) * 6
        + (P(None, "tok"), P(None, "tok"), P("tok"), P(None, "tok"), P(None, "tok"), P()),
        check_vma=False,
    )
```

```python
import functools

import jax
import jax.numpy as jnp
from jax import lax
from jax.experimental import pallas as pl
from jax.experimental.pallas import tpu as pltpu
from jax.sharding import PartitionSpec as P

HEADS = 12
HEAD = 64
BUCKETS = 32
PRED = 80
EPS = 1e-05
NEG = -1e30
BORDERS = (12, 16, 23, 32, 46, 64, 91)
LOG2E = 1.4426950408889634
LN2 = 0.6931471805599453
SQRT_HALF = 0.7071067811865476
INV_ROOT = 0.3989422804014327
F32 = jnp.float32
BF16 = jnp.bfloat16
PAIRS = HEADS // 2
TILE = 128
VMEM_LIMIT = 60 * 1024 * 1024
STEP = 320
BACK_STEP = 256
SUB = 64
CHUNK = 768
GRAD_TILE = 1024


def nn(a, b):
    return lax.dot_general(a, b, (((1,), (0,)), ((), ())), preferred_element_type=F32)


def nt(a, b):
    return lax.dot_general(a, b, (((1,), (1,)), ((), ())), preferred_element_type=F32)


def tn(a, b):
    return lax.dot_general(a, b, (((0,), (0,)), ((), ())), preferred_element_type=F32)


def bucket_of(offset):
    distance = jnp.abs(offset)
    beyond = 8 + sum(((distance >= border).astype(jnp.int32) for border in BORDERS))
    return jnp.where(distance < 8, distance, beyond) + 16 * (offset > 0).astype(jnp.int32)


def full_spec(shape):
    zeros = (0,) * len(shape)
    return pl.BlockSpec(shape, lambda *_: zeros, pipeline_mode=pl.Buffered(1))


def params():
    return pltpu.CompilerParams(vmem_limit_bytes=VMEM_LIMIT)


def slot_position(rank_row, slot_rank, width):
    lanes = lax.broadcasted_iota(jnp.int32, (1, width), 1).astype(F32)
    place = jnp.sum(jnp.where(rank_row == slot_rank, lanes, 0.0), axis=1, keepdims=True)
    place = place.astype(jnp.int32)
    return place >> 7, place & 127


def pieces(start, size, length, sub):
    at = start
    while at < start + size:
        limit = length if at < length else start + size
        many = min(sub, start + size - at, limit - at)
        yield at, many
        at += many


def row_steps(total, step):
    return [(at, min(step, total - at)) for at in range(0, total, step)]


def plus(total, term):
    return term if total is None else total + term


Q_SCALE = 0.125 * LOG2E


def project_kernel(xc, wq, wk, wv, before, q_out, k_out, v_out):
    x = xc[0]
    bias = before[...].astype(F32)
    q_out[0] = ((nn(x, wq[...]) + bias[0:1]) * Q_SCALE).astype(BF16)
    k_out[0] = nn(x, wk[...]).astype(BF16)
    v_out[0] = (nn(x, wv[...]) + bias[1:2]).astype(BF16)


def project(xc, wq, wk, wv, before):
    seqs, length, width = xc.shape
    rows = pl.BlockSpec((1, length // 2, width), lambda s, i: (s, i, 0))
    weight = full_spec((width, width))
    return pl.pallas_call(
        project_kernel,
        grid=(seqs, 2),
        in_specs=[rows, weight, weight, weight, full_spec((2, width))],
        out_specs=[rows] * 3,
        out_shape=[jax.ShapeDtypeStruct(xc.shape, BF16)] * 3,
        compiler_params=params(),
        name="project",
    )(xc, wq, wk, wv, before)


def attention_forward_kernel(
    q_in, k_in, v_in, xq, wq, before, rank_row, thr_c, thr_q, offsets, table,
    ctx_out, e_out, rr_out, q_out, mask, s_buf,
):
    pair = pl.program_id(1)
    length = q_in.shape[1]
    slots = xq.shape[1]
    total = length + slots
    tiles = length // TILE

    @pl.when(pair == 0)
    def _():
        bias = before[...].astype(F32)[0:1]
        q_out[0, :length] = q_in[0]
        q_out[0, length:] = ((nn(xq[0], wq[...]) + bias) * Q_SCALE).astype(BF16)
        ranks = rank_row[0]
        for i in range(tiles):
            rows = slice(i * TILE, (i + 1) * TILE)
            seen = ranks < thr_c[0, rows]
            row = lax.broadcasted_iota(jnp.int32, (TILE, length), 0) + i * TILE
            col = lax.broadcasted_iota(jnp.int32, (TILE, length), 1)
            mask[rows] = jnp.where(seen | (row == col), 0.0, NEG)
        mask[length:] = jnp.where(ranks < thr_q[0], 0.0, NEG)

    cols = pl.ds(pl.multiple_of(pair * TILE, TILE), TILE)
    k_pair = k_in[0, :, cols]
    v_pair = v_in[0, :, cols]
    q_pair = q_out[0, :, cols]
    lane = lax.broadcasted_iota(jnp.int32, (1, TILE), 1)
    block_of, row_of = slot_position(rank_row[0], thr_q[0], length)
    pick = (row_of == lax.broadcasted_iota(jnp.int32, (slots, TILE), 1)).astype(BF16)
    zero = jnp.zeros((), BF16)
    setup = []
    for h in range(2):
        own = (lane < HEAD) if h == 0 else (lane >= HEAD)
        strip = pltpu.roll(
            jnp.broadcast_to(offsets[h], (TILE, 512)), 0, 1, stride=1, stride_axis=0
        )[:, : 3 * TILE]
        setup.append((
            jnp.where(own, q_pair, zero),
            jnp.where(own, v_pair, zero),
            strip * LOG2E,
            nn(pick, strip.astype(BF16)) * LOG2E,
            table[2 * pair + h, 15] * LOG2E,
            table[2 * pair + h, 31] * LOG2E,
        ))
    inverse = {}
    context = {}

    def scores(h, at, size):
        s_buf[h, at : at + size] = nt(setup[h][0][at : at + size], k_pair)

    def normalise(h, at, size):
        strip, slot_strip, far_low, far_high = setup[h][2:]
        for t, m in pieces(at, size, length, SUB):
            s = s_buf[h, t : t + m]
            parts = []
            for j in range(tiles):
                if t < length:
                    i, a = t // TILE, t % TILE
                    d = j - i + 1
                    if 0 <= d <= 2:
                        bias = strip[a : a + m, d * TILE : (d + 1) * TILE]
                    else:
                        bias = far_high if j > i else far_low
                else:
                    a = t - length
                    away = j - block_of[a : a + m]
                    bias = jnp.where(away >= 2, far_high, far_low)
                    for d in range(3):
                        near = slot_strip[a : a + m, d * TILE : (d + 1) * TILE]
                        bias = jnp.where(away == d - 1, near, bias)
                parts.append(s[:, j * TILE : (j + 1) * TILE] + bias)
            s = jnp.concatenate(parts, axis=1) + mask[t : t + m]
            top = jnp.max(s, axis=1, keepdims=True)
            e = jnp.exp2(s - top)
            e_out[0, h, t : t + m] = e.astype(BF16)
            inverse[h, t] = 1.0 / jnp.sum(e, axis=1, keepdims=True)

    def attend(h, at, size):
        context[h, at] = nn(e_out[0, h, at : at + size], setup[h][1])
        if h == 0:
            return
        both = context.pop((0, at)) + context.pop((1, at))
        for t, m in pieces(at, size, length, SUB):
            r = jnp.where(lane < HEAD, inverse[0, t], inverse[1, t])
            rr_out[0, t : t + m] = r
            ctx_out[0, t : t + m] = (both[t - at : t - at + m] * r).astype(BF16)

    work = [(h, at, size) for at, size in row_steps(total, STEP) for h in range(2)]
    scores(*work[0])
    for n, item in enumerate(work):
        if n + 1 < len(work):
            scores(*work[n + 1])
        normalise(*item)
        if n:
            attend(*work[n - 1])
    attend(*work[-1])


def attention_forward(q, k, v, xq, wq, before, rank_row, thr_c, thr_q, offsets, table):
    seqs, length, width = q.shape
    slots = xq.shape[1]
    rows = length + slots

    def by_seq(shape):
        return pl.BlockSpec((1,) + shape, lambda s, p: (s, 0, 0))

    by_pair = pl.BlockSpec((1, rows, TILE), lambda s, p: (s, 0, p))
    return pl.pallas_call(
        attention_forward_kernel,
        grid=(seqs, PAIRS),
        in_specs=[
            by_seq((length, width)),
            by_seq((length, width)),
            by_seq((length, width)),
            by_seq((slots, width)),
            full_spec((width, width)),
            full_spec((2, width)),
            by_seq((1, length)),
            by_seq((length, 1)),
            by_seq((slots, 1)),
            pl.BlockSpec((2, 1, 512), lambda s, p: (p, 0, 0)),
            pl.BlockSpec(memory_space=pltpu.SMEM),
        ],
        out_specs=[
            by_pair,
            pl.BlockSpec((1, 2, rows, length), lambda s, p: (s, p, 0, 0)),
            by_pair,
            by_seq((rows, width)),
        ],
        out_shape=[
            jax.ShapeDtypeStruct((seqs, rows, width), BF16),
            jax.ShapeDtypeStruct((seqs, HEADS, rows, length), BF16),
            jax.ShapeDtypeStruct((seqs, rows, width), F32),
            jax.ShapeDtypeStruct((seqs, rows, width), BF16),
        ],
        scratch_shapes=[pltpu.VMEM((rows, length), F32), pltpu.VMEM((2, rows, length), F32)],
        compiler_params=params(),
        name="attention_forward",
    )(q, k, v, xq, wq, before, rank_row, thr_c, thr_q, offsets, table)


def attention_backward_kernel(
    first, q, k, v, e_in, ctx, d_ctx, rr, rank_row, thr_q,
    dq_out, dk_out, dv_out, sums, table_out, near_acc, far_acc, dp_buf, ds_buf, sums_acc,
):
    seq = pl.program_id(1)
    length = k.shape[1]
    slots = thr_q.shape[1]
    total = length + slots
    tiles = length // TILE

    @pl.when(seq == 0)
    def _():
        near_acc[...] = jnp.zeros_like(near_acc)
        far_acc[...] = jnp.zeros_like(far_acc)
        sums_acc[...] = jnp.zeros_like(sums_acc)

    lane = lax.broadcasted_iota(jnp.int32, (1, TILE), 1)
    block_of, row_of = slot_position(rank_row[0], thr_q[0], length)
    pick = (row_of == lax.broadcasted_iota(jnp.int32, (slots, TILE), 1)).astype(BF16)
    q_pair, k_pair, v_pair = q[0], k[0], v[0]
    d_context = d_ctx[0].astype(F32) * rr[0]
    product = d_context * ctx[0].astype(F32)
    zero = jnp.zeros((), BF16)
    low_d = d_context.astype(BF16)
    d_turned, q_turned = low_d.T, q_pair.T
    setup = []
    for h in range(2):
        own = (lane < HEAD) if h == 0 else (lane >= HEAD)
        setup.append((
            jnp.where(own, k_pair, zero),
            jnp.where(own, low_d, zero),
            jnp.sum(jnp.where(own, product, 0.0), axis=1, keepdims=True),
        ))
    near = [[{}, {}, {}], [{}, {}, {}]]
    far = [[None, None], [None, None]]
    spread = [None, None]
    dq, dk, dv = {}, [None, None], [None, None]

    def fold(x):
        return jnp.sum(x.reshape(-1, 8, TILE), axis=0)

    def d_probs(h, at, size):
        dp_buf[h, at : at + size] = nt(setup[h][1][at : at + size], v_pair)

    def d_scores(h, at, size):
        for t, m in pieces(at, size, length, SUB):
            ds = e_in[0, h, t : t + m].astype(F32) * (dp_buf[h, t : t + m] - setup[h][2][t : t + m])
            ds_buf[h, t : t + m] = ds.astype(BF16)
            parts = [ds[:, j * TILE : (j + 1) * TILE] for j in range(tiles)]
            if t < length:
                i, a = t // TILE, t % TILE
                for j in range(tiles):
                    if abs(j - i) <= 1:
                        group = near[h][j - i + 1]
                        group[a] = plus(group.get(a), parts[j])
                    else:
                        side = 1 if j > i else 0
                        far[h][side] = plus(far[h][side], fold(parts[j]))
            else:
                a = t - length
                slot_near = [0.0] * 3
                low = high = 0.0
                for j in range(tiles):
                    away = j - block_of[a : a + m]
                    for d in range(3):
                        slot_near[d] = slot_near[d] + jnp.where(away == d - 1, parts[j], 0.0)
                    high = high + jnp.where(away >= 2, parts[j], 0.0)
                    low = low + jnp.where(away <= -2, parts[j], 0.0)
                far[h][0] = plus(far[h][0], fold(low))
                far[h][1] = plus(far[h][1], fold(high))
                slot_near = jnp.concatenate(slot_near, axis=1).astype(BF16)
                spread[h] = plus(spread[h], tn(pick[a : a + m], slot_near))

    def d_queries(h, at, size):
        dq[at] = plus(dq.get(at), nn(ds_buf[h, at : at + size], setup[h][0]))

    def d_values(h):
        dv[h] = nn(d_turned[h * HEAD : (h + 1) * HEAD], e_in[0, h])

    def d_keys(h):
        dk[h] = nn(q_turned[h * HEAD : (h + 1) * HEAD], ds_buf[h])

    steps = row_steps(total, BACK_STEP)
    work = [(h, at, size) for h in range(2) for at, size in steps]
    d_probs(*work[0])
    d_values(0)
    for n, item in enumerate(work):
        if n + 1 < len(work):
            d_probs(*work[n + 1])
        d_scores(*item)
        if n == len(steps) - 1:
            d_values(1)
        if n:
            d_queries(*work[n - 1])
        if n == len(steps):
            d_keys(0)
    d_queries(*work[-1])
    d_keys(1)

    for h in range(2):
        columns = [
            jnp.concatenate([group[a] for a in sorted(group)], axis=0) for group in near[h]
        ]
        near_acc[h] += jnp.concatenate(columns, axis=1) + spread[h]
        far_acc[h, 0] += far[h][0]
        far_acc[h, 1] += far[h][1]
    dq_sum = None
    for at, size in steps:
        low = (dq[at] * 0.125).astype(BF16)
        dq_out[0, at : at + size] = low
        dq_sum = plus(dq_sum, fold(low.astype(F32)))
    dk_out[0] = (jnp.concatenate(dk, axis=0).T * LN2).astype(BF16)
    low = jnp.concatenate(dv, axis=0).T.astype(BF16)
    dv_out[0] = low
    sums_acc[0] += dq_sum
    sums_acc[1] += fold(low.astype(F32))

    @pl.when(seq == pl.num_programs(1) - 1)
    def _():
        for n in range(2):
            sums[n : n + 1] = jnp.sum(sums_acc[n], axis=0, keepdims=True)
        row = lax.broadcasted_iota(jnp.int32, (8, 512), 0)
        place = lax.broadcasted_iota(jnp.int32, (512, TILE), 0)
        bucket = bucket_of(jnp.where(place < 384, place, place - 512) - 128)
        column = lax.broadcasted_iota(jnp.int32, (512, TILE), 1)
        one_hot = (bucket == column).astype(BF16)
        lane32 = lax.broadcasted_iota(jnp.int32, (1, TILE), 1)
        for h in range(2):
            x = jnp.concatenate([near_acc[h], jnp.zeros((TILE, 512 - 3 * TILE), F32)], axis=1)
            half = TILE // 2
            while half >= 8:
                x = x[:half] + pltpu.roll(x[half:], 512 - half, 1)
                half //= 2
            for bit in (4, 2, 1):
                x = jnp.where((row & bit) != 0, pltpu.roll(x, 512 - bit, 1), x)
            high = x.astype(BF16)
            rest = (x - high.astype(F32)).astype(BF16)
            total_h = jnp.sum(nn(high, one_hot) + nn(rest, one_hot), axis=0, keepdims=True)
            low_far = jnp.sum(far_acc[h, 0])
            high_far = jnp.sum(far_acc[h, 1])
            total_h = total_h + jnp.where(lane32 == 15, low_far, 0.0)
            table_out[0, h : h + 1] = total_h + jnp.where(lane32 == 31, high_far, 0.0)


def attention_backward(half, q, k, v, e, ctx, d_ctx, rr, rank_row, thr_q):
    seqs, length, width = k.shape
    rows = q.shape[1]
    slots = rows - length
    count = PAIRS // 2

    def pick(n):
        return pl.BlockSpec((1, n, TILE), lambda p, s, half: (s, 0, half[0] * count + p))

    def put(n):
        return pl.BlockSpec((1, n, TILE), lambda p, s, half: (s, 0, p))

    def by_seq(shape):
        return pl.BlockSpec((1,) + shape, lambda p, s, half: (s, 0, 0))

    wide = count * TILE
    return pl.pallas_call(
        attention_backward_kernel,
        grid_spec=pltpu.PrefetchScalarGridSpec(
            num_scalar_prefetch=1,
            grid=(count, seqs),
            in_specs=[
                pick(rows), pick(length), pick(length),
                pl.BlockSpec(
                    (1, 2, rows, length), lambda p, s, half: (s, half[0] * count + p, 0, 0)
                ),
                pick(rows), pick(rows), pick(rows),
                by_seq((1, length)), by_seq((slots, 1)),
            ],
            out_specs=[
                put(rows), put(length), put(length),
                pl.BlockSpec((2, TILE), lambda p, s, half: (0, p)),
                pl.BlockSpec((1, 2, TILE), lambda p, s, half: (p, 0, 0)),
            ],
            scratch_shapes=[
                pltpu.VMEM((2, TILE, 3 * TILE), F32),
                pltpu.VMEM((2, 2, 8, TILE), F32),
                pltpu.VMEM((2, rows, length), F32),
                pltpu.VMEM((2, rows, length), BF16),
                pltpu.VMEM((2, 8, TILE), F32),
            ],
        ),
        out_shape=[
            jax.ShapeDtypeStruct((seqs, rows, wide), BF16),
            jax.ShapeDtypeStruct((seqs, length, wide), BF16),
            jax.ShapeDtypeStruct((seqs, length, wide), BF16),
            jax.ShapeDtypeStruct((2, wide), F32),
            jax.ShapeDtypeStruct((count, 2, TILE), F32),
        ],
        compiler_params=params(),
        name="attention_backward",
    )(half, q, k, v, e, ctx, d_ctx, rr, rank_row, thr_q)


def normal_parts(u):
    density = jnp.exp2((-0.5 * LOG2E) * (u * u))
    t = 1.0 / (1.0 + (0.3275911 * SQRT_HALF) * jnp.abs(u))
    tail = t * (
        0.127414796
        + t * (-0.142248368 + t * (0.7107068705 + t * (-0.7265760135 + t * 0.5307027145)))
    )
    tail = tail * density
    return jnp.where(u >= 0, 1.0 - tail, tail), density


def norm_parts(u):
    mean = jnp.mean(u, axis=1, keepdims=True)
    centre = u - mean
    spread = jnp.mean(centre * centre, axis=1, keepdims=True)
    scale = lax.rsqrt(spread + EPS)
    return centre * scale, scale


def norm_back(y, gain, unit, scale):
    e = y * gain
    mean = jnp.mean(e, axis=1, keepdims=True)
    along = jnp.mean(e * unit, axis=1, keepdims=True)
    return (e - mean - unit * along) * scale


def column_sum(x):
    return jnp.sum(x.reshape(-1, 8, x.shape[1]), axis=0)


def weight_copies(w_output, w_inner, w_outer, wo, wi, wu, sems, forward):
    first = [pltpu.make_async_copy(w_output, wo, sems.at[0])]
    chunks = []
    for n in range(w_inner.shape[1] // CHUNK):
        part = pl.ds(n * CHUNK, CHUNK)
        inner = pltpu.make_async_copy(w_inner.at[:, part], wi.at[:, part], sems.at[1 + 2 * n])
        outer = pltpu.make_async_copy(w_outer.at[part], wu.at[part], sems.at[2 + 2 * n])
        chunks += [inner, outer] if forward else [outer, inner]
    return first + chunks if forward else chunks + first


def weight_scratch(width, ff):
    return [
        pltpu.VMEM((width, width), BF16),
        pltpu.VMEM((width, ff), BF16),
        pltpu.VMEM((ff, width), BF16),
        pltpu.SemaphoreType.DMA((1 + 2 * (ff // CHUNK),)),
    ]


def rows_forward_kernel(
    ctx, xc, xq, cot_c, cot_q, w_output, w_inner, w_outer, after, hidden_bias, gain, shift,
    out_c, out_q, slope_out, hidden_out, unit_out, scale_out, outer_out, sums, grad_out,
    wo, wi, wu, sems, acc, act, outer, sums_acc,
):
    step = pl.program_id(0)
    seqs = pl.num_programs(0) - act.shape[1] // GRAD_TILE
    rows = acc.shape[0]

    def row_part():
        copies = weight_copies(w_output, w_inner, w_outer, wo, wi, wu, sems, True)

        @pl.when(step == 0)
        def _():
            for copy in copies:
                copy.start()

        def ready(n):
            @pl.when(step == 0)
            def _():
                copies[n].wait()

        at = pl.multiple_of(step * rows, 16)
        length = xc.shape[1]
        after_f, gain_f, shift_f = (a[...].astype(F32) for a in (after, gain, shift))
        stream = jnp.concatenate([xc[0], xq[0]], axis=0).astype(F32)
        ready(0)
        first = stream + nn(ctx[0], wo[...]) + after_f[0:1]
        unit, scale = norm_parts(first)
        unit_out[...] = unit.astype(BF16)
        scale_out[...] = jnp.broadcast_to(scale, scale_out.shape)
        hidden = unit * gain_f[0:1] + shift_f[0:1]
        low = hidden.astype(BF16)
        hidden_out[...] = low
        acc[...] = hidden + after_f[1:2]
        for n in range(wi.shape[1] // CHUNK):
            part = slice(n * CHUNK, (n + 1) * CHUNK)
            if n == 0:
                for number in range(1, len(copies)):
                    ready(number)
            u = nn(low, wi[:, part]) + hidden_bias[:, part].astype(F32)
            phi, density = normal_parts(u)
            active = (u * phi).astype(BF16)
            act[pl.ds(at, rows), part] = active
            slope_out[:, part] = (phi + u * density * INV_ROOT).astype(BF16)
            acc[...] += nn(active, wu[part, :])
        unit2, scale2 = norm_parts(acc[...])
        out = (unit2 * gain_f[1:2] + shift_f[1:2]).astype(BF16)
        out_c[0] = out[:length]
        out_q[0] = out[length:]
        y = jnp.concatenate([cot_c[0], cot_q[0]], axis=0).astype(F32)
        d_second = norm_back(y, gain_f[1:2], unit2, scale2)
        d_outer = d_second.astype(BF16)
        outer_out[...] = d_outer
        outer[pl.ds(at, rows)] = d_outer
        terms = [column_sum(y * unit2), column_sum(y), column_sum(d_outer.astype(F32))]
        for n, term in enumerate(terms):
            sums_acc[n] += term
            sums[n : n + 1] = jnp.sum(sums_acc[n], axis=0, keepdims=True)

    @pl.when(step == 0)
    def _():
        for acc_ref in (sums_acc,):
            acc_ref[...] = jnp.zeros_like(acc_ref)

    @pl.when(step < seqs)
    def _():
        row_part()

    @pl.when(step >= seqs)
    def _():
        cols = pl.ds(pl.multiple_of((step - seqs) * GRAD_TILE, GRAD_TILE), GRAD_TILE)
        grad_out[...] = tn(act[:, cols], outer[...]).astype(BF16)


def rows_backward_kernel(
    half, outer, slope, unit, scale, hidden, ctx, w_output, w_inner, w_outer, gain,
    first_c, first_q, d_ctx, sums, inner_sums, grad_other, grad_mine,
    wo, wi, wu, sems, acc, inner, attended, hidden_t, ctx_t, sums_acc, inner_acc,
):
    step = pl.program_id(0)
    tiles = 3
    seqs = pl.num_programs(0) - 2 * tiles
    rows = acc.shape[0]
    width, ff = wi.shape

    def row_part():
        copies = weight_copies(w_output, w_inner, w_outer, wo, wi, wu, sems, False)

        @pl.when(step == 0)
        def _():
            for copy in copies:
                copy.start()

        def ready(n):
            @pl.when(step == 0)
            def _():
                copies[n].wait()

        at = pl.multiple_of(step * rows, 16)
        acc[...] = outer[...].astype(F32)
        chunks = ff // CHUNK
        for n in range(chunks):
            part = slice(n * CHUNK, (n + 1) * CHUNK)
            if n % 2 == 0:
                for number in range(2 * n, min(2 * n + 4, 2 * chunks)):
                    ready(number)
            d_act = nt(outer[...], wu[part, :])
            d_inner = (d_act * slope[:, part].astype(F32)).astype(BF16)
            inner[pl.ds(at, rows), part] = d_inner
            term = column_sum(d_inner.astype(F32))
            inner_acc[:, part] += term
            acc[...] += nt(d_inner, wi[:, part])
        inner_sums[...] = jnp.sum(inner_acc[...], axis=0, keepdims=True)
        unit1 = unit[...].astype(F32)
        d_hidden = acc[...]
        d_first = norm_back(d_hidden, gain[0:1].astype(F32), unit1, scale[:, :1])
        length = first_c.shape[1]
        first_c[0] = d_first[:length]
        first_q[0] = d_first[length:]
        low = d_first.astype(BF16)
        attended[pl.ds(at, rows)] = low
        ready(2 * chunks)
        d_ctx[0] = nt(low, wo[...]).astype(BF16)
        terms = [column_sum(d_hidden * unit1), column_sum(d_hidden), column_sum(low.astype(F32))]
        for n, term in enumerate(terms):
            sums_acc[n] += term
            sums[n : n + 1] = jnp.sum(sums_acc[n], axis=0, keepdims=True)

    @pl.when(step == 0)
    def _():
        for acc_ref in (sums_acc, inner_acc):
            acc_ref[...] = jnp.zeros_like(acc_ref)

    @pl.when(step < seqs)
    def _():
        row_part()

    @pl.when(step == seqs)
    def _():
        hidden_t[...] = hidden[...].T
        ctx_t[...] = ctx[...].T

    wide, narrow = ff // 2 // tiles, width // 2 // tiles

    def grad(which, tile):
        at = pl.multiple_of(which * (ff // 2) + tile * wide, wide)
        to = pl.multiple_of(which * (width // 2) + tile * narrow, narrow)
        left = nn(hidden_t[...], inner[:, pl.ds(at, wide)]).astype(BF16)
        right = nn(ctx_t[...], attended[:, pl.ds(to, narrow)]).astype(BF16)
        return jnp.concatenate([left, right], axis=1)

    @pl.when(jnp.logical_and(step >= seqs, step < seqs + tiles))
    def _():
        grad_other[...] = grad(1 - half[0], step - seqs)

    @pl.when(step >= seqs + tiles)
    def _():
        grad_mine[...] = grad(half[0], step - seqs - tiles)


def rows_forward(
    ctx, xc, xq, cot_c, cot_q, w_output, w_inner, w_outer, after, hidden_bias, gain, shift
):
    seqs, rows, width = ctx.shape
    length, slots = xc.shape[1], xq.shape[1]
    ff = w_inner.shape[1]
    total = seqs * rows

    def by_seq(n):
        return pl.BlockSpec((1, n, width), lambda s: (jnp.minimum(s, seqs - 1), 0, 0))

    def block(n):
        return pl.BlockSpec((rows, n), lambda s: (jnp.minimum(s, seqs - 1), 0))

    grad_block = pl.BlockSpec(
        (GRAD_TILE, width), lambda s: (jnp.maximum(s - seqs, 0), 0)
    )
    hbm = pl.BlockSpec(memory_space=pl.ANY)
    return pl.pallas_call(
        rows_forward_kernel,
        grid_spec=pltpu.PrefetchScalarGridSpec(
            num_scalar_prefetch=0,
            grid=(seqs + ff // GRAD_TILE,),
            in_specs=[
            by_seq(rows), by_seq(length), by_seq(slots), by_seq(length), by_seq(slots),
            hbm, hbm, hbm,
            full_spec((2, width)), full_spec((1, ff)), full_spec((2, width)), full_spec((2, width)),
        ],
        out_specs=[
            by_seq(length), by_seq(slots), block(ff), block(width),
            block(width), block(TILE), block(width), full_spec((3, width)),
            grad_block,
        ],
        scratch_shapes=weight_scratch(width, ff) + [
            pltpu.VMEM((rows, width), F32),
            pltpu.VMEM((total, ff), BF16),
            pltpu.VMEM((total, width), BF16),
            pltpu.VMEM((3, 8, width), F32),
        ],
        ),
        out_shape=[
            jax.ShapeDtypeStruct((seqs, length, width), BF16),
            jax.ShapeDtypeStruct((seqs, slots, width), BF16),
            jax.ShapeDtypeStruct((total, ff), BF16),
            jax.ShapeDtypeStruct((total, width), BF16),
            jax.ShapeDtypeStruct((total, width), BF16),
            jax.ShapeDtypeStruct((total, TILE), F32),
            jax.ShapeDtypeStruct((total, width), BF16),
            jax.ShapeDtypeStruct((3, width), F32),
            jax.ShapeDtypeStruct((ff, width), BF16),
        ],
        compiler_params=params(),
        name="rows_forward",
    )(ctx, xc, xq, cot_c, cot_q, w_output, w_inner, w_outer, after, hidden_bias, gain, shift)


def rows_backward(half, seqs, slots, outer, slope, unit, scale, hidden, ctx, w_output, w_inner, w_outer, gain):
    total, width = outer.shape
    rows = total // seqs
    ff = w_inner.shape[1]
    tiles = 3
    wide = (ff + width) // 2

    def block(n):
        return pl.BlockSpec((rows, n), lambda s, half: (jnp.minimum(s, seqs - 1), 0))

    def by_seq(n):
        return pl.BlockSpec((1, n, width), lambda s, half: (jnp.minimum(s, seqs - 1), 0, 0))

    def grad_block(start):
        return pl.BlockSpec(
            (width, wide // tiles), lambda s, half: (0, jnp.clip(s - start, 0, tiles - 1))
        )

    hbm = pl.BlockSpec(memory_space=pl.ANY)
    return pl.pallas_call(
        rows_backward_kernel,
        grid_spec=pltpu.PrefetchScalarGridSpec(
            num_scalar_prefetch=1,
            grid=(seqs + 2 * tiles,),
            in_specs=[
                block(width), block(ff), block(width), block(TILE),
                full_spec((total, width)), full_spec((total, width)),
                hbm, hbm, hbm, full_spec((2, width)),
            ],
            out_specs=[
                by_seq(rows - slots), by_seq(slots), by_seq(rows),
                full_spec((3, width)), full_spec((1, ff)),
                grad_block(seqs), grad_block(seqs + tiles),
            ],
            scratch_shapes=weight_scratch(width, ff) + [
                pltpu.VMEM((rows, width), F32),
                pltpu.VMEM((total, ff), BF16),
                pltpu.VMEM((total, width), BF16),
                pltpu.VMEM((width, total), BF16),
                pltpu.VMEM((width, total), BF16),
                pltpu.VMEM((3, 8, width), F32),
                pltpu.VMEM((8, ff), F32),
            ],
        ),
        out_shape=[
            jax.ShapeDtypeStruct((seqs, rows - slots, width), F32),
            jax.ShapeDtypeStruct((seqs, slots, width), F32),
            jax.ShapeDtypeStruct((seqs, rows, width), BF16),
            jax.ShapeDtypeStruct((3, width), F32),
            jax.ShapeDtypeStruct((1, ff), F32),
            jax.ShapeDtypeStruct((width, wide), BF16),
            jax.ShapeDtypeStruct((width, wide), BF16),
        ],
        compiler_params=params(),
        name="rows_backward",
    )(half, outer, slope, unit, scale, hidden, ctx, w_output, w_inner, w_outer, gain)


def grad_before_kernel(xc, xq, dq, dk, dv, *rest):
    out = rest[-1]
    length = xc.shape[1]
    wide = dq.shape[2]
    q_sum = k_sum = v_sum = None
    for s in range(xc.shape[0]):
        turned = jnp.concatenate([xc[s], xq[s]], axis=0).T
        q_sum = plus(q_sum, nn(turned, dq[s]))
        k_sum = plus(k_sum, nn(turned[:, :length], dk[s]))
        v_sum = plus(v_sum, nn(turned[:, :length], dv[s]))
    for n, total in enumerate((q_sum, k_sum, v_sum)):
        cols = slice(n * wide, (n + 1) * wide)
        if len(rest) == 3:
            total = total + rest[1][:, cols].astype(F32)
        out[:, cols] = total.astype(BF16)
    if len(rest) == 3:
        out[:, 3 * wide :] = rest[0][...].T.astype(BF16)


def grad_before(xc, xq, dq, dk, dv, vectors=None, got=None):
    seqs, length, width = xc.shape
    slots = xq.shape[1]
    wide = dq.shape[2]
    part = width // 2
    total = 3 * wide
    extra, extra_specs = [], []
    if vectors is not None:
        total += vectors.shape[0]
        extra = [vectors, got]
        extra_specs = [
            pl.BlockSpec((vectors.shape[0], part), lambda i: (0, i)),
            pl.BlockSpec((part, 3 * wide), lambda i: (i, 0)),
        ]
    return pl.pallas_call(
        grad_before_kernel,
        grid=(2,),
        in_specs=[
            pl.BlockSpec((seqs, length, part), lambda i: (0, 0, i)),
            pl.BlockSpec((seqs, slots, part), lambda i: (0, 0, i)),
            full_spec(dq.shape), full_spec(dk.shape), full_spec(dv.shape),
        ] + extra_specs,
        out_specs=pl.BlockSpec((part, total), lambda i: (i, 0)),
        out_shape=jax.ShapeDtypeStruct((width, total), BF16),
        compiler_params=params(),
        name="grad_before",
    )(xc, xq, dq, dk, dv, *extra)


def input_grad_kernel(
    half, first_c, first_q, dq_o, dk_o, dv_o, dq_m, dk_m, dv_m, wq_o, wk_o, wv_o, wq_m, wk_m, wv_m,
    out_c, out_q,
):
    length = dk_o.shape[1]
    left = [dq_o[0, :length], dk_o[0], dv_o[0], dq_m[0, :length], dk_m[0], dv_m[0]]
    right = [wq_o[...], wk_o[...], wv_o[...], wq_m[...], wk_m[...], wv_m[...]]
    out_c[0] = first_c[0] + nt(jnp.concatenate(left, axis=1), jnp.concatenate(right, axis=1))
    dq = jnp.concatenate([dq_o[0, length:], dq_m[0, length:]], axis=1)
    wq = jnp.concatenate([wq_o[...], wq_m[...]], axis=1)
    out_q[0] = (first_q[0] + nt(dq, wq)).astype(BF16)


def input_grad(half, first_c, first_q, other, mine, wq, wk, wv):
    seqs, rows, part = other[0].shape
    length = other[1].shape[1]
    width = wq.shape[0]

    def by_seq(n, cols):
        return pl.BlockSpec((1, n, cols), lambda s, half: (s, 0, 0))

    grads = [by_seq(rows, part), by_seq(length, part), by_seq(length, part)]
    firsts = [by_seq(length, width), by_seq(rows - length, width)]
    w_other = pl.BlockSpec((width, part), lambda s, half: (0, 1 - half[0]))
    w_mine = pl.BlockSpec((width, part), lambda s, half: (0, half[0]))
    return pl.pallas_call(
        input_grad_kernel,
        grid_spec=pltpu.PrefetchScalarGridSpec(
            num_scalar_prefetch=1,
            grid=(seqs,),
            in_specs=firsts + grads * 2 + [w_other] * 3 + [w_mine] * 3,
            out_specs=firsts,
        ),
        out_shape=[
            jax.ShapeDtypeStruct((seqs, length, width), F32),
            jax.ShapeDtypeStruct((seqs, rows - length, width), BF16),
        ],
        compiler_params=params(),
        name="input_grad",
    )(half, first_c, first_q, *other, *mine, wq, wk, wv, wq, wk, wv)


def swap(value, axis, count, stride):
    return lax.ppermute(value, axis, [(i, i ^ stride) for i in range(count)])


def take(value, dim, index):
    return lax.dynamic_index_in_dim(value, index, dim, keepdims=False)


def low_sum(*terms):
    total = None
    for term in terms:
        total = plus(total, term.astype(F32))
    return total.astype(BF16)


def first_kernel(bits, *refs):
    terms, (send_a, send_b, keep_a, keep_b) = refs[:-4], refs[-4:]
    x, y = bits[0], bits[1]
    cut = send_a.shape[2]

    def total(g, row, col, rows):
        out = None
        for term in terms:
            out = plus(out, term[g, row, col, rows].astype(F32))
        return out.astype(BF16)

    for g in range(send_a.shape[0]):
        for n in range(2):
            send_a[g, n] = total(g, n, 1 - x, slice(0, cut))
            keep_a[g, n] = total(g, n, x, slice(0, cut))
            send_b[g, n] = total(g, 1 - y, n, slice(cut, 2 * cut))
            keep_b[g, n] = total(g, y, n, slice(cut, 2 * cut))


def second_kernel(bits, keep_a, keep_b, got_a, got_b, send_a, send_b, left_a, left_b):
    x, y = bits[0], bits[1]

    def total(keep, got, g, n):
        return (keep[g, n].astype(F32) + got[g, n].astype(F32)).astype(BF16)

    for g in range(send_a.shape[0]):
        send_a[g] = total(keep_a, got_a, g, 1 - y)
        left_a[g] = total(keep_a, got_a, g, y)
        send_b[g] = total(keep_b, got_b, g, 1 - x)
        left_b[g] = total(keep_b, got_b, g, x)


def third_kernel(bits, left_a, left_b, got_a, got_b, out):
    cut = left_a.shape[1]
    out[:, :cut] = (left_a[...].astype(F32) + got_a[...].astype(F32)).astype(BF16)
    out[:, cut:] = (left_b[...].astype(F32) + got_b[...].astype(F32)).astype(BF16)


def part_sum_kernel(parts, out):
    total = parts[0].astype(F32)
    for n in range(1, parts.shape[0]):
        total = total + parts[n].astype(F32)
    out[...] = total.astype(BF16)


def staged(kernel, bits, arrays, shapes, name):
    vmem = pl.BlockSpec(memory_space=pltpu.VMEM)
    return pl.pallas_call(
        kernel,
        in_specs=[pl.BlockSpec(memory_space=pltpu.SMEM)] + [vmem] * len(arrays),
        out_specs=[vmem] * len(shapes),
        out_shape=[jax.ShapeDtypeStruct(shape, BF16) for shape in shapes],
        compiler_params=params(),
        name=name,
    )(bits, *arrays)


class Reduction:
    def __init__(self, tok):
        self.tok = tok
        x = lax.axis_index("qry") // 2
        y = lax.axis_index("tok") % 2
        self.x = x
        self.bits = jnp.stack([x, y]).astype(jnp.int32)

    def first_sends(self, *terms):
        rows, cols = terms[0].shape
        deep = rows // self.tok // 2
        shape = (self.tok // 2, 2, 2, deep, cols)
        outs = [(self.tok // 2, 2, deep // 2, cols)] * 4
        *sends, self.keep_a, self.keep_b = staged(
            first_kernel, self.bits, [t.reshape(shape) for t in terms], outs, "first_sums"
        )
        return sends

    def first_moves(self, sends):
        return [swap(sends[0], "qry", 4, 2), swap(sends[1], "tok", self.tok, 1)]

    def second_sends(self, got):
        shape = self.keep_a.shape
        outs = [(shape[0],) + shape[2:]] * 4
        *sends, self.left_a, self.left_b = staged(
            second_kernel, self.bits, [self.keep_a, self.keep_b, *got], outs, "second_sums"
        )
        return sends

    def second_moves(self, sends):
        return [swap(sends[0], "tok", self.tok, 1), swap(sends[1], "qry", 4, 2)]

    def third_sends(self, got):
        rest, deep, cols = self.left_a.shape
        (out,) = staged(
            third_kernel, self.bits, [self.left_a, self.left_b, *got], [(rest, 2 * deep, cols)], "third_sums"
        )
        return out

    def third_moves(self, send):
        if self.tok == 2:
            return send
        groups = [list(range(bit, self.tok, 2)) for bit in range(2)]
        return lax.all_to_all(send, "tok", 0, 0, tiled=True, axis_index_groups=groups)

    def far_sends(self, got):
        self.own = pl.pallas_call(
            part_sum_kernel,
            out_shape=jax.ShapeDtypeStruct(got.shape[1:], BF16),
            name="part_sums",
        )(got)
        return self.own

    def far_moves(self, send):
        return swap(send, "qry", 4, 2)

    def near_sends(self, got):
        low = self.x == 0
        self.own = jnp.concatenate(
            [jnp.where(low, self.own, got), jnp.where(low, got, self.own)], axis=0
        )
        return self.own

    def near_moves(self, send):
        return swap(send, "qry", 4, 1)


def beside(transfers, compute=None, arrays=()):
    moves = [move for move, _ in transfers]
    sends = [send for _, send in transfers]
    sends, arrays = lax.optimization_barrier((sends, tuple(arrays)))
    got = [move(send) for move, send in zip(moves, sends)]
    out = compute(*arrays) if compute is not None else ()
    return lax.optimization_barrier((got, out))


def in_core_order(first, own, got):
    a, b = own[...].astype(F32), got[...].astype(F32)
    return jnp.where(first, a, b), jnp.where(first, b, a)


def place_outer_kernel(core, own, got, outer):
    part = own.shape[1]
    first, second = in_core_order(core[0] == 0, own, got)
    outer[:, :part] = first
    outer[:, part:] = second


def place_inner_kernel(core, own, got, inner, output):
    tiles = 3
    wide, narrow = inner.shape[1] // 2 // tiles, output.shape[1] // 2 // tiles
    for n, half in enumerate(in_core_order(core[0] == 0, own, got)):
        for t in range(tiles):
            at = t * (wide + narrow)
            to = (n * tiles + t) * wide
            inner[:, to : to + wide] = half[:, at : at + wide]
            to = (n * tiles + t) * narrow
            output[:, to : to + narrow] = half[:, at + wide : at + wide + narrow]


def place_before_kernel(core, own, got, query, key, value, *vectors):
    part = query.shape[1] // 2
    first, second = in_core_order(core[0] == 0, own, got)
    for n, ref in enumerate((query, key, value)):
        ref[:, :part] = first[:, n * part : (n + 1) * part]
        ref[:, part:] = second[:, n * part : (n + 1) * part]
    every = (first[:, 3 * part :] + second[:, 3 * part :]).T
    at = 0
    for ref in vectors:
        ref[...] = every[at : at + ref.shape[0]]
        at += ref.shape[0]


def place_sums(kernel, core, own, got, shapes):
    vmem = pl.BlockSpec(memory_space=pltpu.VMEM)
    return pl.pallas_call(
        kernel,
        in_specs=[pl.BlockSpec(memory_space=pltpu.SMEM), vmem, vmem],
        out_specs=[vmem] * len(shapes),
        out_shape=[jax.ShapeDtypeStruct(shape, F32) for shape in shapes],
        name="place_sums",
    )(core, own, got)


def on_device(
    content_in, query_in, seq_lengths, perm_ranks, w_query, w_key, w_value, w_output, w_inner,
    w_outer, b_before, b_after, b_hidden, norm_gain, norm_shift, rel_table, cot_content, cot_query,
    tok,
):
    seqs, length, width = content_in.shape
    group = lax.axis_index("qry")
    core = group % 2
    other = jnp.reshape(1 - core, (1,)).astype(jnp.int32)
    mine = jnp.reshape(core, (1,)).astype(jnp.int32)
    lengths = lax.dynamic_slice_in_dim(seq_lengths, group * seqs, seqs)
    ranks = lax.dynamic_slice_in_dim(perm_ranks, group * seqs, seqs, 0)

    both = jnp.concatenate([query_in, cot_query], axis=2)
    (both,), (q_content, k, v) = beside(
        [(lambda a: lax.all_to_all(a, "qry", 0, 1, tiled=True), both)],
        lambda: project(content_in, w_query, w_key, w_value, b_before),
    )
    xq, cot_q = both[:, :, :width], both[:, :, width:]
    slots = xq.shape[1]
    floor = lengths[:, None] - PRED
    thr_c = jnp.maximum(floor, jnp.minimum(ranks, lengths[:, None]))[:, :, None]
    thr_q = (floor + jnp.arange(slots, dtype=jnp.int32)[None, :])[:, :, None]
    rank_row = ranks[:, None, :]
    place = jnp.arange(512, dtype=jnp.int32)
    one_hot = bucket_of(jnp.where(place < 384, place, place - 512) - 128)
    one_hot = (one_hot[None, :] == jnp.arange(BUCKETS, dtype=jnp.int32)[:, None]).astype(BF16)
    offsets = jnp.dot(rel_table, one_hot, preferred_element_type=F32)[:, None, :]

    ctx, e, rr, q = attention_forward(
        q_content, k, v, xq, w_query, b_before, rank_row, thr_c, thr_q, offsets,
        rel_table.astype(F32),
    )
    (out_c, out_q, slope, hidden, unit, scale, outer, sums_f, g_outer) = rows_forward(
        ctx, content_in, xq, cot_content, cot_q, w_output, w_inner, w_outer, b_after,
        b_hidden[None], norm_gain, norm_shift,
    )
    ff = slope.shape[1]
    share = width // tok
    part = width // 2

    red_i = Reduction(tok)
    red_b = Reduction(tok)

    def slot_blocks(a):
        a = a.reshape(seqs, 4, slots // 4, a.shape[2])
        return [take(a, 1, group ^ n) for n in range(4)]

    def slot_moves(blocks):
        return [swap(blocks[n], "qry", 4, n) for n in range(1, 4)]

    def slot_rows(own, got):
        every = jnp.stack([own, *got])
        return jnp.concatenate([take(every, 0, group ^ n) for n in range(4)], axis=0)

    def swap_core(a):
        return swap(a, "qry", 4, 1)

    def over_tok(a):
        return lax.psum_scatter(a, "tok", scatter_dimension=0, tiled=True)

    o_sum = over_tok(g_outer)
    first_c, first_q, d_ctx, sums_b, inner_sums, i_other, i_mine = rows_backward(
        mine, seqs, slots, outer, slope, unit, scale, hidden, ctx.reshape(-1, width), w_output,
        w_inner, w_outer, norm_gain,
    )
    (got_i,), back_other = beside(
        [(swap_core, i_other)],
        lambda a: attention_backward(other, q, k, v, e, ctx, a, rr, rank_row, thr_q),
        (d_ctx,),
    )

    def grad_and_backward(dq, dk, dv, cotangent):
        b_other = grad_before(content_in, xq, dq, dk, dv)
        b_other, cotangent = lax.optimization_barrier((b_other, cotangent))
        got = swap_core(b_other)
        return got, attention_backward(mine, q, k, v, e, ctx, cotangent, rr, rank_row, thr_q)

    (got_i,), (got_b, back_mine) = beside(
        [(red_i.first_moves, red_i.first_sends(i_mine, got_i))],
        grad_and_backward,
        (*back_other[:3], d_ctx),
    )

    def in_order(a, b, axis):
        return jnp.where(
            core == 0, jnp.concatenate([b, a], axis=axis), jnp.concatenate([a, b], axis=axis)
        )

    table = in_order(back_other[4], back_mine[4], 0)[:, :, :BUCKETS]
    table = jnp.tile(table.reshape(-1, share), (1, tok))
    wide_sums = jnp.swapaxes(inner_sums.reshape(tok, ff // width, share), 0, 1)
    vectors = jnp.concatenate(
        [
            in_order(back_other[3], back_mine[3], 1),
            sums_b[2:], sums_f[2:], sums_b[:1], sums_f[:1], sums_b[1:2], sums_f[1:2],
            wide_sums.reshape(-1, width), table,
        ]
    )
    vectors = jnp.pad(vectors, ((0, TILE - vectors.shape[0]), (0, 0)))
    o_parts = o_sum.reshape(ff // tok, 2, part)
    (got_i, got_o), b_mine = beside(
        [
            (red_i.second_moves, red_i.second_sends(got_i)),
            (swap_core, take(o_parts, 1, 1 - core)),
        ],
        lambda a: grad_before(content_in, xq, a, *back_mine[1:3], vectors, got_b),
        (back_mine[0],),
    )
    o_sum = low_sum(take(o_parts, 1, core), got_o)
    send_i = red_i.third_sends(got_i)
    send_b = red_b.first_sends(b_mine)
    send_i, send_b, first_c = lax.optimization_barrier((send_i, send_b, first_c))
    got_i = red_i.third_moves(send_i)
    got_b = red_b.first_moves(send_b)
    d_content, d_query = input_grad(
        mine, first_c, first_q, back_other[:3], back_mine[:3], w_query, w_key, w_value
    )
    got_b, d_content, d_query = lax.optimization_barrier((got_b, d_content, d_query))
    (got_b,), rows_q = beside(
        [(red_b.second_moves, red_b.second_sends(got_b))],
        lambda *a: slot_blocks(jnp.concatenate(a, axis=2)),
        (out_q, d_query),
    )

    def swap_x(a):
        return swap(a, "qry", 4, 2)

    (got_b, got_i, got_o, got_q), _ = beside(
        [
            (red_b.third_moves, red_b.third_sends(got_b)),
            (red_i.far_moves, red_i.far_sends(got_i)),
            (swap_x, o_sum),
            (slot_moves, rows_q),
        ],
    )
    o_sum = low_sum(o_sum, got_o)
    (got_b, got_o, got_i), rows_q = beside(
        [
            (red_b.far_moves, red_b.far_sends(got_b)),
            (swap_core, o_sum),
            (red_i.near_moves, red_i.near_sends(got_i)),
        ],
        lambda *a: slot_rows(a[0], a[1:]),
        (rows_q[0], *got_q),
    )
    out_q, d_query = rows_q[:, :, :width], rows_q[:, :, width:].astype(F32)
    (got_b,), ((g_outer,), (g_inner, g_output)) = beside(
        [(red_b.near_moves, red_b.near_sends(got_b))],
        lambda a, b: (
            place_sums(place_outer_kernel, mine, o_sum, a, [(ff // tok, width)]),
            place_sums(place_inner_kernel, mine, red_i.own, b, [(share, ff), (share, width)]),
        ),
        (got_o, got_i),
    )
    pair = (2, share)
    (
        g_query, g_key, g_value, g_before, g_after, g_gain, g_shift, g_hidden, g_table,
    ) = place_sums(
        place_before_kernel, mine, red_b.own, got_b,
        [(share, width)] * 3 + [pair] * 4
        + [(ff // width, share), (HEADS * BUCKETS // share, share)],
    )
    return (
        out_c, out_q, d_content, d_query, g_query, g_key, g_value, g_output, g_inner, g_outer,
        g_before, g_after, g_hidden.reshape(-1), g_gain, g_shift, g_table.reshape(HEADS, BUCKETS),
    )


def solution(mesh):
    rows = P(("tok", "qry"), None, None)
    slots = P("tok", "qry", None)
    return jax.shard_map(
        functools.partial(on_device, tok=mesh.shape["tok"]),
        mesh=mesh,
        in_specs=(rows, slots, P("tok"), P("tok", None)) + (P(),) * 12 + (rows, slots),
        out_specs=(rows, slots, rows, slots)
        + (P("tok", None),) * 6
        + (P(None, "tok"), P(None, "tok"), P("tok"), P(None, "tok"), P(None, "tok"), P()),
        check_vma=False,
    )
```

```python
import functools

import jax
import jax.numpy as jnp
from jax import lax
from jax.experimental import pallas as pl
from jax.experimental.pallas import tpu as pltpu
from jax.sharding import PartitionSpec as P

HEADS = 12
HEAD = 64
BUCKETS = 32
PRED = 80
EPS = 1e-05
NEG = -1e30
BORDERS = (12, 16, 23, 32, 46, 64, 91)
LOG2E = 1.4426950408889634
LN2 = 0.6931471805599453
SQRT_HALF = 0.7071067811865476
INV_ROOT = 0.3989422804014327
F32 = jnp.float32
BF16 = jnp.bfloat16
PAIRS = HEADS // 2
TILE = 128
VMEM_LIMIT = 60 * 1024 * 1024
STEP = 320
BACK_STEP = 256
SUB = 64
CHUNK = 768
GRAD_TILE = 1024


def nn(a, b):
    return lax.dot_general(a, b, (((1,), (0,)), ((), ())), preferred_element_type=F32)


def nt(a, b):
    return lax.dot_general(a, b, (((1,), (1,)), ((), ())), preferred_element_type=F32)


def tn(a, b):
    return lax.dot_general(a, b, (((0,), (0,)), ((), ())), preferred_element_type=F32)


def bucket_of(offset):
    distance = jnp.abs(offset)
    beyond = 8 + sum(((distance >= border).astype(jnp.int32) for border in BORDERS))
    return jnp.where(distance < 8, distance, beyond) + 16 * (offset > 0).astype(jnp.int32)


def full_spec(shape):
    zeros = (0,) * len(shape)
    return pl.BlockSpec(shape, lambda *_: zeros, pipeline_mode=pl.Buffered(1))


def params():
    return pltpu.CompilerParams(vmem_limit_bytes=VMEM_LIMIT)


def slot_position(rank_row, slot_rank, width):
    lanes = lax.broadcasted_iota(jnp.int32, (1, width), 1).astype(F32)
    place = jnp.sum(jnp.where(rank_row == slot_rank, lanes, 0.0), axis=1, keepdims=True)
    place = place.astype(jnp.int32)
    return place >> 7, place & 127


def pieces(start, size, length, sub):
    at = start
    while at < start + size:
        limit = length if at < length else start + size
        many = min(sub, start + size - at, limit - at)
        yield at, many
        at += many


def row_steps(total, step):
    return [(at, min(step, total - at)) for at in range(0, total, step)]


def plus(total, term):
    return term if total is None else total + term


Q_SCALE = 0.125 * LOG2E


def project_kernel(xc, wq, wk, wv, before, q_out, k_out, v_out):
    x = xc[0]
    bias = before[...].astype(F32)
    q_out[0] = ((nn(x, wq[...]) + bias[0:1]) * Q_SCALE).astype(BF16)
    k_out[0] = nn(x, wk[...]).astype(BF16)
    v_out[0] = (nn(x, wv[...]) + bias[1:2]).astype(BF16)


def project(xc, wq, wk, wv, before):
    seqs, length, width = xc.shape
    rows = pl.BlockSpec((1, length, width), lambda s: (s, 0, 0))
    weight = full_spec((width, width))
    return pl.pallas_call(
        project_kernel,
        grid=(seqs,),
        in_specs=[rows, weight, weight, weight, full_spec((2, width))],
        out_specs=[rows] * 3,
        out_shape=[jax.ShapeDtypeStruct(xc.shape, BF16)] * 3,
        compiler_params=params(),
        name="project",
    )(xc, wq, wk, wv, before)


def attention_forward_kernel(
    q_in, k_in, v_in, xq, wq, before, rank_row, thr_c, thr_q, offsets, table,
    ctx_out, e_out, rr_out, q_out, mask, s_buf,
):
    pair = pl.program_id(1)
    length = q_in.shape[1]
    slots = xq.shape[1]
    total = length + slots
    tiles = length // TILE

    @pl.when(pair == 0)
    def _():
        bias = before[...].astype(F32)[0:1]
        q_out[0, :length] = q_in[0]
        q_out[0, length:] = ((nn(xq[0], wq[...]) + bias) * Q_SCALE).astype(BF16)
        ranks = rank_row[0]
        for i in range(tiles):
            rows = slice(i * TILE, (i + 1) * TILE)
            seen = ranks < thr_c[0, rows]
            row = lax.broadcasted_iota(jnp.int32, (TILE, length), 0) + i * TILE
            col = lax.broadcasted_iota(jnp.int32, (TILE, length), 1)
            mask[rows] = jnp.where(seen | (row == col), 0.0, NEG)
        mask[length:] = jnp.where(ranks < thr_q[0], 0.0, NEG)

    cols = pl.ds(pl.multiple_of(pair * TILE, TILE), TILE)
    k_pair = k_in[0, :, cols]
    v_pair = v_in[0, :, cols]
    q_pair = q_out[0, :, cols]
    lane = lax.broadcasted_iota(jnp.int32, (1, TILE), 1)
    block_of, row_of = slot_position(rank_row[0], thr_q[0], length)
    pick = (row_of == lax.broadcasted_iota(jnp.int32, (slots, TILE), 1)).astype(BF16)
    zero = jnp.zeros((), BF16)
    setup = []
    for h in range(2):
        own = (lane < HEAD) if h == 0 else (lane >= HEAD)
        strip = pltpu.roll(
            jnp.broadcast_to(offsets[h], (TILE, 512)), 0, 1, stride=1, stride_axis=0
        )[:, : 3 * TILE]
        setup.append((
            jnp.where(own, q_pair, zero),
            jnp.where(own, v_pair, zero),
            strip * LOG2E,
            nn(pick, strip.astype(BF16)) * LOG2E,
            table[2 * pair + h, 15] * LOG2E,
            table[2 * pair + h, 31] * LOG2E,
        ))
    inverse = {}
    context = {}

    def scores(h, at, size):
        s_buf[h, at : at + size] = nt(setup[h][0][at : at + size], k_pair)

    def normalise(h, at, size):
        strip, slot_strip, far_low, far_high = setup[h][2:]
        for t, m in pieces(at, size, length, SUB):
            s = s_buf[h, t : t + m]
            parts = []
            for j in range(tiles):
                if t < length:
                    i, a = t // TILE, t % TILE
                    d = j - i + 1
                    if 0 <= d <= 2:
                        bias = strip[a : a + m, d * TILE : (d + 1) * TILE]
                    else:
                        bias = far_high if j > i else far_low
                else:
                    a = t - length
                    away = j - block_of[a : a + m]
                    bias = jnp.where(away >= 2, far_high, far_low)
                    for d in range(3):
                        near = slot_strip[a : a + m, d * TILE : (d + 1) * TILE]
                        bias = jnp.where(away == d - 1, near, bias)
                parts.append(s[:, j * TILE : (j + 1) * TILE] + bias)
            s = jnp.concatenate(parts, axis=1) + mask[t : t + m]
            top = jnp.max(s, axis=1, keepdims=True)
            e = jnp.exp2(s - top)
            e_out[0, h, t : t + m] = e.astype(BF16)
            inverse[h, t] = 1.0 / jnp.sum(e, axis=1, keepdims=True)

    def attend(h, at, size):
        context[h, at] = nn(e_out[0, h, at : at + size], setup[h][1])
        if h == 0:
            return
        both = context.pop((0, at)) + context.pop((1, at))
        for t, m in pieces(at, size, length, SUB):
            r = jnp.where(lane < HEAD, inverse[0, t], inverse[1, t])
            rr_out[0, t : t + m] = r
            ctx_out[0, t : t + m] = (both[t - at : t - at + m] * r).astype(BF16)

    work = [(h, at, size) for at, size in row_steps(total, STEP) for h in range(2)]
    scores(*work[0])
    for n, item in enumerate(work):
        if n + 1 < len(work):
            scores(*work[n + 1])
        normalise(*item)
        if n:
            attend(*work[n - 1])
    attend(*work[-1])


def attention_forward(q, k, v, xq, wq, before, rank_row, thr_c, thr_q, offsets, table):
    seqs, length, width = q.shape
    slots = xq.shape[1]
    rows = length + slots

    def by_seq(shape):
        return pl.BlockSpec((1,) + shape, lambda s, p: (s, 0, 0))

    by_pair = pl.BlockSpec((1, rows, TILE), lambda s, p: (s, 0, p))
    return pl.pallas_call(
        attention_forward_kernel,
        grid=(seqs, PAIRS),
        in_specs=[
            by_seq((length, width)),
            by_seq((length, width)),
            by_seq((length, width)),
            by_seq((slots, width)),
            full_spec((width, width)),
            full_spec((2, width)),
            by_seq((1, length)),
            by_seq((length, 1)),
            by_seq((slots, 1)),
            pl.BlockSpec((2, 1, 512), lambda s, p: (p, 0, 0)),
            pl.BlockSpec(memory_space=pltpu.SMEM),
        ],
        out_specs=[
            by_pair,
            pl.BlockSpec((1, 2, rows, length), lambda s, p: (s, p, 0, 0)),
            by_pair,
            by_seq((rows, width)),
        ],
        out_shape=[
            jax.ShapeDtypeStruct((seqs, rows, width), BF16),
            jax.ShapeDtypeStruct((seqs, HEADS, rows, length), BF16),
            jax.ShapeDtypeStruct((seqs, rows, width), F32),
            jax.ShapeDtypeStruct((seqs, rows, width), BF16),
        ],
        scratch_shapes=[pltpu.VMEM((rows, length), F32), pltpu.VMEM((2, rows, length), F32)],
        compiler_params=params(),
        name="attention_forward",
    )(q, k, v, xq, wq, before, rank_row, thr_c, thr_q, offsets, table)


def attention_backward_kernel(
    first, q, k, v, e_in, ctx, d_ctx, rr, rank_row, thr_q,
    dq_out, dk_out, dv_out, sums, table_out, near_acc, far_acc, dp_buf, ds_buf, sums_acc,
):
    seq = pl.program_id(1)
    length = k.shape[1]
    slots = thr_q.shape[1]
    total = length + slots
    tiles = length // TILE

    @pl.when(seq == 0)
    def _():
        near_acc[...] = jnp.zeros_like(near_acc)
        far_acc[...] = jnp.zeros_like(far_acc)
        sums_acc[...] = jnp.zeros_like(sums_acc)

    lane = lax.broadcasted_iota(jnp.int32, (1, TILE), 1)
    block_of, row_of = slot_position(rank_row[0], thr_q[0], length)
    pick = (row_of == lax.broadcasted_iota(jnp.int32, (slots, TILE), 1)).astype(BF16)
    q_pair, k_pair, v_pair = q[0], k[0], v[0]
    d_context = d_ctx[0].astype(F32) * rr[0]
    product = d_context * ctx[0].astype(F32)
    zero = jnp.zeros((), BF16)
    low_d = d_context.astype(BF16)
    d_turned, q_turned = low_d.T, q_pair.T
    setup = []
    for h in range(2):
        own = (lane < HEAD) if h == 0 else (lane >= HEAD)
        setup.append((
            jnp.where(own, k_pair, zero),
            jnp.where(own, low_d, zero),
            jnp.sum(jnp.where(own, product, 0.0), axis=1, keepdims=True),
        ))
    near = [[{}, {}, {}], [{}, {}, {}]]
    far = [[None, None], [None, None]]
    spread = [None, None]
    dq, dk, dv = {}, [None, None], [None, None]

    def fold(x):
        return jnp.sum(x.reshape(-1, 8, TILE), axis=0)

    def d_probs(h, at, size):
        dp_buf[h, at : at + size] = nt(setup[h][1][at : at + size], v_pair)

    def d_scores(h, at, size):
        for t, m in pieces(at, size, length, SUB):
            ds = e_in[0, h, t : t + m].astype(F32) * (dp_buf[h, t : t + m] - setup[h][2][t : t + m])
            ds_buf[h, t : t + m] = ds.astype(BF16)
            parts = [ds[:, j * TILE : (j + 1) * TILE] for j in range(tiles)]
            if t < length:
                i, a = t // TILE, t % TILE
                for j in range(tiles):
                    if abs(j - i) <= 1:
                        group = near[h][j - i + 1]
                        group[a] = plus(group.get(a), parts[j])
                    else:
                        side = 1 if j > i else 0
                        far[h][side] = plus(far[h][side], fold(parts[j]))
            else:
                a = t - length
                slot_near = [0.0] * 3
                low = high = 0.0
                for j in range(tiles):
                    away = j - block_of[a : a + m]
                    for d in range(3):
                        slot_near[d] = slot_near[d] + jnp.where(away == d - 1, parts[j], 0.0)
                    high = high + jnp.where(away >= 2, parts[j], 0.0)
                    low = low + jnp.where(away <= -2, parts[j], 0.0)
                far[h][0] = plus(far[h][0], fold(low))
                far[h][1] = plus(far[h][1], fold(high))
                slot_near = jnp.concatenate(slot_near, axis=1).astype(BF16)
                spread[h] = plus(spread[h], tn(pick[a : a + m], slot_near))

    def d_queries(h, at, size):
        dq[at] = plus(dq.get(at), nn(ds_buf[h, at : at + size], setup[h][0]))

    def d_values(h):
        dv[h] = nn(d_turned[h * HEAD : (h + 1) * HEAD], e_in[0, h])

    def d_keys(h):
        dk[h] = nn(q_turned[h * HEAD : (h + 1) * HEAD], ds_buf[h])

    steps = row_steps(total, BACK_STEP)
    work = [(h, at, size) for h in range(2) for at, size in steps]
    d_probs(*work[0])
    d_values(0)
    for n, item in enumerate(work):
        if n + 1 < len(work):
            d_probs(*work[n + 1])
        d_scores(*item)
        if n == len(steps) - 1:
            d_values(1)
        if n:
            d_queries(*work[n - 1])
        if n == len(steps):
            d_keys(0)
    d_queries(*work[-1])
    d_keys(1)

    for h in range(2):
        columns = [
            jnp.concatenate([group[a] for a in sorted(group)], axis=0) for group in near[h]
        ]
        near_acc[h] += jnp.concatenate(columns, axis=1) + spread[h]
        far_acc[h, 0] += far[h][0]
        far_acc[h, 1] += far[h][1]
    dq_sum = None
    for at, size in steps:
        low = (dq[at] * 0.125).astype(BF16)
        dq_out[0, at : at + size] = low
        dq_sum = plus(dq_sum, fold(low.astype(F32)))
    dk_out[0] = (jnp.concatenate(dk, axis=0).T * LN2).astype(BF16)
    low = jnp.concatenate(dv, axis=0).T.astype(BF16)
    dv_out[0] = low
    sums_acc[0] += dq_sum
    sums_acc[1] += fold(low.astype(F32))

    @pl.when(seq == pl.num_programs(1) - 1)
    def _():
        for n in range(2):
            sums[n : n + 1] = jnp.sum(sums_acc[n], axis=0, keepdims=True)
        row = lax.broadcasted_iota(jnp.int32, (8, 512), 0)
        place = lax.broadcasted_iota(jnp.int32, (512, TILE), 0)
        bucket = bucket_of(jnp.where(place < 384, place, place - 512) - 128)
        column = lax.broadcasted_iota(jnp.int32, (512, TILE), 1)
        one_hot = (bucket == column).astype(BF16)
        lane32 = lax.broadcasted_iota(jnp.int32, (1, TILE), 1)
        for h in range(2):
            x = jnp.concatenate([near_acc[h], jnp.zeros((TILE, 512 - 3 * TILE), F32)], axis=1)
            half = TILE // 2
            while half >= 8:
                x = x[:half] + pltpu.roll(x[half:], 512 - half, 1)
                half //= 2
            for bit in (4, 2, 1):
                x = jnp.where((row & bit) != 0, pltpu.roll(x, 512 - bit, 1), x)
            high = x.astype(BF16)
            rest = (x - high.astype(F32)).astype(BF16)
            total_h = jnp.sum(nn(high, one_hot) + nn(rest, one_hot), axis=0, keepdims=True)
            low_far = jnp.sum(far_acc[h, 0])
            high_far = jnp.sum(far_acc[h, 1])
            total_h = total_h + jnp.where(lane32 == 15, low_far, 0.0)
            table_out[0, h : h + 1] = total_h + jnp.where(lane32 == 31, high_far, 0.0)


def attention_backward(half, q, k, v, e, ctx, d_ctx, rr, rank_row, thr_q):
    seqs, length, width = k.shape
    rows = q.shape[1]
    slots = rows - length
    count = PAIRS // 2

    def pick(n):
        return pl.BlockSpec((1, n, TILE), lambda p, s, half: (s, 0, half[0] * count + p))

    def put(n):
        return pl.BlockSpec((1, n, TILE), lambda p, s, half: (s, 0, p))

    def by_seq(shape):
        return pl.BlockSpec((1,) + shape, lambda p, s, half: (s, 0, 0))

    wide = count * TILE
    return pl.pallas_call(
        attention_backward_kernel,
        grid_spec=pltpu.PrefetchScalarGridSpec(
            num_scalar_prefetch=1,
            grid=(count, seqs),
            in_specs=[
                pick(rows), pick(length), pick(length),
                pl.BlockSpec(
                    (1, 2, rows, length), lambda p, s, half: (s, half[0] * count + p, 0, 0)
                ),
                pick(rows), pick(rows), pick(rows),
                by_seq((1, length)), by_seq((slots, 1)),
            ],
            out_specs=[
                put(rows), put(length), put(length),
                pl.BlockSpec((2, TILE), lambda p, s, half: (0, p)),
                pl.BlockSpec((1, 2, TILE), lambda p, s, half: (p, 0, 0)),
            ],
            scratch_shapes=[
                pltpu.VMEM((2, TILE, 3 * TILE), F32),
                pltpu.VMEM((2, 2, 8, TILE), F32),
                pltpu.VMEM((2, rows, length), F32),
                pltpu.VMEM((2, rows, length), BF16),
                pltpu.VMEM((2, 8, TILE), F32),
            ],
        ),
        out_shape=[
            jax.ShapeDtypeStruct((seqs, rows, wide), BF16),
            jax.ShapeDtypeStruct((seqs, length, wide), BF16),
            jax.ShapeDtypeStruct((seqs, length, wide), BF16),
            jax.ShapeDtypeStruct((2, wide), F32),
            jax.ShapeDtypeStruct((count, 2, TILE), F32),
        ],
        compiler_params=params(),
        name="attention_backward",
    )(half, q, k, v, e, ctx, d_ctx, rr, rank_row, thr_q)


def normal_parts(u):
    density = jnp.exp2((-0.5 * LOG2E) * (u * u))
    t = 1.0 / (1.0 + (0.3275911 * SQRT_HALF) * jnp.abs(u))
    tail = t * (
        0.127414796
        + t * (-0.142248368 + t * (0.7107068705 + t * (-0.7265760135 + t * 0.5307027145)))
    )
    tail = tail * density
    return jnp.where(u >= 0, 1.0 - tail, tail), density


def norm_parts(u):
    mean = jnp.mean(u, axis=1, keepdims=True)
    centre = u - mean
    spread = jnp.mean(centre * centre, axis=1, keepdims=True)
    scale = lax.rsqrt(spread + EPS)
    return centre * scale, scale


def norm_back(y, gain, unit, scale):
    e = y * gain
    mean = jnp.mean(e, axis=1, keepdims=True)
    along = jnp.mean(e * unit, axis=1, keepdims=True)
    return (e - mean - unit * along) * scale


def column_sum(x):
    return jnp.sum(x.reshape(-1, 8, x.shape[1]), axis=0)


def weight_copies(w_output, w_inner, w_outer, wo, wi, wu, sems, forward):
    first = [pltpu.make_async_copy(w_output, wo, sems.at[0])]
    chunks = []
    for n in range(w_inner.shape[1] // CHUNK):
        part = pl.ds(n * CHUNK, CHUNK)
        inner = pltpu.make_async_copy(w_inner.at[:, part], wi.at[:, part], sems.at[1 + 2 * n])
        outer = pltpu.make_async_copy(w_outer.at[part], wu.at[part], sems.at[2 + 2 * n])
        chunks += [inner, outer] if forward else [outer, inner]
    return first + chunks if forward else chunks + first


def weight_scratch(width, ff):
    return [
        pltpu.VMEM((width, width), BF16),
        pltpu.VMEM((width, ff), BF16),
        pltpu.VMEM((ff, width), BF16),
        pltpu.SemaphoreType.DMA((1 + 2 * (ff // CHUNK),)),
    ]


def rows_forward_kernel(
    ctx, xc, xq, cot_c, cot_q, w_output, w_inner, w_outer, after, hidden_bias, gain, shift,
    out_c, out_q, slope_out, hidden_out, unit_out, scale_out, outer_out, sums, grad_out,
    wo, wi, wu, sems, acc, act, outer, sums_acc,
):
    step = pl.program_id(0)
    seqs = pl.num_programs(0) - act.shape[1] // GRAD_TILE
    rows = acc.shape[0]

    def row_part():
        copies = weight_copies(w_output, w_inner, w_outer, wo, wi, wu, sems, True)

        @pl.when(step == 0)
        def _():
            for copy in copies:
                copy.start()

        def ready(n):
            @pl.when(step == 0)
            def _():
                copies[n].wait()

        at = pl.multiple_of(step * rows, 16)
        length = xc.shape[1]
        after_f, gain_f, shift_f = (a[...].astype(F32) for a in (after, gain, shift))
        stream = jnp.concatenate([xc[0], xq[0]], axis=0).astype(F32)
        ready(0)
        first = stream + nn(ctx[0], wo[...]) + after_f[0:1]
        unit, scale = norm_parts(first)
        unit_out[...] = unit.astype(BF16)
        scale_out[...] = jnp.broadcast_to(scale, scale_out.shape)
        hidden = unit * gain_f[0:1] + shift_f[0:1]
        low = hidden.astype(BF16)
        hidden_out[...] = low
        acc[...] = hidden + after_f[1:2]
        for n in range(wi.shape[1] // CHUNK):
            part = slice(n * CHUNK, (n + 1) * CHUNK)
            if n == 0:
                for number in range(1, len(copies)):
                    ready(number)
            u = nn(low, wi[:, part]) + hidden_bias[:, part].astype(F32)
            phi, density = normal_parts(u)
            active = (u * phi).astype(BF16)
            act[pl.ds(at, rows), part] = active
            slope_out[:, part] = (phi + u * density * INV_ROOT).astype(BF16)
            acc[...] += nn(active, wu[part, :])
        unit2, scale2 = norm_parts(acc[...])
        out = (unit2 * gain_f[1:2] + shift_f[1:2]).astype(BF16)
        out_c[0] = out[:length]
        out_q[0] = out[length:]
        y = jnp.concatenate([cot_c[0], cot_q[0]], axis=0).astype(F32)
        d_second = norm_back(y, gain_f[1:2], unit2, scale2)
        d_outer = d_second.astype(BF16)
        outer_out[...] = d_outer
        outer[pl.ds(at, rows)] = d_outer
        terms = [column_sum(y * unit2), column_sum(y), column_sum(d_outer.astype(F32))]
        for n, term in enumerate(terms):
            sums_acc[n] += term
            sums[n : n + 1] = jnp.sum(sums_acc[n], axis=0, keepdims=True)

    @pl.when(step == 0)
    def _():
        for acc_ref in (sums_acc,):
            acc_ref[...] = jnp.zeros_like(acc_ref)

    @pl.when(step < seqs)
    def _():
        row_part()

    @pl.when(step >= seqs)
    def _():
        cols = pl.ds(pl.multiple_of((step - seqs) * GRAD_TILE, GRAD_TILE), GRAD_TILE)
        grad_out[...] = tn(act[:, cols], outer[...]).astype(BF16)


def rows_backward_kernel(
    half, outer, slope, unit, scale, hidden, ctx, w_output, w_inner, w_outer, gain,
    first_c, first_q, d_ctx, sums, inner_sums, grad_other, grad_mine,
    wo, wi, wu, sems, acc, inner, attended, hidden_t, ctx_t, sums_acc, inner_acc,
):
    step = pl.program_id(0)
    tiles = 3
    seqs = pl.num_programs(0) - 2 * tiles
    rows = acc.shape[0]
    width, ff = wi.shape

    def row_part():
        copies = weight_copies(w_output, w_inner, w_outer, wo, wi, wu, sems, False)

        @pl.when(step == 0)
        def _():
            for copy in copies:
                copy.start()

        def ready(n):
            @pl.when(step == 0)
            def _():
                copies[n].wait()

        at = pl.multiple_of(step * rows, 16)
        acc[...] = outer[...].astype(F32)
        chunks = ff // CHUNK
        for n in range(chunks):
            part = slice(n * CHUNK, (n + 1) * CHUNK)
            if n % 2 == 0:
                for number in range(2 * n, min(2 * n + 4, 2 * chunks)):
                    ready(number)
            d_act = nt(outer[...], wu[part, :])
            d_inner = (d_act * slope[:, part].astype(F32)).astype(BF16)
            inner[pl.ds(at, rows), part] = d_inner
            term = column_sum(d_inner.astype(F32))
            inner_acc[:, part] += term
            acc[...] += nt(d_inner, wi[:, part])
        inner_sums[...] = jnp.sum(inner_acc[...], axis=0, keepdims=True)
        unit1 = unit[...].astype(F32)
        d_hidden = acc[...]
        d_first = norm_back(d_hidden, gain[0:1].astype(F32), unit1, scale[:, :1])
        length = first_c.shape[1]
        first_c[0] = d_first[:length]
        first_q[0] = d_first[length:]
        low = d_first.astype(BF16)
        attended[pl.ds(at, rows)] = low
        ready(2 * chunks)
        d_ctx[0] = nt(low, wo[...]).astype(BF16)
        terms = [column_sum(d_hidden * unit1), column_sum(d_hidden), column_sum(low.astype(F32))]
        for n, term in enumerate(terms):
            sums_acc[n] += term
            sums[n : n + 1] = jnp.sum(sums_acc[n], axis=0, keepdims=True)

    @pl.when(step == 0)
    def _():
        for acc_ref in (sums_acc, inner_acc):
            acc_ref[...] = jnp.zeros_like(acc_ref)

    @pl.when(step < seqs)
    def _():
        row_part()

    @pl.when(step == seqs)
    def _():
        hidden_t[...] = hidden[...].T
        ctx_t[...] = ctx[...].T

    wide, narrow = ff // 2 // tiles, width // 2 // tiles

    def grad(which, tile):
        at = pl.multiple_of(which * (ff // 2) + tile * wide, wide)
        to = pl.multiple_of(which * (width // 2) + tile * narrow, narrow)
        left = nn(hidden_t[...], inner[:, pl.ds(at, wide)]).astype(BF16)
        right = nn(ctx_t[...], attended[:, pl.ds(to, narrow)]).astype(BF16)
        return jnp.concatenate([left, right], axis=1)

    @pl.when(jnp.logical_and(step >= seqs, step < seqs + tiles))
    def _():
        grad_other[...] = grad(1 - half[0], step - seqs)

    @pl.when(step >= seqs + tiles)
    def _():
        grad_mine[...] = grad(half[0], step - seqs - tiles)


def rows_forward(
    ctx, xc, xq, cot_c, cot_q, w_output, w_inner, w_outer, after, hidden_bias, gain, shift
):
    seqs, rows, width = ctx.shape
    length, slots = xc.shape[1], xq.shape[1]
    ff = w_inner.shape[1]
    total = seqs * rows

    def by_seq(n):
        return pl.BlockSpec((1, n, width), lambda s: (jnp.minimum(s, seqs - 1), 0, 0))

    def block(n):
        return pl.BlockSpec((rows, n), lambda s: (jnp.minimum(s, seqs - 1), 0))

    grad_block = pl.BlockSpec(
        (GRAD_TILE, width), lambda s: (jnp.maximum(s - seqs, 0), 0)
    )
    hbm = pl.BlockSpec(memory_space=pl.ANY)
    return pl.pallas_call(
        rows_forward_kernel,
        grid_spec=pltpu.PrefetchScalarGridSpec(
            num_scalar_prefetch=0,
            grid=(seqs + ff // GRAD_TILE,),
            in_specs=[
            by_seq(rows), by_seq(length), by_seq(slots), by_seq(length), by_seq(slots),
            hbm, hbm, hbm,
            full_spec((2, width)), full_spec((1, ff)), full_spec((2, width)), full_spec((2, width)),
        ],
        out_specs=[
            by_seq(length), by_seq(slots), block(ff), block(width),
            block(width), block(TILE), block(width), full_spec((3, width)),
            grad_block,
        ],
        scratch_shapes=weight_scratch(width, ff) + [
            pltpu.VMEM((rows, width), F32),
            pltpu.VMEM((total, ff), BF16),
            pltpu.VMEM((total, width), BF16),
            pltpu.VMEM((3, 8, width), F32),
        ],
        ),
        out_shape=[
            jax.ShapeDtypeStruct((seqs, length, width), BF16),
            jax.ShapeDtypeStruct((seqs, slots, width), BF16),
            jax.ShapeDtypeStruct((total, ff), BF16),
            jax.ShapeDtypeStruct((total, width), BF16),
            jax.ShapeDtypeStruct((total, width), BF16),
            jax.ShapeDtypeStruct((total, TILE), F32),
            jax.ShapeDtypeStruct((total, width), BF16),
            jax.ShapeDtypeStruct((3, width), F32),
            jax.ShapeDtypeStruct((ff, width), BF16),
        ],
        compiler_params=params(),
        name="rows_forward",
    )(ctx, xc, xq, cot_c, cot_q, w_output, w_inner, w_outer, after, hidden_bias, gain, shift)


def rows_backward(half, seqs, slots, outer, slope, unit, scale, hidden, ctx, w_output, w_inner, w_outer, gain):
    total, width = outer.shape
    rows = total // seqs
    ff = w_inner.shape[1]
    tiles = 3
    wide = (ff + width) // 2

    def block(n):
        return pl.BlockSpec((rows, n), lambda s, half: (jnp.minimum(s, seqs - 1), 0))

    def by_seq(n):
        return pl.BlockSpec((1, n, width), lambda s, half: (jnp.minimum(s, seqs - 1), 0, 0))

    def grad_block(start):
        return pl.BlockSpec(
            (width, wide // tiles), lambda s, half: (0, jnp.clip(s - start, 0, tiles - 1))
        )

    hbm = pl.BlockSpec(memory_space=pl.ANY)
    return pl.pallas_call(
        rows_backward_kernel,
        grid_spec=pltpu.PrefetchScalarGridSpec(
            num_scalar_prefetch=1,
            grid=(seqs + 2 * tiles,),
            in_specs=[
                block(width), block(ff), block(width), block(TILE),
                full_spec((total, width)), full_spec((total, width)),
                hbm, hbm, hbm, full_spec((2, width)),
            ],
            out_specs=[
                by_seq(rows - slots), by_seq(slots), by_seq(rows),
                full_spec((3, width)), full_spec((1, ff)),
                grad_block(seqs), grad_block(seqs + tiles),
            ],
            scratch_shapes=weight_scratch(width, ff) + [
                pltpu.VMEM((rows, width), F32),
                pltpu.VMEM((total, ff), BF16),
                pltpu.VMEM((total, width), BF16),
                pltpu.VMEM((width, total), BF16),
                pltpu.VMEM((width, total), BF16),
                pltpu.VMEM((3, 8, width), F32),
                pltpu.VMEM((8, ff), F32),
            ],
        ),
        out_shape=[
            jax.ShapeDtypeStruct((seqs, rows - slots, width), F32),
            jax.ShapeDtypeStruct((seqs, slots, width), F32),
            jax.ShapeDtypeStruct((seqs, rows, width), BF16),
            jax.ShapeDtypeStruct((3, width), F32),
            jax.ShapeDtypeStruct((1, ff), F32),
            jax.ShapeDtypeStruct((width, wide), BF16),
            jax.ShapeDtypeStruct((width, wide), BF16),
        ],
        compiler_params=params(),
        name="rows_backward",
    )(half, outer, slope, unit, scale, hidden, ctx, w_output, w_inner, w_outer, gain)


def grad_before_kernel(xc, xq, dq, dk, dv, *rest):
    out = rest[-1]
    length = xc.shape[1]
    wide = dq.shape[2]
    q_sum = k_sum = v_sum = None
    for s in range(xc.shape[0]):
        turned = jnp.concatenate([xc[s], xq[s]], axis=0).T
        q_sum = plus(q_sum, nn(turned, dq[s]))
        k_sum = plus(k_sum, nn(turned[:, :length], dk[s]))
        v_sum = plus(v_sum, nn(turned[:, :length], dv[s]))
    for n, total in enumerate((q_sum, k_sum, v_sum)):
        cols = slice(n * wide, (n + 1) * wide)
        if len(rest) == 3:
            total = total + rest[1][:, cols].astype(F32)
        out[:, cols] = total.astype(BF16)
    if len(rest) == 3:
        out[:, 3 * wide :] = rest[0][...].T.astype(BF16)


def grad_before(xc, xq, dq, dk, dv, vectors=None, got=None):
    seqs, length, width = xc.shape
    slots = xq.shape[1]
    wide = dq.shape[2]
    part = width // 2
    total = 3 * wide
    extra, extra_specs = [], []
    if vectors is not None:
        total += vectors.shape[0]
        extra = [vectors, got]
        extra_specs = [
            pl.BlockSpec((vectors.shape[0], part), lambda i: (0, i)),
            pl.BlockSpec((part, 3 * wide), lambda i: (i, 0)),
        ]
    return pl.pallas_call(
        grad_before_kernel,
        grid=(2,),
        in_specs=[
            pl.BlockSpec((seqs, length, part), lambda i: (0, 0, i)),
            pl.BlockSpec((seqs, slots, part), lambda i: (0, 0, i)),
            full_spec(dq.shape), full_spec(dk.shape), full_spec(dv.shape),
        ] + extra_specs,
        out_specs=pl.BlockSpec((part, total), lambda i: (i, 0)),
        out_shape=jax.ShapeDtypeStruct((width, total), BF16),
        compiler_params=params(),
        name="grad_before",
    )(xc, xq, dq, dk, dv, *extra)


def input_grad_kernel(
    half, first_c, first_q, dq_o, dk_o, dv_o, dq_m, dk_m, dv_m, wq_o, wk_o, wv_o, wq_m, wk_m, wv_m,
    out_c, out_q,
):
    length = dk_o.shape[1]
    left = [dq_o[0, :length], dk_o[0], dv_o[0], dq_m[0, :length], dk_m[0], dv_m[0]]
    right = [wq_o[...], wk_o[...], wv_o[...], wq_m[...], wk_m[...], wv_m[...]]
    out_c[0] = first_c[0] + nt(jnp.concatenate(left, axis=1), jnp.concatenate(right, axis=1))
    dq = jnp.concatenate([dq_o[0, length:], dq_m[0, length:]], axis=1)
    wq = jnp.concatenate([wq_o[...], wq_m[...]], axis=1)
    out_q[0] = (first_q[0] + nt(dq, wq)).astype(BF16)


def input_grad(half, first_c, first_q, other, mine, wq, wk, wv):
    seqs, rows, part = other[0].shape
    length = other[1].shape[1]
    width = wq.shape[0]

    def by_seq(n, cols):
        return pl.BlockSpec((1, n, cols), lambda s, half: (s, 0, 0))

    grads = [by_seq(rows, part), by_seq(length, part), by_seq(length, part)]
    firsts = [by_seq(length, width), by_seq(rows - length, width)]
    w_other = pl.BlockSpec((width, part), lambda s, half: (0, 1 - half[0]))
    w_mine = pl.BlockSpec((width, part), lambda s, half: (0, half[0]))
    return pl.pallas_call(
        input_grad_kernel,
        grid_spec=pltpu.PrefetchScalarGridSpec(
            num_scalar_prefetch=1,
            grid=(seqs,),
            in_specs=firsts + grads * 2 + [w_other] * 3 + [w_mine] * 3,
            out_specs=firsts,
        ),
        out_shape=[
            jax.ShapeDtypeStruct((seqs, length, width), F32),
            jax.ShapeDtypeStruct((seqs, rows - length, width), BF16),
        ],
        compiler_params=params(),
        name="input_grad",
    )(half, first_c, first_q, *other, *mine, wq, wk, wv, wq, wk, wv)


def swap(value, axis, count, stride):
    return lax.ppermute(value, axis, [(i, i ^ stride) for i in range(count)])


def take(value, dim, index):
    return lax.dynamic_index_in_dim(value, index, dim, keepdims=False)


def low_sum(*terms):
    total = None
    for term in terms:
        total = plus(total, term.astype(F32))
    return total.astype(BF16)


def first_kernel(bits, *refs):
    terms, (send_a, send_b, keep_a, keep_b) = refs[:-4], refs[-4:]
    x, y = bits[0], bits[1]
    cut = send_a.shape[2]

    def total(g, row, col, rows):
        out = None
        for term in terms:
            out = plus(out, term[g, row, col, rows].astype(F32))
        return out.astype(BF16)

    for g in range(send_a.shape[0]):
        for n in range(2):
            send_a[g, n] = total(g, n, 1 - x, slice(0, cut))
            keep_a[g, n] = total(g, n, x, slice(0, cut))
            send_b[g, n] = total(g, 1 - y, n, slice(cut, 2 * cut))
            keep_b[g, n] = total(g, y, n, slice(cut, 2 * cut))


def second_kernel(bits, keep_a, keep_b, got_a, got_b, send_a, send_b, left_a, left_b):
    x, y = bits[0], bits[1]

    def total(keep, got, g, n):
        return (keep[g, n].astype(F32) + got[g, n].astype(F32)).astype(BF16)

    for g in range(send_a.shape[0]):
        send_a[g] = total(keep_a, got_a, g, 1 - y)
        left_a[g] = total(keep_a, got_a, g, y)
        send_b[g] = total(keep_b, got_b, g, 1 - x)
        left_b[g] = total(keep_b, got_b, g, x)


def third_kernel(bits, left_a, left_b, got_a, got_b, out):
    cut = left_a.shape[1]
    out[:, :cut] = (left_a[...].astype(F32) + got_a[...].astype(F32)).astype(BF16)
    out[:, cut:] = (left_b[...].astype(F32) + got_b[...].astype(F32)).astype(BF16)


def part_sum_kernel(parts, out):
    total = parts[0].astype(F32)
    for n in range(1, parts.shape[0]):
        total = total + parts[n].astype(F32)
    out[...] = total.astype(BF16)


def staged(kernel, bits, arrays, shapes, name):
    vmem = pl.BlockSpec(memory_space=pltpu.VMEM)
    return pl.pallas_call(
        kernel,
        in_specs=[pl.BlockSpec(memory_space=pltpu.SMEM)] + [vmem] * len(arrays),
        out_specs=[vmem] * len(shapes),
        out_shape=[jax.ShapeDtypeStruct(shape, BF16) for shape in shapes],
        compiler_params=params(),
        name=name,
    )(bits, *arrays)


class Reduction:
    def __init__(self, tok):
        self.tok = tok
        x = lax.axis_index("qry") // 2
        y = lax.axis_index("tok") % 2
        self.x = x
        self.bits = jnp.stack([x, y]).astype(jnp.int32)

    def first_sends(self, *terms):
        rows, cols = terms[0].shape
        deep = rows // self.tok // 2
        shape = (self.tok // 2, 2, 2, deep, cols)
        outs = [(self.tok // 2, 2, deep // 2, cols)] * 4
        *sends, self.keep_a, self.keep_b = staged(
            first_kernel, self.bits, [t.reshape(shape) for t in terms], outs, "first_sums"
        )
        return sends

    def first_moves(self, sends):
        return [swap(sends[0], "qry", 4, 2), swap(sends[1], "tok", self.tok, 1)]

    def second_sends(self, got):
        shape = self.keep_a.shape
        outs = [(shape[0],) + shape[2:]] * 4
        *sends, self.left_a, self.left_b = staged(
            second_kernel, self.bits, [self.keep_a, self.keep_b, *got], outs, "second_sums"
        )
        return sends

    def second_moves(self, sends):
        return [swap(sends[0], "tok", self.tok, 1), swap(sends[1], "qry", 4, 2)]

    def third_sends(self, got):
        rest, deep, cols = self.left_a.shape
        (out,) = staged(
            third_kernel, self.bits, [self.left_a, self.left_b, *got], [(rest, 2 * deep, cols)], "third_sums"
        )
        return out

    def third_moves(self, send):
        if self.tok == 2:
            return send
        groups = [list(range(bit, self.tok, 2)) for bit in range(2)]
        return lax.all_to_all(send, "tok", 0, 0, tiled=True, axis_index_groups=groups)

    def far_sends(self, got):
        self.own = pl.pallas_call(
            part_sum_kernel,
            out_shape=jax.ShapeDtypeStruct(got.shape[1:], BF16),
            name="part_sums",
        )(got)
        return self.own

    def far_moves(self, send):
        return swap(send, "qry", 4, 2)

    def near_sends(self, got):
        low = self.x == 0
        self.own = jnp.concatenate(
            [jnp.where(low, self.own, got), jnp.where(low, got, self.own)], axis=0
        )
        return self.own

    def near_moves(self, send):
        return swap(send, "qry", 4, 1)


def beside(transfers, compute=None, arrays=()):
    moves = [move for move, _ in transfers]
    sends = [send for _, send in transfers]
    sends, arrays = lax.optimization_barrier((sends, tuple(arrays)))
    got = [move(send) for move, send in zip(moves, sends)]
    out = compute(*arrays) if compute is not None else ()
    return lax.optimization_barrier((got, out))


def in_core_order(first, own, got):
    a, b = own[...].astype(F32), got[...].astype(F32)
    return jnp.where(first, a, b), jnp.where(first, b, a)


def place_outer_kernel(core, own, got, outer):
    part = own.shape[1]
    first, second = in_core_order(core[0] == 0, own, got)
    outer[:, :part] = first
    outer[:, part:] = second


def place_inner_kernel(core, own, got, inner, output):
    tiles = 3
    wide, narrow = inner.shape[1] // 2 // tiles, output.shape[1] // 2 // tiles
    for n, half in enumerate(in_core_order(core[0] == 0, own, got)):
        for t in range(tiles):
            at = t * (wide + narrow)
            to = (n * tiles + t) * wide
            inner[:, to : to + wide] = half[:, at : at + wide]
            to = (n * tiles + t) * narrow
            output[:, to : to + narrow] = half[:, at + wide : at + wide + narrow]


def place_before_kernel(core, own, got, query, key, value, *vectors):
    part = query.shape[1] // 2
    first, second = in_core_order(core[0] == 0, own, got)
    for n, ref in enumerate((query, key, value)):
        ref[:, :part] = first[:, n * part : (n + 1) * part]
        ref[:, part:] = second[:, n * part : (n + 1) * part]
    every = (first[:, 3 * part :] + second[:, 3 * part :]).T
    at = 0
    for ref in vectors:
        ref[...] = every[at : at + ref.shape[0]]
        at += ref.shape[0]


def place_sums(kernel, core, own, got, shapes):
    vmem = pl.BlockSpec(memory_space=pltpu.VMEM)
    return pl.pallas_call(
        kernel,
        in_specs=[pl.BlockSpec(memory_space=pltpu.SMEM), vmem, vmem],
        out_specs=[vmem] * len(shapes),
        out_shape=[jax.ShapeDtypeStruct(shape, F32) for shape in shapes],
        name="place_sums",
    )(core, own, got)


def on_device(
    content_in, query_in, seq_lengths, perm_ranks, w_query, w_key, w_value, w_output, w_inner,
    w_outer, b_before, b_after, b_hidden, norm_gain, norm_shift, rel_table, cot_content, cot_query,
    tok,
):
    seqs, length, width = content_in.shape
    group = lax.axis_index("qry")
    core = group % 2
    other = jnp.reshape(1 - core, (1,)).astype(jnp.int32)
    mine = jnp.reshape(core, (1,)).astype(jnp.int32)
    lengths = lax.dynamic_slice_in_dim(seq_lengths, group * seqs, seqs)
    ranks = lax.dynamic_slice_in_dim(perm_ranks, group * seqs, seqs, 0)

    both = jnp.concatenate([query_in, cot_query], axis=2)
    (both,), (q_content, k, v) = beside(
        [(lambda a: lax.all_to_all(a, "qry", 0, 1, tiled=True), both)],
        lambda: project(content_in, w_query, w_key, w_value, b_before),
    )
    xq, cot_q = both[:, :, :width], both[:, :, width:]
    slots = xq.shape[1]
    floor = lengths[:, None] - PRED
    thr_c = jnp.maximum(floor, jnp.minimum(ranks, lengths[:, None]))[:, :, None]
    thr_q = (floor + jnp.arange(slots, dtype=jnp.int32)[None, :])[:, :, None]
    rank_row = ranks[:, None, :]
    place = jnp.arange(512, dtype=jnp.int32)
    one_hot = bucket_of(jnp.where(place < 384, place, place - 512) - 128)
    one_hot = (one_hot[None, :] == jnp.arange(BUCKETS, dtype=jnp.int32)[:, None]).astype(BF16)
    offsets = jnp.dot(rel_table, one_hot, preferred_element_type=F32)[:, None, :]

    ctx, e, rr, q = attention_forward(
        q_content, k, v, xq, w_query, b_before, rank_row, thr_c, thr_q, offsets,
        rel_table.astype(F32),
    )
    (out_c, out_q, slope, hidden, unit, scale, outer, sums_f, g_outer) = rows_forward(
        ctx, content_in, xq, cot_content, cot_q, w_output, w_inner, w_outer, b_after,
        b_hidden[None], norm_gain, norm_shift,
    )
    ff = slope.shape[1]
    share = width // tok
    part = width // 2

    red_i = Reduction(tok)
    red_b = Reduction(tok)

    def slot_blocks(a):
        a = a.reshape(seqs, 4, slots // 4, a.shape[2])
        return [take(a, 1, group ^ n) for n in range(4)]

    def slot_moves(blocks):
        return [swap(blocks[n], "qry", 4, n) for n in range(1, 4)]

    def slot_rows(own, got):
        every = jnp.stack([own, *got])
        return jnp.concatenate([take(every, 0, group ^ n) for n in range(4)], axis=0)

    def swap_core(a):
        return swap(a, "qry", 4, 1)

    def over_tok(a):
        return lax.psum_scatter(a, "tok", scatter_dimension=0, tiled=True)

    o_sum = over_tok(g_outer)
    first_c, first_q, d_ctx, sums_b, inner_sums, i_other, i_mine = rows_backward(
        mine, seqs, slots, outer, slope, unit, scale, hidden, ctx.reshape(-1, width), w_output,
        w_inner, w_outer, norm_gain,
    )
    (got_i,), back_other = beside(
        [(swap_core, i_other)],
        lambda a: attention_backward(other, q, k, v, e, ctx, a, rr, rank_row, thr_q),
        (d_ctx,),
    )

    def grad_and_backward(dq, dk, dv, cotangent):
        b_other = grad_before(content_in, xq, dq, dk, dv)
        b_other, cotangent = lax.optimization_barrier((b_other, cotangent))
        got = swap_core(b_other)
        return got, attention_backward(mine, q, k, v, e, ctx, cotangent, rr, rank_row, thr_q)

    (got_i,), (got_b, back_mine) = beside(
        [(red_i.first_moves, red_i.first_sends(i_mine, got_i))],
        grad_and_backward,
        (*back_other[:3], d_ctx),
    )

    def in_order(a, b, axis):
        return jnp.where(
            core == 0, jnp.concatenate([b, a], axis=axis), jnp.concatenate([a, b], axis=axis)
        )

    table = in_order(back_other[4], back_mine[4], 0)[:, :, :BUCKETS]
    table = jnp.tile(table.reshape(-1, share), (1, tok))
    wide_sums = jnp.swapaxes(inner_sums.reshape(tok, ff // width, share), 0, 1)
    vectors = jnp.concatenate(
        [
            in_order(back_other[3], back_mine[3], 1),
            sums_b[2:], sums_f[2:], sums_b[:1], sums_f[:1], sums_b[1:2], sums_f[1:2],
            wide_sums.reshape(-1, width), table,
        ]
    )
    vectors = jnp.pad(vectors, ((0, TILE - vectors.shape[0]), (0, 0)))
    o_parts = o_sum.reshape(ff // tok, 2, part)
    (got_i, got_o), b_mine = beside(
        [
            (red_i.second_moves, red_i.second_sends(got_i)),
            (swap_core, take(o_parts, 1, 1 - core)),
        ],
        lambda a: grad_before(content_in, xq, a, *back_mine[1:3], vectors, got_b),
        (back_mine[0],),
    )
    o_sum = low_sum(take(o_parts, 1, core), got_o)
    send_i = red_i.third_sends(got_i)
    send_b = red_b.first_sends(b_mine)
    send_i, send_b, first_c = lax.optimization_barrier((send_i, send_b, first_c))
    got_i = red_i.third_moves(send_i)
    got_b = red_b.first_moves(send_b)
    d_content, d_query = input_grad(
        mine, first_c, first_q, back_other[:3], back_mine[:3], w_query, w_key, w_value
    )
    got_b, d_content, d_query = lax.optimization_barrier((got_b, d_content, d_query))
    (got_b,), rows_q = beside(
        [(red_b.second_moves, red_b.second_sends(got_b))],
        lambda *a: slot_blocks(jnp.concatenate(a, axis=2)),
        (out_q, d_query),
    )

    def swap_x(a):
        return swap(a, "qry", 4, 2)

    (got_b, got_i, got_o, got_q), _ = beside(
        [
            (red_b.third_moves, red_b.third_sends(got_b)),
            (red_i.far_moves, red_i.far_sends(got_i)),
            (swap_x, o_sum),
            (slot_moves, rows_q),
        ],
    )
    o_sum = low_sum(o_sum, got_o)
    (got_b, got_o, got_i), rows_q = beside(
        [
            (red_b.far_moves, red_b.far_sends(got_b)),
            (swap_core, o_sum),
            (red_i.near_moves, red_i.near_sends(got_i)),
        ],
        lambda *a: slot_rows(a[0], a[1:]),
        (rows_q[0], *got_q),
    )
    out_q, d_query = rows_q[:, :, :width], rows_q[:, :, width:].astype(F32)
    (got_b,), ((g_outer,), (g_inner, g_output)) = beside(
        [(red_b.near_moves, red_b.near_sends(got_b))],
        lambda a, b: (
            place_sums(place_outer_kernel, mine, o_sum, a, [(ff // tok, width)]),
            place_sums(place_inner_kernel, mine, red_i.own, b, [(share, ff), (share, width)]),
        ),
        (got_o, got_i),
    )
    pair = (2, share)
    (
        g_query, g_key, g_value, g_before, g_after, g_gain, g_shift, g_hidden, g_table,
    ) = place_sums(
        place_before_kernel, mine, red_b.own, got_b,
        [(share, width)] * 3 + [pair] * 4
        + [(ff // width, share), (HEADS * BUCKETS // share, share)],
    )
    return (
        out_c, out_q, d_content, d_query, g_query, g_key, g_value, g_output, g_inner, g_outer,
        g_before, g_after, g_hidden.reshape(-1), g_gain, g_shift, g_table.reshape(HEADS, BUCKETS),
    )


def solution(mesh):
    rows = P(("tok", "qry"), None, None)
    slots = P("tok", "qry", None)
    return jax.shard_map(
        functools.partial(on_device, tok=mesh.shape["tok"]),
        mesh=mesh,
        in_specs=(rows, slots, P("tok"), P("tok", None)) + (P(),) * 12 + (rows, slots),
        out_specs=(rows, slots, rows, slots)
        + (P("tok", None),) * 6
        + (P(None, "tok"), P(None, "tok"), P("tok"), P(None, "tok"), P(None, "tok"), P()),
        check_vma=False,
    )
```
